128 devices in a mesh: sec: 8 (over x, z_lo), blk: 16 (over y, z_hi, core).
Axes of the slice: x: 4, y: 4, z: 4 (z_hi: 2, z_lo: 2; z = z_hi * 2 + z_lo), core: 2. Of those that a mesh axis runs over, the one named last changes fastest.
Arguments:
- thermal_kelvin: float32 [2048, 16384], P('sec', 'blk'), may hold values from -6 to 6
- diffusion_factor: float32 [2048, 16384], P('sec', 'blk'), may hold values from 0.15 to 0.6
- speed_lateral: float32 [2048, 16384], P('sec', 'blk'), may hold values from -0.45 to 0.45
- speed_lineward: float32 [2048, 16384], P('sec', 'blk'), may hold values from -0.45 to 0.45
- patch_mesh_slot: int32 [1048576], P(('sec', 'blk')), may hold values from 0 to 262143
- patch_holder_lateral: int32 [1048576, 1], P(('sec', 'blk')), may hold values from 0 to 15; in each aligned block of 8192 rows (0 to 8191, 8192 to 16383, ...) at most 768 rows name the same one
- patch_boundary_dest: int32 [1048576], P(('sec', 'blk')), may hold values from 0 to 262143
- patch_film_factor: float32 [1048576], P(('sec', 'blk')), may hold values from 0.05 to 0.5
- patch_kelvin_prior: float32 [1048576], P(('sec', 'blk')), may hold values from -6 to 6
Outputs:
- new_temperature: float32 [2048, 16384], P('sec', 'blk')
- wall_out: float32 [1048576], P(('sec', 'blk'))
The draws below stay inside these ranges and needn't reach their ends.
Inputs may be any that keep to these rules, and one draw needn't show every extreme that they name: In every block's 8192 faces at most 768 name one column, and some block has a column named exactly 768 times. On blocks of solid rows patch_holder_lateral and patch_boundary_dest are not read.
All inputs are finite; a program needn't handle non-finite values.
Results may differ from the reference program's by a relative error of at most 0.00002.
Values sent between devices are 32-bit elements; how exact they have to be, the bound alone decides.
A program may use at most 64 MiB of HBM per device.

```python
import math
import jax
import jax.numpy as jnp
import numpy as np

CY = 256
CZ = 1024
FPD = 8192
GAS_MINOR_PASSES = 10
SOLID_SUBSTEPS = 4
FR = 6
NS = 2
MESH_LINES = 2048
MESH_LATERALS = 16384
SURFACE_PATCHES = 1048576
WCELLS = 131072
CAP = 768
N_BLK = 16


def touch_ends(entries, key, least, high):
    longest = entries.shape.index(max(entries.shape))
    spots = []
    for shift in (0, 1):
        where = [jax.random.randint(jax.random.fold_in(key, axis), (), 0, length) for axis, length in enumerate(entries.shape)]
        where[longest] = (where[longest] + shift) % entries.shape[longest]
        spots.append(tuple(where))
    return entries.at[spots[0]].set(least).at[spots[1]].set(high)


def block_levels(own_key, extent, split, smallest, largest):
    def one(position, parts):
        heights = jax.random.uniform(jax.random.fold_in(jax.random.fold_in(own_key, 6), position), (parts,), jnp.float32, smallest / len(split), largest / len(split))
        return jnp.repeat(jnp.exp(heights), extent[position] // parts).reshape((-1,) + (1,) * (len(extent) - position - 1))

    loudness = one(*split[0])
    for cut in split[1:]:
        loudness = loudness * one(*cut)
    return loudness


def routed_block(stream_key, own, number, rows, count, top, reach, slope):
    ranking = jax.random.permutation(stream_key, count)
    crowded, usual = portions_of(count, rows * top, reach, slope, True), portions_of(count, rows * top, reach, slope, False)
    places = jnp.arange(count)

    def named(lengths, offset_by):
        used = int((lengths > 0).sum())
        fixed = max(1, used // 4)
        moved = fixed + (places - fixed + offset_by * (used - fixed)) % max(1, count - fixed)
        return jnp.zeros((count,), jnp.int32).at[ranking[jnp.where(places < fixed, places, moved)]].set(jnp.asarray(lengths, jnp.int32))

    lengths = jnp.where(number % 4 == 0, named(crowded, number // 4), named(usual, number - number // 4 - 1))
    mixed = jax.random.permutation(jax.random.fold_in(own, 3), count)
    source_of, taker = mixed[0:count // 2 * 2:2], mixed[1:count // 2 * 2:2]
    room = jnp.minimum(lengths[source_of] - 1, reach - lengths[taker]) // 2
    room = jnp.where((source_of == ranking[0]) | (taker == ranking[0]) | (lengths[taker] == 0), 0, jnp.maximum(room, 0))
    moved = jax.random.randint(jax.random.fold_in(own, 4), (count // 2,), 0, 1 << 20) % (room + 1)
    lengths = lengths.at[source_of].add(-moved).at[taker].add(moved)
    labels = jnp.searchsorted(jnp.cumsum(lengths), jnp.arange(rows * top), side="right").astype(jnp.int32)
    table = labels.reshape(top, rows).T
    table = table[jax.random.permutation(jax.random.fold_in(own, 1), rows)]
    offset_by = jax.random.randint(jax.random.fold_in(own, 2), (rows, 1), 0, top)
    return jnp.take_along_axis(table, (jnp.arange(top)[None, :] + offset_by) % top, axis=1)


def portions_of(amount, total, bound, lean, full):
    weights = [(1 << 20) // math.isqrt(standing ** lean) + 1 for standing in range(1, amount + 1)]
    largest = bound if full else min(bound, max(-(-total // amount), total * weights[0] // sum(weights)))
    least = 1 if total - largest >= amount - 1 else 0
    given, rest = [largest] + [least] * (amount - 1), total - largest - least * (amount - 1)
    while rest > 0:
        movable = [i for i in range(1, amount) if given[i] < largest] or [i for i in range(1, amount) if given[i] < bound]
        pool, remaining = sum([weights[i] for i in movable]), rest
        for i in movable:
            addition = min(bound - given[i], max(1, remaining * weights[i] // pool), rest)
            given[i] = given[i] + addition
            rest = rest - addition
    return np.array(given)


def gaussian(stream_key, shape, width, reach, shards=(), kind=jnp.bfloat16):
    values = width * jax.random.normal(stream_key, shape, jnp.float32)
    if shards:
        values = values * block_levels(stream_key, shape, shards, -0.22, 0.18)
    return jnp.clip(values, -reach, reach).astype(kind)


def setup_inputs(seed: int = 0) -> dict:
    key_list = jax.random.split(jax.random.key(seed), 10)
    thermal_kelvin = gaussian(key_list[0], (MESH_LINES, MESH_LATERALS), 1.0, 6.0, ((0, 8), (1, 16)), jnp.float32)
    diffusion_factor = jnp.clip(jnp.exp(math.log(0.6) - 1.3862944 * jax.random.uniform(key_list[1], (MESH_LINES, MESH_LATERALS), jnp.float32) ** block_levels(key_list[1], (MESH_LINES, MESH_LATERALS), ((0, 8), (1, 16)), -0.2, 0.2)), 0.15, 0.6)
    speed_lateral = gaussian(key_list[2], (MESH_LINES, MESH_LATERALS), 0.15, 0.45, ((0, 8), (1, 16)), jnp.float32)
    speed_lineward = gaussian(key_list[3], (MESH_LINES, MESH_LATERALS), 0.15, 0.45, ((0, 8), (1, 16)), jnp.float32)
    patch_mesh_slot = touch_ends(jax.random.randint(key_list[4], (SURFACE_PATCHES,), 0, CY * CZ), jax.random.fold_in(key_list[4], 1), 0, (CY * CZ) - 1).astype(jnp.int32)
    patch_holder_lateral_keys = jax.random.split(jax.random.fold_in(key_list[5], 1), SURFACE_PATCHES // FPD)
    patch_holder_lateral_turns = jax.random.permutation(jax.random.fold_in(key_list[5], 3), SURFACE_PATCHES // FPD)
    patch_holder_lateral = jax.vmap(lambda own, number: routed_block(jax.random.fold_in(key_list[5], 2), own, number, FPD, N_BLK, 1, CAP, 2))(patch_holder_lateral_keys, patch_holder_lateral_turns).reshape((SURFACE_PATCHES, 1))
    patch_boundary_dest = touch_ends(jax.random.randint(key_list[6], (SURFACE_PATCHES,), 0, NS * WCELLS), jax.random.fold_in(key_list[6], 1), 0, (NS * WCELLS) - 1).astype(jnp.int32)
    patch_film_factor = jnp.clip(jnp.exp(math.log(0.5) - 2.3025851 * jax.random.uniform(key_list[7], (SURFACE_PATCHES,), jnp.float32) ** block_levels(key_list[7], (SURFACE_PATCHES,), ((0, 128),), -0.2, 0.2)), 0.05, 0.5)
    patch_kelvin_prior = gaussian(key_list[8], (SURFACE_PATCHES,), 1.0, 6.0, ((0, 128),), jnp.float32)
    return dict(thermal_kelvin=thermal_kelvin, diffusion_factor=diffusion_factor, speed_lateral=speed_lateral, speed_lineward=speed_lineward, patch_mesh_slot=patch_mesh_slot, patch_holder_lateral=patch_holder_lateral, patch_boundary_dest=patch_boundary_dest, patch_film_factor=patch_film_factor, patch_kelvin_prior=patch_kelvin_prior)


time_step = 0.2


def stencil_terms(padded_temp, padded_cond):
    center = padded_temp[1:-1, 1:-1]
    north = padded_temp[2:, 1:-1]
    south = padded_temp[:-2, 1:-1]
    east = padded_temp[1:-1, 2:]
    west = padded_temp[1:-1, :-2]
    kcenter = padded_cond[1:-1, 1:-1]
    spread = 0.5 * ((kcenter + padded_cond[2:, 1:-1]) * (north - center)
                    + (kcenter + padded_cond[:-2, 1:-1]) * (south - center)
                    + (kcenter + padded_cond[1:-1, 2:]) * (east - center)
                    + (kcenter + padded_cond[1:-1, :-2]) * (west - center))
    return center, spread, east - west, north - south


def fluid_advance(padded_temp, padded_cond, speed_lateral, speed_lineward):
    center, spread, across, upward = stencil_terms(padded_temp, padded_cond)
    return center + time_step * (spread - 0.5 * (speed_lateral * across + speed_lineward * upward))


def solid_advance(padded_temp, padded_cond):
    center, spread, across, upward = stencil_terms(padded_temp, padded_cond)
    return center + time_step * spread


def pad_region(region):
    padded = jnp.pad(region, ((1, 1), (0, 0)), mode="edge")
    return jnp.concatenate([padded[:, -1:], padded, padded[:, :1]], axis=1)


def reference(thermal_kelvin, diffusion_factor, speed_lateral, speed_lineward, patch_mesh_slot, patch_holder_lateral, patch_boundary_dest, patch_film_factor, patch_kelvin_prior):
    gas_tile_number = FR * CY
    hotside_patches = FR * N_BLK * FPD
    gas_state_array = thermal_kelvin[:gas_tile_number]
    metal_state_array = thermal_kelvin[gas_tile_number:]
    fluid_cond = pad_region(diffusion_factor[:gas_tile_number])
    solid_cond = pad_region(diffusion_factor[gas_tile_number:])
    fluid_vx = speed_lateral[:gas_tile_number]
    fluid_vy = speed_lineward[:gas_tile_number]
    order = jnp.arange(SURFACE_PATCHES, dtype=jnp.int32)
    device = order // FPD
    sec_row = device // N_BLK
    column = device % N_BLK
    row_part = patch_mesh_slot // CZ
    col_part = patch_mesh_slot % CZ
    fluid_index = ((sec_row * CY + row_part) * MESH_LATERALS + column * CZ + col_part)[:hotside_patches]
    solid_own = (((sec_row - FR) * CY + row_part) * MESH_LATERALS + column * CZ + col_part)[hotside_patches:]
    gas_coef = patch_film_factor[:hotside_patches]
    hotside_boundary = patch_kelvin_prior[:hotside_patches]
    flux_sum = jnp.zeros((hotside_patches,), jnp.float32)
    for substep_index in range(GAS_MINOR_PASSES):
        heat_flux = gas_coef * (gas_state_array.reshape(-1)[fluid_index] - hotside_boundary)
        flux_sum = flux_sum + heat_flux
        advanced = fluid_advance(pad_region(gas_state_array), fluid_cond, fluid_vx, fluid_vy)
        gas_state_array = advanced.reshape(-1).at[fluid_index].add(-time_step * heat_flux).reshape(gas_state_array.shape)
    mean_flux = flux_sum / GAS_MINOR_PASSES
    target_col = patch_holder_lateral[:hotside_patches, 0]
    target = patch_boundary_dest[:hotside_patches]
    target_row = target // WCELLS
    target_cell = target % WCELLS
    wall_index = (target_row * CY + target_cell // CZ) * MESH_LATERALS + target_col * CZ + target_cell % CZ
    source = jnp.zeros((NS * CY * MESH_LATERALS,), jnp.float32).at[wall_index].add(mean_flux).reshape(NS * CY, MESH_LATERALS)
    cool_coef = patch_film_factor[hotside_patches:]
    chiller_medium = patch_kelvin_prior[hotside_patches:]
    for substep_index in range(SOLID_SUBSTEPS):
        cool_flux = cool_coef * (metal_state_array.reshape(-1)[solid_own] - chiller_medium)
        advanced = solid_advance(pad_region(metal_state_array), solid_cond) + time_step * source
        metal_state_array = advanced.reshape(-1).at[solid_own].add(-time_step * cool_flux).reshape(metal_state_array.shape)
    flat_solid = metal_state_array.reshape(-1)
    wall_out = jnp.concatenate([flat_solid[wall_index], flat_solid[solid_own]])
    return jnp.concatenate([gas_state_array, metal_state_array], axis=0), wall_out
```

```python
import functools

import jax
import jax.numpy as jnp
from jax import lax
from jax.experimental import pallas as pl
from jax.experimental.pallas import tpu as pltpu
from jax.sharding import PartitionSpec as P

F32, BF16, I32 = jnp.float32, jnp.bfloat16, jnp.int32
MESH = pl.DeviceIdType.MESH
NT = (((1,), (1,)), ((), ()))

CY, CX = 256, 1024
FACES = 8192
FLUID_ROWS, SECS, COLS = 6, 8, 16
FLUID_STEPS, SOLID_STEPS = 10, 4
DT = 0.2
KB = 512
NB = FACES // KB
BROWS = 8
SLOTS = COLS * BROWS
PAIRS = 56
CROWS = 2 * PAIRS
ALLP = FLUID_ROWS * PAIRS
QUAD = 4
LIST = ALLP + QUAD
HY, HX = 304, 1280
OY, OX = 24, 128
VLIM = 60 << 20


def params(**kw):
    return pltpu.CompilerParams(vmem_limit_bytes=VLIM, **kw)


def iota(shape, dim):
    return lax.broadcasted_iota(I32, shape, dim)


def split2(x):
    hi = x.astype(BF16).astype(F32)
    return hi, (x - hi).astype(BF16).astype(F32)


def onehot(mask):
    return jnp.where(mask, 1.0, 0.0).astype(BF16)


def dot(a, b):
    return jnp.dot(a, b, preferred_element_type=F32)


def dot_nt(a, b):
    return lax.dot_general(a, b, NT, preferred_element_type=F32)


def lane_row(ref, b, n):
    return jnp.concatenate([ref[pl.ds(n * b + i, 1), :] for i in range(n)], axis=1)


def put_lane_row(ref, b, n, v):
    for i in range(n):
        ref[pl.ds(n * b + i, 1), :] = v[:, i * 128:(i + 1) * 128]


def ranks(groups_of, nb, ng, o_ref, p_ref):
    def build(b, _):
        o_ref[pl.ds(pl.multiple_of(b * ng, 8), ng), :] = jnp.where(iota((ng, KB), 0) == groups_of(b), 1.0, 0.0)
        return 0
    lax.fori_loop(0, nb, build, 0)
    before = onehot(iota((KB, KB), 0) < iota((KB, KB), 1))
    o = o_ref[...].astype(BF16)
    p_ref[...] = dot(o, before)
    return dot(o, onehot(iota((KB, 128), 0) >= 0))


def spread_rows(pos, pieces, rows):
    hit = iota((rows, KB), 0) == (pos >> 7)
    a = jnp.concatenate([jnp.where(hit, v, 0.0).astype(BF16) for v in pieces], axis=0)
    c = onehot(iota((128, KB), 0) == (pos & 127))
    return dot_nt(a, c)


def pick(vt, pos, rows):
    r = onehot(iota((rows, KB), 0) == (pos >> 7))
    g = dot(vt, jnp.concatenate([r, r], axis=0))
    return jnp.sum(jnp.where(iota((128, KB), 0) == (pos & 127), g, 0.0), axis=0, keepdims=True)


def transposed_parts(v):
    hi, lo = split2(v.T)
    return jnp.concatenate([hi, lo], axis=1).astype(BF16)


def target_parts(t):
    return (t >> 10).astype(F32), ((t >> 5) & 31).astype(F32), (t & 31).astype(F32)


def target_join(x, rows):
    return (x[0:rows] * 1024.0 + x[rows:2 * rows] * 32.0 + x[2 * rows:3 * rows]).astype(I32)


def prep_kernel(slot, coef, prior, lateral, dest, cm, dm, pos1, tb, acc, o_ref, p_ref):
    acc[...] = jnp.zeros_like(acc)

    def maps(b, _):
        s, c = slot[b], coef[b]
        parts = split2(c) + split2(c * prior[b])
        hit = iota((CY, KB), 0) == (s >> 10)
        a = jnp.concatenate([jnp.where(hit, v, 0.0).astype(BF16) for v in parts], axis=0)
        acc[...] += dot_nt(a, onehot(iota((CX, KB), 0) == (s & 1023)))
        return 0

    lax.fori_loop(0, NB, maps, 0)
    cm[...] = acc[0:CY] + acc[CY:2 * CY]
    dm[...] = acc[2 * CY:3 * CY] + acc[3 * CY:4 * CY]

    @pl.when(lax.axis_index("sec") < FLUID_ROWS)
    def _():
        totals = ranks(lambda b: lateral[b], NB, COLS, o_ref, p_ref)
        carry = jnp.zeros((COLS, 128), F32)
        out = jnp.zeros((3 * SLOTS, 128), F32)
        for b in range(NB):
            rows = slice(b * COLS, (b + 1) * COLS)
            place = p_ref[rows] + jnp.concatenate([carry] * (KB // 128), axis=1)
            rank = jnp.sum(o_ref[rows] * place, axis=0, keepdims=True)
            pos = lateral[b] * (BROWS * 128) + rank.astype(I32)
            pos1[b] = pos
            carry = carry + totals[rows]
            out = out + spread_rows(pos, target_parts(dest[b] + 1024), SLOTS)
        tb[...] = target_join(out, SLOTS)

    @pl.when(lax.axis_index("sec") >= FLUID_ROWS)
    def _():
        pos1[...] = jnp.zeros_like(pos1)
        tb[...] = jnp.zeros_like(tb)


def prep(slot, coef, prior, lateral, dest):
    return pl.pallas_call(
        prep_kernel,
        out_shape=[jax.ShapeDtypeStruct((CY, CX), F32)] * 2
        + [jax.ShapeDtypeStruct((NB, 1, KB), I32), jax.ShapeDtypeStruct((SLOTS, 128), I32)],
        scratch_shapes=[pltpu.VMEM((4 * CY, CX), F32), pltpu.VMEM((NB * COLS, KB), F32), pltpu.VMEM((NB * COLS, KB), F32)],
        compiler_params=params(),
    )(slot, coef, prior, lateral, dest)


def compact_kernel(t, pos2, t2, o_ref, p_ref):
    nb, ng = SLOTS // 4, 8

    @pl.when(lax.axis_index("sec") < FLUID_ROWS)
    def _():
        def group(b):
            v = lane_row(t, b, 4)
            return jnp.where(v >= 1024, ((v - 1024) >> 17) * 4 + ((v >> 8) & 3), -1)

        totals = ranks(group, nb, ng, o_ref, p_ref)
        count = jnp.zeros((ng, 128), F32)
        for b in range(nb):
            count = count + totals[b * ng:(b + 1) * ng]
        units = ((count.astype(I32) + 255) >> 8).astype(F32).astype(BF16)
        lower = onehot(iota((ng, ng), 1) < iota((ng, ng), 0))
        carry = dot(lower, units) * 256.0
        out = jnp.zeros((3 * CROWS, 128), F32)
        for b in range(nb):
            rows = slice(b * ng, (b + 1) * ng)
            place = p_ref[rows] + jnp.concatenate([carry] * (KB // 128), axis=1)
            rank = jnp.sum(o_ref[rows] * place, axis=0, keepdims=True)
            v = lane_row(t, b, 4)
            pos = jnp.where(v >= 1024, rank.astype(I32), -1)
            pos2[b] = pos
            carry = carry + totals[rows]
            out = out + spread_rows(pos, target_parts(v), CROWS)
        t2[...] = target_join(out, CROWS)

    @pl.when(lax.axis_index("sec") >= FLUID_ROWS)
    def _():
        pos2[...] = jnp.zeros_like(pos2)
        t2[...] = jnp.zeros_like(t2)


def compact(t):
    nb = SLOTS // 4
    return pl.pallas_call(
        compact_kernel,
        out_shape=[jax.ShapeDtypeStruct((nb, 1, KB), I32), jax.ShapeDtypeStruct((CROWS, 128), I32)],
        scratch_shapes=[pltpu.VMEM((nb * 8, KB), F32), pltpu.VMEM((nb * 8, KB), F32)],
        compiler_params=params(),
    )(t)


def list_kernel(first, counts, lists):
    sec = lax.axis_index("sec")
    for g in range(4):
        counts[g] = 0

    @pl.when(sec >= FLUID_ROWS)
    def _():
        mine = sec - FLUID_ROWS

        def one(p, _):
            v = first[p]

            @pl.when((v >= 1024) & (((v - 1024) >> 17) == mine))
            def _():
                g = (v >> 8) & 3
                n = counts[g]
                lists[g, n] = p
                counts[g] = n + 1
            return 0

        lax.fori_loop(0, ALLP, one, 0)
        for g in range(4):
            n = counts[g]
            for i in range(QUAD):
                lists[g, n + i] = ALLP


def make_lists(first):
    return pl.pallas_call(
        list_kernel,
        in_specs=[pl.BlockSpec(memory_space=pltpu.SMEM)],
        out_specs=[pl.BlockSpec(memory_space=pltpu.SMEM)] * 2,
        out_shape=[jax.ShapeDtypeStruct((4,), I32), jax.ShapeDtypeStruct((4, LIST), I32)],
        compiler_params=params(),
    )(first)


def pair_row(ref, lists, g, i):
    rows = []
    for j in range(QUAD):
        p = lists[g, QUAD * i + j]
        rows += [ref[pl.ds(2 * p, 1), :], ref[pl.ds(2 * p + 1, 1), :]]
    return jnp.concatenate(rows, axis=1)


def advance(e, c, add, src, dst, k, total):
    r = pl.multiple_of(8 * k, 8)
    x = e[src, pl.ds(r - 8, 24), :]
    mid = x[8:16]
    rows = pl.ds(r, 8)
    if total is not None:
        total[rows, :] += mid[:, OX:OX + CX]
    e[dst, rows, :] = (
        c[4, rows, :] * mid
        + c[0, rows, :] * x[9:17]
        + c[1, rows, :] * x[7:15]
        + c[2, rows, :] * pltpu.roll(mid, HX - 1, 1)
        + c[3, rows, :] * pltpu.roll(mid, 1, 1)
        + c[5, rows, :]
    )


def coefficients(e, c, low, high, k):
    r = pl.multiple_of(8 * k, 8)
    rows = pl.ds(r, 8)
    x = e[1, pl.ds(r - 8, 24), :]
    kc, kn, ks = x[8:16], x[9:17], x[7:15]
    ke, kw = pltpu.roll(kc, HX - 1, 1), pltpu.roll(kc, 1, 1)
    vx, vy = (0.5 * DT) * e[2, rows, :], (0.5 * DT) * e[3, rows, :]
    hn, hs, he, hw = ((0.5 * DT) * (kc + v) for v in (kn, ks, ke, kw))
    an, as_ = hn - vy, hs + vy
    c0 = 1.0 - (hn + hs + he + hw) - DT * e[4, rows, :]
    at = r + iota((8, HX), 0)
    first, last = low & (at == OY), high & (at == OY + CY - 1)
    c0 = c0 + jnp.where(first, as_, 0.0) + jnp.where(last, an, 0.0)
    c[0, rows, :] = jnp.where(last, 0.0, an)
    c[1, rows, :] = jnp.where(first, 0.0, as_)
    c[2, rows, :] = he - vx
    c[3, rows, :] = hw + vx
    c[4, rows, :] = c0
    c[5, rows, :] = DT * e[5, rows, :]


def fluid_kernel(temp, cond, vx, vy, cm, dm, t_out, s_out, ext, e, c, total, pack, land, send, recv, local):
    sec, blk = lax.axis_index("sec"), lax.axis_index("blk")
    fluid = sec < FLUID_ROWS
    low = (sec == 0) | (sec == FLUID_ROWS)
    high = (sec == FLUID_ROWS - 1) | (sec == SECS - 1)
    left, right = lax.rem(blk + COLS - 1, COLS), lax.rem(blk + 1, COLS)
    bar = pltpu.get_barrier_semaphore()

    def signal(to):
        pl.semaphore_signal(bar, inc=1, device_id=to, device_id_type=MESH)

    signal((sec, left))
    signal((sec, right))

    @pl.when(jnp.logical_not(low))
    def _():
        signal((sec - 1, blk))

    @pl.when(jnp.logical_not(high))
    def _():
        signal((sec + 1, blk))

    mid_y, mid_x = slice(OY, OY + CY), slice(OX, OX + CX)
    e[0, mid_y, mid_x] = temp[...]
    e[1, mid_y, mid_x] = cond[...]
    keep = jnp.where(fluid, 1.0, 0.0)
    e[2, mid_y, mid_x] = vx[...] * keep
    e[3, mid_y, mid_x] = vy[...] * keep
    e[4, mid_y, mid_x] = cm[...]
    e[5, mid_y, mid_x] = dm[...]
    total[...] = jnp.zeros_like(total)

    pl.semaphore_wait(bar, 4 - low.astype(I32) - high.astype(I32))

    def rows_copy(src, dst, i, to):
        return pltpu.make_async_remote_copy(
            e.at[pl.ds(0, 6), pl.ds(src, 16), pl.ds(OX, CX)], e.at[pl.ds(0, 6), pl.ds(dst, 16), pl.ds(OX, CX)],
            send.at[i], recv.at[i], device_id=to, device_id_type=MESH)

    to_low = rows_copy(OY, OY + CY, 0, (sec - 1, blk))
    to_high = rows_copy(OY + CY - 16, OY - 16, 1, (sec + 1, blk))

    @pl.when(jnp.logical_not(low))
    def _():
        to_low.start()

    @pl.when(jnp.logical_not(high))
    def _():
        to_high.start()

    @pl.when(low)
    def _():
        for a in range(6):
            e[a, OY - 16:OY, mid_x] = jnp.zeros((16, CX), F32)

    @pl.when(high)
    def _():
        for a in range(6):
            e[a, OY + CY:OY + CY + 16, mid_x] = jnp.zeros((16, CX), F32)

    @pl.when(jnp.logical_not(low))
    def _():
        to_low.wait_send()
        to_high.wait_recv()

    @pl.when(jnp.logical_not(high))
    def _():
        to_high.wait_send()
        to_low.wait_recv()

    lane = iota((8, 128), 1)

    def pack_strip(k, _):
        rows = pl.ds(pl.multiple_of(8 * k, 8), 8)
        lo = jnp.zeros((8, 128), F32)
        hi = jnp.zeros((8, 128), F32)
        for a in range(6):
            here = (lane >> 4) == a
            lo = jnp.where(here, pltpu.roll(e[a, rows, OX:OX + 128], 16 * a, 1), lo)
            hi = jnp.where(here, pltpu.roll(e[a, rows, OX + CX - 128:OX + CX], 16 * a + 16, 1), hi)
        pack[0, rows, :] = lo
        pack[1, rows, :] = hi
        return 0

    lax.fori_loop(1, 37, pack_strip, 0)

    def cols_copy(i, to):
        return pltpu.make_async_remote_copy(
            pack.at[i], land.at[i], send.at[2 + i], recv.at[2 + i], device_id=to, device_id_type=MESH)

    to_left, to_right = cols_copy(0, (sec, left)), cols_copy(1, (sec, right))
    to_left.start()
    to_right.start()
    to_left.wait()
    to_right.wait()

    def unpack_strip(k, _):
        rows = pl.ds(pl.multiple_of(8 * k, 8), 8)
        lo, hi = land[0, rows, :], land[1, rows, :]
        for a in range(6):
            e[a, rows, OX + CX:] = pltpu.roll(lo, (128 - 16 * a) % 128, 1)
            e[a, rows, 0:OX] = pltpu.roll(hi, 112 - 16 * a, 1)
        return 0

    lax.fori_loop(1, 37, unpack_strip, 0)

    def coef_strip(k, _):
        coefficients(e, c, low, high, k)
        return 0

    lax.fori_loop(1, 37, coef_strip, 0)

    @pl.when(fluid)
    def _():
        def step(n, _):
            src = lax.rem(n, 2) * 6

            def strip(k, _):
                advance(e, c, None, src, 6 - src, k, total)
                return 0

            lax.fori_loop(jnp.where(n == 0, 1, 2), jnp.where(n == 0, 37, 36), strip, 0)
            return 0

        lax.fori_loop(0, FLUID_STEPS, step, 0)
        t_out[...] = e[0, mid_y, mid_x]
        s_out[...] = total[mid_y, :]

    @pl.when(jnp.logical_not(fluid))
    def _():
        first = pltpu.make_async_copy(e.at[0], ext.at[0], local.at[0])
        rest = pltpu.make_async_copy(c, ext.at[pl.ds(1, 6)], local.at[1])
        first.start()
        rest.start()
        t_out[...] = jnp.zeros_like(t_out)
        s_out[...] = jnp.zeros_like(s_out)
        first.wait()
        rest.wait()


def fluid(temp, cond, vx, vy, cm, dm):
    return pl.pallas_call(
        fluid_kernel,
        out_shape=[jax.ShapeDtypeStruct((CY, CX), F32)] * 2 + [jax.ShapeDtypeStruct((7, HY, HX), F32)],
        in_specs=[pl.BlockSpec(memory_space=pltpu.VMEM)] * 6,
        out_specs=[pl.BlockSpec(memory_space=pltpu.VMEM)] * 2 + [pl.BlockSpec(memory_space=pl.ANY)],
        scratch_shapes=[
            pltpu.VMEM((7, HY, HX), F32), pltpu.VMEM((6, HY, HX), F32), pltpu.VMEM((HY, CX), F32),
            pltpu.VMEM((2, HY, 128), F32), pltpu.VMEM((2, HY, 128), F32),
            pltpu.SemaphoreType.DMA((4,)), pltpu.SemaphoreType.DMA((4,)), pltpu.SemaphoreType.DMA((2,)),
        ],
        compiler_params=params(collective_id=0, has_side_effects=True),
    )(temp, cond, vx, vy, cm, dm)


def gather_cells(state, st):
    hi, lo = split2(state.T)
    st[:, 0:CY] = hi.astype(BF16)
    st[:, CY:2 * CY] = lo.astype(BF16)


def cell_values(st, s):
    r = onehot(iota((CY, KB), 0) == (s >> 10))
    g = dot(st[...], jnp.concatenate([r, r], axis=0))
    tile = (s & 1023) >> 7
    a = g[0:128]
    for i in range(1, CX // 128):
        a = jnp.where(tile == i, g[128 * i:128 * i + 128], a)
    return jnp.sum(jnp.where(iota((128, KB), 0) == (s & 127), a, 0.0), axis=0, keepdims=True)


def flux_kernel(total, slot, coef, prior, pos1, out, st):
    @pl.when(lax.axis_index("sec") < FLUID_ROWS)
    def _():
        gather_cells(total[...], st)
        out[...] = jnp.zeros_like(out)

        def one(b, _):
            flux = coef[b] * (cell_values(st, slot[b]) * (1.0 / FLUID_STEPS) - prior[b])
            x = spread_rows(pos1[b], split2(flux), SLOTS)
            out[...] += x[0:SLOTS] + x[SLOTS:2 * SLOTS]
            return 0

        lax.fori_loop(0, NB, one, 0)

    @pl.when(lax.axis_index("sec") >= FLUID_ROWS)
    def _():
        out[...] = jnp.zeros_like(out)


def face_flux(total, slot, coef, prior, pos1):
    return pl.pallas_call(
        flux_kernel,
        out_shape=jax.ShapeDtypeStruct((SLOTS, 128), F32),
        scratch_shapes=[pltpu.VMEM((CX, 2 * CY), BF16)],
        compiler_params=params(),
    )(total, slot, coef, prior, pos1)


def second_kernel(flux, pos2, out):
    out[...] = jnp.zeros_like(out)

    @pl.when(lax.axis_index("sec") < FLUID_ROWS)
    def _():
        def one(b, _):
            x = spread_rows(pos2[b], split2(lane_row(flux, b, 4)), CROWS)
            out[...] += x[0:CROWS] + x[CROWS:2 * CROWS]
            return 0

        lax.fori_loop(0, SLOTS // 4, one, 0)


def second(flux, pos2):
    return pl.pallas_call(
        second_kernel,
        out_shape=jax.ShapeDtypeStruct((CROWS, 128), F32),
        compiler_params=params(),
    )(flux, pos2)


def source_kernel(counts, lists, t, f, out, acc):
    sec = lax.axis_index("sec")

    @pl.when(sec >= FLUID_ROWS)
    def _():
        base = 128 * (sec - FLUID_ROWS) + 1
        n = QUAD * 256
        for g in range(4):
            acc[...] = jnp.zeros_like(acc)

            def one(i, _):
                v = pair_row(t, lists, g, i)
                hi, lo = split2(pair_row(f, lists, g, i))
                hit = iota((128, n), 0) == (v >> 10) - base
                a = jnp.concatenate([jnp.where(hit, p, 0.0).astype(BF16) for p in (hi, lo)], axis=0)
                acc[...] += dot_nt(a, onehot(iota((256, n), 0) == (v & 255)))
                return 0

            lax.fori_loop(0, (counts[g] + QUAD - 1) // QUAD, one, 0)
            out[:, 256 * g:256 * (g + 1)] = acc[0:128] + acc[128:256]

    @pl.when(sec < FLUID_ROWS)
    def _():
        out[...] = jnp.zeros_like(out)


def wall_source(counts, lists, t, f):
    return pl.pallas_call(
        source_kernel,
        in_specs=[pl.BlockSpec(memory_space=pltpu.SMEM)] * 2 + [pl.BlockSpec(memory_space=pltpu.VMEM)] * 2,
        out_shape=jax.ShapeDtypeStruct((128, CX), F32),
        scratch_shapes=[pltpu.VMEM((256, 256), F32)],
        compiler_params=params(),
    )(counts, lists, t, f)


def wall_kernel(counts, lists, t, state, out):
    sec = lax.axis_index("sec")
    out[...] = jnp.zeros_like(out)

    @pl.when(sec >= FLUID_ROWS)
    def _():
        base = 128 * (sec - FLUID_ROWS) + 1
        n = QUAD * 256
        for g in range(4):
            table = transposed_parts(state[:, 256 * g:256 * (g + 1)])

            def one(i, _):
                v = pair_row(t, lists, g, i)
                r = onehot(iota((128, n), 0) == (v >> 10) - base)
                x = dot(table, jnp.concatenate([r, r], axis=0))
                x = jnp.where(((v >> 7) & 1) == 1, x[128:256], x[0:128])
                x = jnp.sum(jnp.where(iota((128, n), 0) == (v & 127), x, 0.0), axis=0, keepdims=True)
                for j in range(QUAD):
                    p = lists[g, QUAD * i + j]
                    out[pl.ds(2 * p, 1), :] = x[:, 256 * j:256 * j + 128]
                    out[pl.ds(2 * p + 1, 1), :] = x[:, 256 * j + 128:256 * j + 256]
                return 0

            lax.fori_loop(0, (counts[g] + QUAD - 1) // QUAD, one, 0)


def wall_values(counts, lists, t, state):
    return pl.pallas_call(
        wall_kernel,
        in_specs=[pl.BlockSpec(memory_space=pltpu.SMEM)] * 2 + [pl.BlockSpec(memory_space=pltpu.VMEM)] * 2,
        out_shape=jax.ShapeDtypeStruct((2 * ALLP + 8, 128), F32),
        compiler_params=params(),
    )(counts, lists, t, state)


def solid_kernel(source, t_fluid, ext, t_out, e, c, x, pack, land, send, recv, local):
    sec, blk = lax.axis_index("sec"), lax.axis_index("blk")
    solid = sec >= FLUID_ROWS
    mid_y, mid_x = slice(OY, OY + CY), slice(OX, OX + CX)

    @pl.when(jnp.logical_not(solid))
    def _():
        t_out[...] = t_fluid[...]

    @pl.when(solid)
    def _():
        left, right = lax.rem(blk + COLS - 1, COLS), lax.rem(blk + 1, COLS)
        other = 2 * FLUID_ROWS + 1 - sec
        bar = pltpu.get_barrier_semaphore()
        for to in ((sec, left), (sec, right), (other, blk)):
            pl.semaphore_signal(bar, inc=1, device_id=to, device_id_type=MESH)
        first = pltpu.make_async_copy(ext.at[0], e.at[0], local.at[0])
        rest = pltpu.make_async_copy(ext.at[pl.ds(1, 6)], c, local.at[1])
        first.start()
        rest.start()
        x[0:OY] = jnp.zeros((OY, HX), F32)
        x[OY + 128:OY + CY] = jnp.zeros((CY - 128, HX), F32)
        x[OY:OY + 128, mid_x] = DT * source[...]

        @pl.when(sec == SECS - 1)
        def _():
            x[OY + CY:] = jnp.zeros((HY - OY - CY, HX), F32)

        pl.semaphore_wait(bar, 3)
        up = pltpu.make_async_remote_copy(
            x.at[pl.ds(OY, 16), pl.ds(OX, CX)], x.at[pl.ds(OY + CY, 16), pl.ds(OX, CX)],
            send.at[2], recv.at[2], device_id=(other, blk), device_id_type=MESH)

        @pl.when(sec == SECS - 1)
        def _():
            up.start()
            up.wait_send()

        @pl.when(sec == FLUID_ROWS)
        def _():
            up.wait_recv()

        for at, fro, size in ((0, OY, 128), (128, OY + CY, 16)):
            pack[0, at:at + size] = x[fro:fro + size, OX:OX + 128]
            pack[1, at:at + size] = x[fro:fro + size, OX + CX - 128:OX + CX]

        def cols_copy(i, to):
            return pltpu.make_async_remote_copy(
                pack.at[i], land.at[i], send.at[i], recv.at[i], device_id=to, device_id_type=MESH)

        to_left, to_right = cols_copy(0, (sec, left)), cols_copy(1, (sec, right))
        to_left.start()
        to_right.start()
        to_left.wait()
        to_right.wait()
        for at, fro, size in ((0, OY, 128), (128, OY + CY, 16)):
            x[fro:fro + size, OX + CX:] = land[0, at:at + size]
            x[fro:fro + size, 0:OX] = land[1, at:at + size]
        first.wait()
        rest.wait()

        def drive(k, _):
            rows = pl.ds(pl.multiple_of(8 * k, 8), 8)
            c[5, rows, :] += x[rows, :]
            return 0

        lax.fori_loop(2, 36, drive, 0)

        def step(n, _):
            src = lax.rem(n, 2)

            def strip(k, _):
                advance(e, c, None, src, 1 - src, k, None)
                return 0

            lax.fori_loop(2, 36, strip, 0)
            return 0

        lax.fori_loop(0, SOLID_STEPS, step, 0)
        t_out[...] = e[0, mid_y, mid_x]


def solid_steps(source, t_fluid, ext):
    return pl.pallas_call(
        solid_kernel,
        out_shape=jax.ShapeDtypeStruct((CY, CX), F32),
        in_specs=[pl.BlockSpec(memory_space=pltpu.VMEM)] * 2 + [pl.BlockSpec(memory_space=pl.ANY)],
        out_specs=pl.BlockSpec(memory_space=pltpu.VMEM),
        scratch_shapes=[
            pltpu.VMEM((2, HY, HX), F32), pltpu.VMEM((6, HY, HX), F32), pltpu.VMEM((HY, HX), F32),
            pltpu.VMEM((2, 144, 128), F32), pltpu.VMEM((2, 144, 128), F32),
            pltpu.SemaphoreType.DMA((3,)), pltpu.SemaphoreType.DMA((3,)), pltpu.SemaphoreType.DMA((2,)),
        ],
        compiler_params=params(collective_id=1, has_side_effects=True),
    )(source, t_fluid, ext)


def back_kernel(v, pos2, out):
    out[...] = jnp.zeros_like(out)

    @pl.when(lax.axis_index("sec") < FLUID_ROWS)
    def _():
        vt = transposed_parts(v[0] + v[1])

        def one(b, _):
            put_lane_row(out, b, 4, pick(vt, pos2[b], CROWS))
            return 0

        lax.fori_loop(0, SLOTS // 4, one, 0)


def back(v, pos2):
    return pl.pallas_call(
        back_kernel,
        out_shape=jax.ShapeDtypeStruct((SLOTS, 128), F32),
        compiler_params=params(),
    )(v, pos2)


def final_kernel(v, pos1, state, slot, out, st):
    @pl.when(lax.axis_index("sec") < FLUID_ROWS)
    def _():
        vt = transposed_parts(v[...])

        def one(b, _):
            out[b] = pick(vt, pos1[b], SLOTS)
            return 0

        lax.fori_loop(0, NB, one, 0)

    @pl.when(lax.axis_index("sec") >= FLUID_ROWS)
    def _():
        gather_cells(state[...], st)

        def one(b, _):
            out[b] = cell_values(st, slot[b])
            return 0

        lax.fori_loop(0, NB, one, 0)


def final(v, pos1, state, slot):
    return pl.pallas_call(
        final_kernel,
        out_shape=jax.ShapeDtypeStruct((NB, 1, KB), F32),
        scratch_shapes=[pltpu.VMEM((CX, 2 * CY), BF16)],
        compiler_params=params(),
    )(v, pos1, state, slot)


def over_blk(x):
    return lax.all_to_all(x.reshape(COLS, BROWS, 128), "blk", split_axis=0, concat_axis=0, tiled=True).reshape(SLOTS, 128)


def to_solid(x):
    y = lax.all_gather(x, "sec", axis=0, tiled=True)[:FLUID_ROWS * CROWS]
    return jnp.pad(y, ((0, 8), (0, 0)))


def body(temp, cond, vx, vy, slot, lateral, dest, coef, prior):
    slot, lateral, dest, coef, prior = (v.reshape(NB, 1, KB) for v in (slot, lateral, dest, coef, prior))
    cm, dm, pos1, tb = prep(slot, coef, prior, lateral, dest)
    t_fluid, total, ext = fluid(temp, cond, vx, vy, cm, dm)
    pos2, t2 = compact(over_blk(tb))
    t3 = to_solid(t2)
    counts, lists = make_lists(t3[:2 * ALLP].reshape(ALLP, 256)[:, 0])
    flux = face_flux(total, slot, coef, prior, pos1)
    f3 = to_solid(second(over_blk(flux), pos2))
    source = wall_source(counts, lists, t3, f3)
    t_new = solid_steps(source, t_fluid, ext)
    values = wall_values(counts, lists, t3, t_new[:128])
    reply = jnp.pad(values[:2 * ALLP].reshape(FLUID_ROWS, CROWS, 128), ((0, 2), (0, 0), (0, 0)))
    mine = lax.all_to_all(reply, "sec", split_axis=0, concat_axis=0, tiled=True)[FLUID_ROWS:]
    wall = final(over_blk(back(mine, pos2)), pos1, t_new, slot)
    return t_new, wall.reshape(FACES)


def solution(mesh):
    block, face = P("sec", "blk"), P(("sec", "blk"))
    in_specs = (block, block, block, block, face, P(("sec", "blk"), None), face, face, face)
    return jax.shard_map(body, mesh=mesh, in_specs=in_specs, out_specs=(block, face), check_vma=False)
```

```python
import functools

import jax
import jax.numpy as jnp
from jax import lax
from jax.experimental import pallas as pl
from jax.experimental.pallas import tpu as pltpu
from jax.sharding import PartitionSpec as P

F32, BF16, I32 = jnp.float32, jnp.bfloat16, jnp.int32
MESH = pl.DeviceIdType.MESH
NT = (((1,), (1,)), ((), ()))

CY, CX = 256, 1024
FACES = 8192
FLUID_ROWS, SECS, COLS = 6, 8, 16
FLUID_STEPS, SOLID_STEPS = 10, 4
DT = 0.2
FROWS = FACES // 128
KR = 512
HALO = 16
BROWS = 8
SLOTS = COLS * BROWS
PAIRS = 56
CROWS = 2 * PAIRS
ALLP = FLUID_ROWS * PAIRS
QUAD = 4
LROWS = 4
HY, OY, TILES = 304, 24, 9
VLIM = 60 << 20


def params(**kw):
    return pltpu.CompilerParams(vmem_limit_bytes=VLIM, **kw)


def iota(shape, dim):
    return lax.broadcasted_iota(I32, shape, dim)


def split2(x):
    hi = x.astype(BF16).astype(F32)
    return hi, (x - hi).astype(BF16).astype(F32)


def onehot(mask):
    return jnp.where(mask, 1.0, 0.0).astype(BF16)


def dot(a, b):
    return jnp.dot(a, b, preferred_element_type=F32)


def dot_nt(a, b):
    return lax.dot_general(a, b, NT, preferred_element_type=F32)


def lane_row(ref, b, n):
    return jnp.concatenate([ref[pl.ds(n * b + i, 1), :] for i in range(n)], axis=1)


def put_lane_row(ref, b, n, v):
    for i in range(n):
        ref[pl.ds(n * b + i, 1), :] = v[:, i * 128:(i + 1) * 128]


def ranks(group, nb, ng, o_ref, p_ref):
    for b in range(nb):
        o_ref[b * ng:(b + 1) * ng, :] = jnp.where(iota((ng, KR), 0) == group(b), 1.0, 0.0)
    o = o_ref[...].astype(BF16)
    p_ref[...] = dot(o, onehot(iota((KR, KR), 0) < iota((KR, KR), 1)))
    return dot(o, onehot(iota((KR, 128), 0) >= 0))


def ranked(b, ng, carry, o_ref, p_ref):
    rows = slice(b * ng, (b + 1) * ng)
    place = p_ref[rows] + jnp.concatenate([carry] * (KR // 128), axis=1)
    return jnp.sum(o_ref[rows] * place, axis=0, keepdims=True).astype(I32)


def spread_rows(pos, pieces, rows):
    k = pos.shape[1]
    hit = iota((rows, k), 0) == (pos >> 7)
    a = jnp.concatenate([jnp.where(hit, v, 0.0).astype(BF16) for v in pieces], axis=0)
    return dot_nt(a, onehot(iota((128, k), 0) == (pos & 127)))


def spread_all(pos, parts_of, n_parts, rows, total_rows, out):
    out[...] = jnp.zeros_like(out)

    def one(b, _):
        out[...] += spread_rows(lane_row(pos, b, 16), parts_of(b), rows)
        return 0

    lax.fori_loop(0, total_rows // 16, one, 0)


def pick(vt, pos, rows):
    k = pos.shape[1]
    r = onehot(iota((rows, k), 0) == (pos >> 7))
    g = dot(vt, jnp.concatenate([r, r], axis=0))
    return jnp.sum(jnp.where(iota((128, k), 0) == (pos & 127), g, 0.0), axis=0, keepdims=True)


def pick_all(vt, pos, rows, total_rows, out):
    def one(b, _):
        put_lane_row(out, b, 16, pick(vt, lane_row(pos, b, 16), rows))
        return 0

    lax.fori_loop(0, total_rows // 16, one, 0)


def transposed_parts(v):
    hi, lo = split2(v.T)
    return jnp.concatenate([hi, lo], axis=1).astype(BF16)


def target_parts(t):
    return (t >> 10).astype(F32), ((t >> 5) & 31).astype(F32), (t & 31).astype(F32)


def target_join(x, rows):
    return (x[0:rows] * 1024.0 + x[rows:2 * rows] * 32.0 + x[2 * rows:3 * rows]).astype(I32)


def gather_cells(tile_of, st):
    for j in range(CX // 128):
        hi, lo = split2(tile_of(j).T)
        st[128 * j:128 * j + 128, 0:CY] = hi.astype(BF16)
        st[128 * j:128 * j + 128, CY:2 * CY] = lo.astype(BF16)


def cell_values(st, s):
    k = s.shape[1]
    r = onehot(iota((CY, k), 0) == (s >> 10))
    g = dot(st[...], jnp.concatenate([r, r], axis=0))
    tile = (s & 1023) >> 7
    a = g[0:128]
    for i in range(1, CX // 128):
        a = jnp.where(tile == i, g[128 * i:128 * i + 128], a)
    return jnp.sum(jnp.where(iota((128, k), 0) == (s & 127), a, 0.0), axis=0, keepdims=True)


def signal(to):
    pl.semaphore_signal(pltpu.get_barrier_semaphore(), inc=1, device_id=to, device_id_type=MESH)


def arrive(ref, sem):
    pltpu.make_async_copy(ref, ref, sem).wait()


def push(src, dst, send, recv, to):
    copy = pltpu.make_async_remote_copy(src, dst, send, recv, device_id=to, device_id_type=MESH)
    copy.start()
    return copy


def exchange(src, land, send, recv, sec, blk):
    def one(q, _):
        @pl.when(q != blk)
        def _():
            push(src.at[pl.ds(pl.multiple_of(q * BROWS, 8), BROWS)], land.at[pl.ds(pl.multiple_of(blk * BROWS, 8), BROWS)],
                 send, recv, (sec, q))
        return 0

    lax.fori_loop(0, COLS, one, 0)
    own = pl.ds(pl.multiple_of(blk * BROWS, 8), BROWS)
    land[own, :] = src[own, :]
    arrive(src.at[pl.ds(0, SLOTS - BROWS)], send)
    arrive(land.at[pl.ds(0, SLOTS - BROWS)], recv)


def greet_peers(sec, blk):
    def one(q, _):
        @pl.when(q != blk)
        def _():
            signal((sec, q))
        return 0

    lax.fori_loop(0, COLS, one, 0)


def lane_roll(x, n):
    return pltpu.roll(x, n % 128, 1)


def beside(x):
    lane = iota((8, 128), 1)
    east, west = [lane_roll(v, 127) for v in x], [lane_roll(v, 1) for v in x]
    e = [jnp.where(lane == 127, east[(j + 1) % TILES], east[j]) for j in range(TILES)]
    w = [jnp.where(lane == 0, west[j - 1], west[j]) for j in range(TILES)]
    return e, w


def advance(src, dst, c, total, r):
    rows = pl.ds(r, 8)
    x = [src[j, rows, :] for j in range(TILES)]
    e, w = beside(x)
    for j in range(TILES):
        n, s = src[j, pl.ds(r + 1, 8), :], src[j, pl.ds(r - 1, 8), :]
        if total is not None and j < TILES - 1:
            total[j, rows, :] += x[j]
        dst[j, rows, :] = (
            (c[4, j, rows, :] * x[j] + c[0, j, rows, :] * n)
            + (c[1, j, rows, :] * s + c[2, j, rows, :] * e[j])
            + (c[3, j, rows, :] * w[j] + c[5, j, rows, :])
        )


def strips(fn, first, count, unroll):
    def body(i, _):
        for u in range(unroll):
            fn(pl.multiple_of(8 * first + 8 * unroll * i + 8 * u, 8))
        return 0

    lax.fori_loop(0, count // unroll, body, 0)


def substeps(a, b, c, total, count):
    def two(i, _):
        strips(lambda r: advance(a, b, c, total, r), 1, 36, 6)
        strips(lambda r: advance(b, a, c, total, r), 1, 36, 6)
        return 0

    lax.fori_loop(0, count // 2, two, 0)


def coefficients(e, c, low, high, r):
    rows = pl.ds(r, 8)
    x = [e[1, j, rows, :] for j in range(TILES)]
    east, west = beside(x)
    at = r + iota((8, 128), 0)
    first, last = low & (at == OY), high & (at == OY + CY - 1)
    h = 0.5 * DT
    for j in range(TILES):
        hn, hs = h * (x[j] + e[1, j, pl.ds(r + 1, 8), :]), h * (x[j] + e[1, j, pl.ds(r - 1, 8), :])
        he, hw = h * (x[j] + east[j]), h * (x[j] + west[j])
        vx, vy = h * e[2, j, rows, :], h * e[3, j, rows, :]
        an, as_ = hn - vy, hs + vy
        c0 = 1.0 - ((hn + hs) + (he + hw)) - DT * e[4, j, rows, :]
        c[0, j, rows, :] = jnp.where(last, 0.0, an)
        c[1, j, rows, :] = jnp.where(first, 0.0, as_)
        c[2, j, rows, :] = he - vx
        c[3, j, rows, :] = hw + vx
        c[4, j, rows, :] = c0 + jnp.where(first, as_, 0.0) + jnp.where(last, an, 0.0)
        c[5, j, rows, :] = DT * e[5, j, rows, :]


def compact(t, pos, t2, o_ref, p_ref, out):
    nb, ng = SLOTS // 4, 8

    def group(b):
        v = lane_row(t, b, 4)
        return jnp.where(v >= 1024, ((v - 1024) >> 17) * 4 + ((v >> 8) & 3), -1)

    totals = ranks(group, nb, ng, o_ref, p_ref)
    count = jnp.zeros((ng, 128), F32)
    for b in range(nb):
        count = count + totals[b * ng:(b + 1) * ng]
    units = ((count.astype(I32) + 255) >> 8).astype(F32).astype(BF16)
    carry = dot(onehot(iota((ng, ng), 1) < iota((ng, ng), 0)), units) * 256.0
    for b in range(nb):
        put_lane_row(pos, b, 4, jnp.where(lane_row(t, b, 4) >= 1024, ranked(b, ng, carry, o_ref, p_ref), -1))
        carry = carry + totals[b * ng:(b + 1) * ng]
    spread_all(pos, lambda b: target_parts(lane_row(t, b, 16)), 3, CROWS, SLOTS, out)
    t2[...] = target_join(out[...], CROWS)


def fluid_kernel(temp, cond, vx, vy, slot, coef, prior, lateral, dest,
                 t_out, s_out, ext, pos1, pos2, t3,
                 e, t_b, c, total, acc, pack, land, packm, landm, tb, tb_land, p2, p2_land, t2, o_ref, p_ref, tb_out, t2_out,
                 send, recv, face_send, face_recv, local):
    sec, blk = lax.axis_index("sec"), lax.axis_index("blk")
    fluid = sec < FLUID_ROWS
    solid = jnp.logical_not(fluid)
    low = (sec == 0) | (sec == FLUID_ROWS)
    high = (sec == FLUID_ROWS - 1) | (sec == SECS - 1)
    has_low, has_high = jnp.logical_not(low), jnp.logical_not(high)
    left, right = lax.rem(blk + COLS - 1, COLS), lax.rem(blk + 1, COLS)
    server = FLUID_ROWS + sec // 3
    mine = 3 * (sec - FLUID_ROWS)
    other = 2 * FLUID_ROWS + 1 - sec

    signal((sec, left))
    signal((sec, right))

    @pl.when(has_low)
    def _():
        signal((sec - 1, blk))

    @pl.when(has_high)
    def _():
        signal((sec + 1, blk))

    @pl.when(fluid)
    def _():
        signal((server, blk))

    @pl.when(solid)
    def _():
        def one(i, _):
            signal((mine + i // COLS, lax.rem(i, COLS)))
            return 0

        lax.fori_loop(0, 3 * COLS, one, 0)

    mid = slice(OY, OY + CY)
    keep = jnp.where(fluid, 1.0, 0.0)
    for j in range(TILES - 1):
        tile = slice(128 * j, 128 * j + 128)
        e[0, j, mid, :] = temp[:, tile]
        e[1, j, mid, :] = cond[:, tile]
        e[2, j, mid, :] = vx[:, tile] * keep
        e[3, j, mid, :] = vy[:, tile] * keep

    @pl.when(low)
    def _():
        for a in range(6):
            for j in range(TILES - 1):
                e[a, j, OY - HALO:OY, :] = jnp.zeros((HALO, 128), F32)

    @pl.when(high)
    def _():
        for a in range(6):
            for j in range(TILES - 1):
                e[a, j, OY + CY:OY + CY + HALO, :] = jnp.zeros((HALO, 128), F32)

    pl.semaphore_wait(
        pltpu.get_barrier_semaphore(),
        4 - low.astype(I32) - high.astype(I32) + jnp.where(fluid, COLS, 3))

    def rows_copy(first, arrays, src, dst, i, to):
        return pltpu.make_async_remote_copy(
            e.at[pl.ds(first, arrays), pl.ds(0, TILES - 1), pl.ds(src, HALO)],
            e.at[pl.ds(first, arrays), pl.ds(0, TILES - 1), pl.ds(dst, HALO)],
            send.at[i], recv.at[i], device_id=to, device_id_type=MESH)

    def rows_pair(first, arrays, i):
        return (rows_copy(first, arrays, OY, OY + CY, i, (sec - 1, blk)),
                rows_copy(first, arrays, OY + CY - HALO, OY - HALO, i + 1, (sec + 1, blk)))

    def rows_start(pair):
        pl.when(has_low)(pair[0].start)
        pl.when(has_high)(pair[1].start)

    def rows_wait(pair):
        @pl.when(has_low)
        def _():
            pair[0].wait_send()
            pair[1].wait_recv()

        @pl.when(has_high)
        def _():
            pair[1].wait_send()
            pair[0].wait_recv()

    def cols_start(first, arrays, i, pack, land):
        lane = iota((8, 128), 1)

        def strip(r):
            rows = pl.ds(r, 8)
            lo = e[first, 0, rows, :]
            hi = lane_roll(e[first, TILES - 2, rows, :], HALO)
            for a in range(1, arrays):
                here = (lane >> 4) == a
                lo = jnp.where(here, lane_roll(e[first + a, 0, rows, :], HALO * a), lo)
                hi = jnp.where(here, lane_roll(e[first + a, TILES - 2, rows, :], HALO * a + HALO), hi)
            pack[0, rows, :] = lo
            pack[1, rows, :] = hi

        strips(strip, 1, 36, 4)
        return (push(pack.at[0, pl.ds(8, 288)], land.at[0, pl.ds(8, 288)], send.at[i], recv.at[i], (sec, left)),
                push(pack.at[1, pl.ds(8, 288)], land.at[1, pl.ds(8, 288)], send.at[i + 1], recv.at[i + 1], (sec, right)))

    def cols_wait(pair, first, arrays, land):
        pair[0].wait()
        pair[1].wait()
        lane = iota((8, 128), 1)

        def strip(r):
            rows = pl.ds(r, 8)
            lo, hi = land[0, rows, :], land[1, rows, :]
            for a in range(arrays):
                e[first + a, TILES - 1, rows, :] = jnp.where(
                    lane < 64, lane_roll(lo, -HALO * a), lane_roll(hi, 128 - HALO - HALO * a))

        strips(strip, 1, 36, 4)

    static_rows = rows_pair(0, 4, 0)
    rows_start(static_rows)

    acc[...] = jnp.zeros_like(acc)

    def maps(b, _):
        s, k = lane_row(slot, b, 8), lane_row(coef, b, 8)
        parts = split2(k) + split2(k * lane_row(prior, b, 8))
        hit = iota((CY, 1024), 0) == (s >> 10)
        a = jnp.concatenate([jnp.where(hit, v, 0.0).astype(BF16) for v in parts], axis=0)
        acc[...] += dot_nt(a, onehot(iota((CX, 1024), 0) == (s & 1023)))
        return 0

    lax.fori_loop(0, 4, maps, 0)
    rows_wait(static_rows)
    static_cols = cols_start(0, 4, 2, pack, land)
    lax.fori_loop(4, 8, maps, 0)
    for j in range(TILES - 1):
        tile = slice(128 * j, 128 * j + 128)
        e[4, j, mid, :] = acc[0:CY, tile] + acc[CY:2 * CY, tile]
        e[5, j, mid, :] = acc[2 * CY:3 * CY, tile] + acc[3 * CY:4 * CY, tile]
    map_rows = rows_pair(4, 2, 4)
    rows_start(map_rows)
    cols_wait(static_cols, 0, 4, land)

    totals = ranks(lambda b: lane_row(lateral, b, 4), FROWS // 4, COLS, o_ref, p_ref)
    carry = jnp.zeros((COLS, 128), F32)
    for b in range(FROWS // 4):
        put_lane_row(pos1, b, 4, lane_row(lateral, b, 4) * (BROWS * 128) + ranked(b, COLS, carry, o_ref, p_ref))
        carry = carry + totals[b * COLS:(b + 1) * COLS]

    rows_wait(map_rows)
    map_cols = cols_start(4, 2, 6, packm, landm)
    spread_all(pos1, lambda b: target_parts(lane_row(dest, b, 16) + 1024), 3, SLOTS, FROWS, tb_out)

    @pl.when(fluid)
    def _():
        tb[...] = target_join(tb_out[...], SLOTS)

        def one(q, _):
            push(tb.at[pl.ds(pl.multiple_of(q * BROWS, 8), BROWS)],
                 tb_land.at[pl.ds(pl.multiple_of(lax.rem(sec, 3) * SLOTS + blk * BROWS, 8), BROWS)],
                 face_send.at[0], face_recv.at[0], (server, q))
            return 0

        lax.fori_loop(0, COLS, one, 0)

    cols_wait(map_cols, 4, 2, landm)
    strips(lambda r: coefficients(e, c, low, high, r), 1, 36, 4)

    @pl.when(fluid)
    def _():
        total[...] = jnp.zeros_like(total)
        substeps(e.at[0], t_b, c, total, FLUID_STEPS)
        for j in range(TILES - 1):
            t_out[:, 128 * j:128 * j + 128] = e[0, j, mid, :]
            s_out[j] = total[j, mid, :]
        arrive(tb, face_send.at[0])
        arrive(p2_land, face_recv.at[1])
        pos2[...] = p2_land[...]
        t3[...] = jnp.zeros_like(t3)

    @pl.when(solid)
    def _():
        first = pltpu.make_async_copy(e.at[0], ext.at[0], local.at[0])
        rest = pltpu.make_async_copy(c, ext.at[pl.ds(1, 6)], local.at[1])
        first.start()
        rest.start()
        t_out[...] = jnp.zeros_like(t_out)
        s_out[...] = jnp.zeros_like(s_out)
        pos2[...] = jnp.zeros_like(pos2)
        arrive(tb_land, face_recv.at[0])
        for i in range(3):
            t = tb_land.at[pl.ds(i * SLOTS, SLOTS)]
            compact(t, p2.at[i], t2.at[0, pl.ds(i * CROWS, CROWS)], o_ref, p_ref, t2_out)
            push(p2.at[i], p2_land, face_send.at[1], face_recv.at[1], (mine + i, blk))
        swap = push(t2.at[0], t2.at[1], face_send.at[2], face_recv.at[2], (other, blk))
        arrive(p2, face_send.at[1])
        swap.wait()
        half = 3 * CROWS

        @pl.when(sec == FLUID_ROWS)
        def _():
            t3[0:half] = t2[0]
            t3[half:2 * half] = t2[1]

        @pl.when(sec == SECS - 1)
        def _():
            t3[0:half] = t2[1]
            t3[half:2 * half] = t2[0]

        t3[2 * half:] = jnp.zeros((8, 128), I32)
        first.wait()
        rest.wait()


def fluid(temp, cond, vx, vy, slot, coef, prior, lateral, dest):
    vm = pl.BlockSpec(memory_space=pltpu.VMEM)
    return pl.pallas_call(
        fluid_kernel,
        out_shape=[
            jax.ShapeDtypeStruct((CY, CX), F32), jax.ShapeDtypeStruct((TILES - 1, CY, 128), F32),
            jax.ShapeDtypeStruct((7, TILES, HY, 128), F32),
            jax.ShapeDtypeStruct((FROWS, 128), I32), jax.ShapeDtypeStruct((SLOTS, 128), I32),
            jax.ShapeDtypeStruct((2 * ALLP + 8, 128), I32),
        ],
        in_specs=[vm] * 9,
        out_specs=[vm, vm, pl.BlockSpec(memory_space=pl.ANY), vm, vm, vm],
        scratch_shapes=[
            pltpu.VMEM((6, TILES, HY, 128), F32), pltpu.VMEM((TILES, HY, 128), F32), pltpu.VMEM((6, TILES, HY, 128), F32),
            pltpu.VMEM((TILES - 1, HY, 128), F32), pltpu.VMEM((4 * CY, CX), F32),
            pltpu.VMEM((2, HY, 128), F32), pltpu.VMEM((2, HY, 128), F32),
            pltpu.VMEM((2, HY, 128), F32), pltpu.VMEM((2, HY, 128), F32),
            pltpu.VMEM((SLOTS, 128), I32), pltpu.VMEM((3 * SLOTS, 128), I32),
            pltpu.VMEM((3, SLOTS, 128), I32), pltpu.VMEM((SLOTS, 128), I32), pltpu.VMEM((2, 3 * CROWS, 128), I32),
            pltpu.VMEM((256, KR), F32), pltpu.VMEM((256, KR), F32),
            pltpu.VMEM((3 * SLOTS, 128), F32), pltpu.VMEM((3 * CROWS, 128), F32),
            pltpu.SemaphoreType.DMA((8,)), pltpu.SemaphoreType.DMA((8,)),
            pltpu.SemaphoreType.DMA((3,)), pltpu.SemaphoreType.DMA((3,)), pltpu.SemaphoreType.DMA((2,)),
        ],
        compiler_params=params(collective_id=0, has_side_effects=True),
    )(temp, cond, vx, vy, slot, coef, prior, lateral, dest)


def list_kernel(t, counts, lists):
    sec = lax.axis_index("sec")

    @pl.when(sec < FLUID_ROWS)
    def _():
        counts[...] = jnp.zeros_like(counts)
        lists[...] = jnp.zeros_like(lists)

    @pl.when(sec >= FLUID_ROWS)
    def _():
        n = 768
        v = jnp.concatenate([t[...].T[0:8], jnp.zeros((8, n - 2 * ALLP - 8), I32)], axis=1)[0:1]
        row = iota((1, n), 1)
        ours = (v >= 1024) & (((v - 1024) >> 17) == sec - FLUID_ROWS) & ((row & 1) == 0)
        group = jnp.where(ours, (v >> 8) & 3, -1)
        member = jnp.where(iota((8, n), 0) == group, 1.0, 0.0)
        before = dot(member.astype(BF16), onehot(iota((n, n), 0) < iota((n, n), 1)))
        rank = jnp.sum(member * before, axis=0, keepdims=True).astype(I32)
        pos = jnp.where(ours, group * (LROWS * 128) + rank, -1)
        back = (row >> 1) - ALLP
        x = spread_rows(pos, ((back >> 1).astype(F32), (back & 1).astype(F32)), 4 * LROWS)
        lists[...] = (2.0 * x[0:4 * LROWS] + x[4 * LROWS:]).astype(I32) + ALLP
        counts[...] = dot(member.astype(BF16), onehot(iota((n, 128), 0) >= 0)).astype(I32)


def make_lists(t):
    return pl.pallas_call(
        list_kernel,
        out_shape=[jax.ShapeDtypeStruct((8, 128), I32), jax.ShapeDtypeStruct((4 * LROWS, 128), I32)],
        compiler_params=params(),
    )(t)


def listed(lists, g, n):
    return lists[g * LROWS + (n >> 7), n & 127]


def pair_row(ref, lists, g, i):
    rows = []
    for j in range(QUAD):
        p = listed(lists, g, QUAD * i + j)
        rows += [ref[pl.ds(2 * p, 1), :], ref[pl.ds(2 * p + 1, 1), :]]
    return jnp.concatenate(rows, axis=1)


def flux_kernel(total, slot, coef, prior, pos1, pos2, counts, f3, st, fb, land, f2, f3_land, spread, send, recv):
    sec, blk = lax.axis_index("sec"), lax.axis_index("blk")

    @pl.when(sec < FLUID_ROWS)
    def _():
        greet_peers(sec, blk)
        gather_cells(lambda j: total[j], st)
        spread[...] = jnp.zeros_like(spread)

        def one(b, _):
            value = cell_values(st, lane_row(slot, b, 8)) * (1.0 / FLUID_STEPS)
            flux = lane_row(coef, b, 8) * (value - lane_row(prior, b, 8))
            spread[...] += spread_rows(lane_row(pos1, b, 8), split2(flux), SLOTS)
            return 0

        lax.fori_loop(0, FROWS // 8, one, 0)
        fb[...] = spread[0:SLOTS] + spread[SLOTS:2 * SLOTS]
        pl.semaphore_wait(pltpu.get_barrier_semaphore(), COLS + 1)
        exchange(fb, land, send.at[0], recv.at[0], sec, blk)
        part = spread.at[pl.ds(0, 2 * CROWS)]
        spread_all(pos2, lambda b: split2(lane_row(land, b, 16)), 2, CROWS, SLOTS, part)
        f2[...] = part[0:CROWS] + part[CROWS:2 * CROWS]
        place = f3_land.at[pl.ds(pl.multiple_of(sec * CROWS, 8), CROWS)]
        a = push(f2, place, send.at[1], recv.at[1], (FLUID_ROWS, blk))
        b = push(f2, place, send.at[2], recv.at[1], (SECS - 1, blk))
        f3[...] = jnp.zeros_like(f3)
        a.wait_send()
        b.wait_send()

    @pl.when(sec >= FLUID_ROWS)
    def _():
        for r in range(FLUID_ROWS):
            signal((r, blk))
        arrive(f3_land, recv.at[1])
        f3[0:2 * ALLP] = f3_land[...]
        f3[2 * ALLP:] = jnp.zeros((8, 128), F32)


def face_flux(total, slot, coef, prior, pos1, pos2, counts):
    return pl.pallas_call(
        flux_kernel,
        out_shape=jax.ShapeDtypeStruct((2 * ALLP + 8, 128), F32),
        in_specs=[pl.BlockSpec(memory_space=pltpu.VMEM)] * 6 + [pl.BlockSpec(memory_space=pl.ANY)],
        scratch_shapes=[
            pltpu.VMEM((CX, 2 * CY), BF16), pltpu.VMEM((SLOTS, 128), F32), pltpu.VMEM((SLOTS, 128), F32),
            pltpu.VMEM((CROWS, 128), F32), pltpu.VMEM((2 * ALLP, 128), F32), pltpu.VMEM((2 * SLOTS, 128), F32),
            pltpu.SemaphoreType.DMA((3,)), pltpu.SemaphoreType.DMA((2,)),
        ],
        compiler_params=params(collective_id=1, has_side_effects=True),
    )(total, slot, coef, prior, pos1, pos2, counts)


def source_kernel(counts, lists, t, f, out, acc):
    sec = lax.axis_index("sec")

    @pl.when(sec >= FLUID_ROWS)
    def _():
        base = 128 * (sec - FLUID_ROWS) + 1
        n = QUAD * 256
        for g in range(4):
            acc[...] = jnp.zeros_like(acc)

            def one(i, _):
                v = pair_row(t, lists, g, i)
                hi, lo = split2(pair_row(f, lists, g, i))
                hit = iota((128, n), 0) == (v >> 10) - base
                a = jnp.concatenate([jnp.where(hit, p, 0.0).astype(BF16) for p in (hi, lo)], axis=0)
                acc[...] += dot_nt(a, onehot(iota((256, n), 0) == (v & 255)))
                return 0

            lax.fori_loop(0, (counts[g, 0] + QUAD - 1) // QUAD, one, 0)
            out[:, 256 * g:256 * (g + 1)] = acc[0:128] + acc[128:256]

    @pl.when(sec < FLUID_ROWS)
    def _():
        out[...] = jnp.zeros_like(out)


def wall_source(counts, lists, t, f):
    return pl.pallas_call(
        source_kernel,
        in_specs=[pl.BlockSpec(memory_space=pltpu.SMEM)] * 2 + [pl.BlockSpec(memory_space=pltpu.VMEM)] * 2,
        out_shape=jax.ShapeDtypeStruct((128, CX), F32),
        scratch_shapes=[pltpu.VMEM((256, 256), F32)],
        compiler_params=params(),
    )(counts, lists, t, f)


def wall_kernel(counts, lists, t, state, out, t_out):
    sec = lax.axis_index("sec")
    out[...] = jnp.zeros_like(out)
    t_out[...] = state[...]

    @pl.when(sec >= FLUID_ROWS)
    def _():
        base = 128 * (sec - FLUID_ROWS) + 1
        n = QUAD * 256
        for g in range(4):
            table = transposed_parts(state[0:128, 256 * g:256 * (g + 1)])

            def one(i, _):
                v = pair_row(t, lists, g, i)
                r = onehot(iota((128, n), 0) == (v >> 10) - base)
                x = dot(table, jnp.concatenate([r, r], axis=0))
                x = jnp.where(((v >> 7) & 1) == 1, x[128:256], x[0:128])
                x = jnp.sum(jnp.where(iota((128, n), 0) == (v & 127), x, 0.0), axis=0, keepdims=True)
                for j in range(QUAD):
                    p = listed(lists, g, QUAD * i + j)
                    out[pl.ds(2 * p, 1), :] = x[:, 256 * j:256 * j + 128]
                    out[pl.ds(2 * p + 1, 1), :] = x[:, 256 * j + 128:256 * j + 256]
                return 0

            lax.fori_loop(0, (counts[g, 0] + QUAD - 1) // QUAD, one, 0)


def wall_values(counts, lists, t, state):
    return pl.pallas_call(
        wall_kernel,
        in_specs=[pl.BlockSpec(memory_space=pltpu.SMEM)] * 2 + [pl.BlockSpec(memory_space=pltpu.VMEM)] * 2,
        out_shape=[jax.ShapeDtypeStruct((2 * ALLP + 8, 128), F32), jax.ShapeDtypeStruct((CY, CX), F32)],
        compiler_params=params(),
    )(counts, lists, t, state)


def solid_kernel(source, t_fluid, ext, t_out, e, c, x, pack, land, send, recv, local):
    sec, blk = lax.axis_index("sec"), lax.axis_index("blk")
    mid = slice(OY, OY + CY)

    @pl.when(sec < FLUID_ROWS)
    def _():
        t_out[...] = t_fluid[...]

    @pl.when(sec >= FLUID_ROWS)
    def _():
        left, right = lax.rem(blk + COLS - 1, COLS), lax.rem(blk + 1, COLS)
        other = 2 * FLUID_ROWS + 1 - sec
        for to in ((sec, left), (sec, right), (other, blk)):
            signal(to)
        first = pltpu.make_async_copy(ext.at[0], e.at[0], local.at[0])
        rest = pltpu.make_async_copy(ext.at[pl.ds(1, 6)], c, local.at[1])
        first.start()
        rest.start()
        for j in range(TILES):
            x[j, 0:OY] = jnp.zeros((OY, 128), F32)
            x[j, OY + 128:OY + CY] = jnp.zeros((CY - 128, 128), F32)
        for j in range(TILES - 1):
            x[j, OY:OY + 128] = DT * source[:, 128 * j:128 * j + 128]

        @pl.when(sec == SECS - 1)
        def _():
            for j in range(TILES):
                x[j, OY + CY:] = jnp.zeros((HY - OY - CY, 128), F32)

        pl.semaphore_wait(pltpu.get_barrier_semaphore(), 3)
        up = pltpu.make_async_remote_copy(
            x.at[pl.ds(0, TILES - 1), pl.ds(OY, HALO)], x.at[pl.ds(0, TILES - 1), pl.ds(OY + CY, HALO)],
            send.at[2], recv.at[2], device_id=(other, blk), device_id_type=MESH)

        @pl.when(sec == SECS - 1)
        def _():
            up.start()
            up.wait_send()

        @pl.when(sec == FLUID_ROWS)
        def _():
            up.wait_recv()

        parts = ((0, OY, 128), (128, OY + CY, HALO))
        for at, fro, size in parts:
            pack[0, at:at + size] = x[0, fro:fro + size]
            pack[1, at:at + size] = x[TILES - 2, fro:fro + size]
        to_left = push(pack.at[0], land.at[0], send.at[0], recv.at[0], (sec, left))
        to_right = push(pack.at[1], land.at[1], send.at[1], recv.at[1], (sec, right))
        to_left.wait()
        to_right.wait()
        for at, fro, size in parts:
            x[TILES - 1, fro:fro + size] = jnp.where(iota((size, 128), 1) < 64, land[0, at:at + size], land[1, at:at + size])
        first.wait()
        rest.wait()

        def drive(r):
            rows = pl.ds(r, 8)
            for j in range(TILES):
                c[5, j, rows, :] += x[j, rows, :]

        strips(drive, 2, 34, 2)
        substeps(e.at[0], e.at[1], c, None, SOLID_STEPS)
        for j in range(TILES - 1):
            t_out[:, 128 * j:128 * j + 128] = e[0, j, mid, :]


def solid_steps(source, t_fluid, ext):
    vm = pl.BlockSpec(memory_space=pltpu.VMEM)
    return pl.pallas_call(
        solid_kernel,
        out_shape=jax.ShapeDtypeStruct((CY, CX), F32),
        in_specs=[vm, vm, pl.BlockSpec(memory_space=pl.ANY)],
        out_specs=vm,
        scratch_shapes=[
            pltpu.VMEM((2, TILES, HY, 128), F32), pltpu.VMEM((6, TILES, HY, 128), F32), pltpu.VMEM((TILES, HY, 128), F32),
            pltpu.VMEM((2, 144, 128), F32), pltpu.VMEM((2, 144, 128), F32),
            pltpu.SemaphoreType.DMA((3,)), pltpu.SemaphoreType.DMA((3,)), pltpu.SemaphoreType.DMA((2,)),
        ],
        compiler_params=params(collective_id=2, has_side_effects=True),
    )(source, t_fluid, ext)


def back_kernel(values, pos1, pos2, state, slot, out, reply, fb, land, st, send, recv):
    sec, blk = lax.axis_index("sec"), lax.axis_index("blk")

    @pl.when(sec < FLUID_ROWS)
    def _():
        greet_peers(sec, blk)
        signal((FLUID_ROWS, blk))
        signal((SECS - 1, blk))
        pl.semaphore_wait(pltpu.get_barrier_semaphore(), COLS - 1)
        arrive(reply, recv.at[0])
        pick_all(transposed_parts(reply[0] + reply[1]), pos2, CROWS, SLOTS, fb)
        exchange(fb, land, send.at[1], recv.at[1], sec, blk)
        pick_all(transposed_parts(land[...]), pos1, SLOTS, FROWS, out)

    @pl.when(sec >= FLUID_ROWS)
    def _():
        pl.semaphore_wait(pltpu.get_barrier_semaphore(), FLUID_ROWS)
        for r in range(FLUID_ROWS):
            push(values.at[pl.ds(r * CROWS, CROWS)], reply.at[sec - FLUID_ROWS], send.at[0], recv.at[0], (r, blk))
        gather_cells(lambda j: state[:, 128 * j:128 * j + 128], st)

        def one(b, _):
            put_lane_row(out, b, 8, cell_values(st, lane_row(slot, b, 8)))
            return 0

        lax.fori_loop(0, FROWS // 8, one, 0)
        arrive(values.at[pl.ds(0, 2 * ALLP)], send.at[0])


def back(values, pos1, pos2, state, slot):
    return pl.pallas_call(
        back_kernel,
        out_shape=jax.ShapeDtypeStruct((FROWS, 128), F32),
        in_specs=[pl.BlockSpec(memory_space=pltpu.VMEM)] * 5,
        scratch_shapes=[
            pltpu.VMEM((2, CROWS, 128), F32), pltpu.VMEM((SLOTS, 128), F32), pltpu.VMEM((SLOTS, 128), F32),
            pltpu.VMEM((CX, 2 * CY), BF16), pltpu.SemaphoreType.DMA((2,)), pltpu.SemaphoreType.DMA((2,)),
        ],
        compiler_params=params(collective_id=3, has_side_effects=True),
    )(values, pos1, pos2, state, slot)


def body(temp, cond, vx, vy, slot, lateral, dest, coef, prior):
    slot, lateral, dest, coef, prior = (v.reshape(FROWS, 128) for v in (slot, lateral, dest, coef, prior))
    t_fluid, total, ext, pos1, pos2, t3 = fluid(temp, cond, vx, vy, slot, coef, prior, lateral, dest)
    counts, lists = make_lists(t3)
    f3 = face_flux(total, slot, coef, prior, pos1, pos2, counts)
    source = wall_source(counts, lists, t3, f3)
    t_new = solid_steps(source, t_fluid, ext)
    values, t_new = wall_values(counts, lists, t3, t_new)
    wall = back(values, pos1, pos2, t_new, slot)
    return t_new, wall.reshape(FACES)


def solution(mesh):
    block, face = P("sec", "blk"), P(("sec", "blk"))
    in_specs = (block, block, block, block, face, P(("sec", "blk"), None), face, face, face)
    return jax.shard_map(body, mesh=mesh, in_specs=in_specs, out_specs=(block, face), check_vma=False)
```

```python
import functools

import jax
import jax.numpy as jnp
from jax import lax
from jax.experimental import pallas as pl
from jax.experimental.pallas import tpu as pltpu
from jax.sharding import PartitionSpec as P

F32, BF16, I32 = jnp.float32, jnp.bfloat16, jnp.int32
MESH = pl.DeviceIdType.MESH
NT = (((1,), (1,)), ((), ()))

CY, CX = 256, 1024
FACES = 8192
FLUID_ROWS, SECS, COLS = 6, 8, 16
FLUID_STEPS, SOLID_STEPS = 10, 4
DT = 0.2
FROWS = FACES // 128
KR = 512
HALO = 16
BROWS = 8
SLOTS = COLS * BROWS
PAIRS = 56
CROWS = 2 * PAIRS
ALLP = FLUID_ROWS * PAIRS
HEAT_PAIRS, WALL_PAIRS = 10, 8
LROWS = 4
HY, OY, TILES = 304, 24, 9
VLIM = 60 << 20


def params(**kw):
    return pltpu.CompilerParams(vmem_limit_bytes=VLIM, **kw)


def iota(shape, dim):
    return lax.broadcasted_iota(I32, shape, dim)


def split2(x):
    hi = x.astype(BF16).astype(F32)
    return hi, (x - hi).astype(BF16).astype(F32)


def onehot(mask):
    return jnp.where(mask, 1.0, 0.0).astype(BF16)


def dot(a, b):
    return jnp.dot(a, b, preferred_element_type=F32)


def dot_nt(a, b):
    return lax.dot_general(a, b, NT, preferred_element_type=F32)


def lane_row(ref, b, n):
    return jnp.concatenate([ref[pl.ds(n * b + i, 1), :] for i in range(n)], axis=1)


def put_lane_row(ref, b, n, v):
    for i in range(n):
        ref[pl.ds(n * b + i, 1), :] = v[:, i * 128:(i + 1) * 128]


def ranks(group, nb, ng, o_ref, p_ref):
    for b in range(nb):
        o_ref[b * ng:(b + 1) * ng, :] = jnp.where(iota((ng, KR), 0) == group(b), 1.0, 0.0)
    o = o_ref[...].astype(BF16)
    p_ref[...] = dot(o, onehot(iota((KR, KR), 0) < iota((KR, KR), 1)))
    return dot(o, onehot(iota((KR, 128), 0) >= 0))


def ranked(b, ng, carry, o_ref, p_ref):
    rows = slice(b * ng, (b + 1) * ng)
    place = p_ref[rows] + jnp.concatenate([carry] * (KR // 128), axis=1)
    return jnp.sum(o_ref[rows] * place, axis=0, keepdims=True).astype(I32)


def spread_rows(pos, pieces, rows):
    k = pos.shape[1]
    hit = iota((rows, k), 0) == (pos >> 7)
    a = jnp.concatenate([jnp.where(hit, v, 0.0).astype(BF16) for v in pieces], axis=0)
    return dot_nt(a, onehot(iota((128, k), 0) == (pos & 127)))


def spread_all(pos, parts_of, n_parts, rows, total_rows, out):
    out[...] = jnp.zeros_like(out)

    def one(b, _):
        out[...] += spread_rows(lane_row(pos, b, 16), parts_of(b), rows)
        return 0

    lax.fori_loop(0, total_rows // 16, one, 0)


def pick(vt, pos, rows):
    k = pos.shape[1]
    r = onehot(iota((rows, k), 0) == (pos >> 7))
    g = dot(vt, jnp.concatenate([r, r], axis=0))
    return jnp.sum(jnp.where(iota((128, k), 0) == (pos & 127), g, 0.0), axis=0, keepdims=True)


def pick_all(vt, pos, rows, total_rows, out):
    def one(b, _):
        put_lane_row(out, b, 16, pick(vt, lane_row(pos, b, 16), rows))
        return 0

    lax.fori_loop(0, total_rows // 16, one, 0)


def transposed_parts(v):
    hi, lo = split2(v.T)
    return jnp.concatenate([hi, lo], axis=1).astype(BF16)


def target_parts(t):
    return (t >> 10).astype(F32), ((t >> 5) & 31).astype(F32), (t & 31).astype(F32)


def target_join(x, rows):
    return (x[0:rows] * 1024.0 + x[rows:2 * rows] * 32.0 + x[2 * rows:3 * rows]).astype(I32)


def gather_cells(tile_of, st):
    for j in range(CX // 128):
        hi, lo = split2(tile_of(j).T)
        st[128 * j:128 * j + 128, 0:CY] = hi.astype(BF16)
        st[128 * j:128 * j + 128, CY:2 * CY] = lo.astype(BF16)


def cell_values(st, s):
    k = s.shape[1]
    r = onehot(iota((CY, k), 0) == (s >> 10))
    g = dot(st[...], jnp.concatenate([r, r], axis=0))
    tile = (s & 1023) >> 7
    a = g[0:128]
    for i in range(1, CX // 128):
        a = jnp.where(tile == i, g[128 * i:128 * i + 128], a)
    return jnp.sum(jnp.where(iota((128, k), 0) == (s & 127), a, 0.0), axis=0, keepdims=True)


def signal(to):
    pl.semaphore_signal(pltpu.get_barrier_semaphore(), inc=1, device_id=to, device_id_type=MESH)


def arrive(ref, sem):
    pltpu.make_async_copy(ref, ref, sem).wait()


def push(src, dst, send, recv, to):
    copy = pltpu.make_async_remote_copy(src, dst, send, recv, device_id=to, device_id_type=MESH)
    copy.start()
    return copy


def exchange(src, land, send, recv, sec, blk):
    def one(q, _):
        @pl.when(q != blk)
        def _():
            push(src.at[pl.ds(pl.multiple_of(q * BROWS, 8), BROWS)], land.at[pl.ds(pl.multiple_of(blk * BROWS, 8), BROWS)],
                 send, recv, (sec, q))
        return 0

    lax.fori_loop(0, COLS, one, 0)
    own = pl.ds(pl.multiple_of(blk * BROWS, 8), BROWS)
    land[own, :] = src[own, :]
    arrive(src.at[pl.ds(0, SLOTS - BROWS)], send)
    arrive(land.at[pl.ds(0, SLOTS - BROWS)], recv)


def greet_peers(sec, blk):
    def one(q, _):
        @pl.when(q != blk)
        def _():
            signal((sec, q))
        return 0

    lax.fori_loop(0, COLS, one, 0)


def lane_roll(x, n):
    return pltpu.roll(x, n % 128, 1)


def beside(x):
    lane = iota((8, 128), 1)
    east, west = [lane_roll(v, 127) for v in x], [lane_roll(v, 1) for v in x]
    e = [jnp.where(lane == 127, east[(j + 1) % TILES], east[j]) for j in range(TILES)]
    w = [jnp.where(lane == 0, west[j - 1], west[j]) for j in range(TILES)]
    return e, w


def advance(src, dst, c, total, r):
    rows = pl.ds(r, 8)
    x = [src[j, rows, :] for j in range(TILES)]
    e, w = beside(x)
    for j in range(TILES):
        n, s = src[j, pl.ds(r + 1, 8), :], src[j, pl.ds(r - 1, 8), :]
        if total is not None and j < TILES - 1:
            total[j, rows, :] += x[j]
        dst[j, rows, :] = (
            (c[4, j, rows, :] * x[j] + c[0, j, rows, :] * n)
            + (c[1, j, rows, :] * s + c[2, j, rows, :] * e[j])
            + (c[3, j, rows, :] * w[j] + c[5, j, rows, :])
        )


def strips(fn, first, count, unroll):
    def body(i, _):
        for u in range(unroll):
            fn(pl.multiple_of(8 * first + 8 * unroll * i + 8 * u, 8))
        return 0

    lax.fori_loop(0, count // unroll, body, 0)


def substeps(a, b, c, total, count):
    def two(i, _):
        strips(lambda r: advance(a, b, c, total, r), 1, 36, 6)
        strips(lambda r: advance(b, a, c, total, r), 1, 36, 6)
        return 0

    lax.fori_loop(0, count // 2, two, 0)


def coefficients(e, c, low, high, r):
    rows = pl.ds(r, 8)
    x = [e[1, j, rows, :] for j in range(TILES)]
    east, west = beside(x)
    at = r + iota((8, 128), 0)
    first, last = low & (at == OY), high & (at == OY + CY - 1)
    h = 0.5 * DT
    for j in range(TILES):
        hn, hs = h * (x[j] + e[1, j, pl.ds(r + 1, 8), :]), h * (x[j] + e[1, j, pl.ds(r - 1, 8), :])
        he, hw = h * (x[j] + east[j]), h * (x[j] + west[j])
        vx, vy = h * e[2, j, rows, :], h * e[3, j, rows, :]
        an, as_ = hn - vy, hs + vy
        c0 = 1.0 - ((hn + hs) + (he + hw))
        c[0, j, rows, :] = jnp.where(last, 0.0, an)
        c[1, j, rows, :] = jnp.where(first, 0.0, as_)
        c[2, j, rows, :] = he - vx
        c[3, j, rows, :] = hw + vx
        c[4, j, rows, :] = c0 + jnp.where(first, as_, 0.0) + jnp.where(last, an, 0.0)


def face_terms(e, c, r):
    rows = pl.ds(r, 8)
    for j in range(TILES):
        c[4, j, rows, :] -= DT * e[4, j, rows, :]
        c[5, j, rows, :] = DT * e[5, j, rows, :]


def compact(t, pos, t2, o_ref, p_ref, out):
    nb, ng = SLOTS // 4, 8

    def group(b):
        v = lane_row(t, b, 4)
        return jnp.where(v >= 1024, ((v - 1024) >> 17) * 4 + ((v >> 8) & 3), -1)

    totals = ranks(group, nb, ng, o_ref, p_ref)
    count = jnp.zeros((ng, 128), F32)
    for b in range(nb):
        count = count + totals[b * ng:(b + 1) * ng]
    units = ((count.astype(I32) + 255) >> 8).astype(F32).astype(BF16)
    carry = dot(onehot(iota((ng, ng), 1) < iota((ng, ng), 0)), units) * 256.0
    for b in range(nb):
        put_lane_row(pos, b, 4, jnp.where(lane_row(t, b, 4) >= 1024, ranked(b, ng, carry, o_ref, p_ref), -1))
        carry = carry + totals[b * ng:(b + 1) * ng]
    spread_all(pos, lambda b: target_parts(lane_row(t, b, 16)), 3, CROWS, SLOTS, out)
    t2[...] = target_join(out[...], CROWS)


def fluid_kernel(temp, cond, vx, vy, slot, coef, prior, lateral, dest,
                 t_out, s_out, ext, pos1, pos2, t3,
                 e, t_b, c, total, acc, pack, land, packm, landm, tb, tb_land, p2, p2_land, t2, o_ref, p_ref, tb_out, t2_out,
                 send, recv, face_send, face_recv, local):
    sec, blk = lax.axis_index("sec"), lax.axis_index("blk")
    fluid = sec < FLUID_ROWS
    solid = jnp.logical_not(fluid)
    low = (sec == 0) | (sec == FLUID_ROWS)
    high = (sec == FLUID_ROWS - 1) | (sec == SECS - 1)
    has_low, has_high = jnp.logical_not(low), jnp.logical_not(high)
    left, right = lax.rem(blk + COLS - 1, COLS), lax.rem(blk + 1, COLS)
    server = FLUID_ROWS + sec // 3
    mine = 3 * (sec - FLUID_ROWS)
    other = 2 * FLUID_ROWS + 1 - sec

    signal((sec, left))
    signal((sec, right))

    @pl.when(has_low)
    def _():
        signal((sec - 1, blk))

    @pl.when(has_high)
    def _():
        signal((sec + 1, blk))

    @pl.when(fluid)
    def _():
        signal((server, blk))

    @pl.when(solid)
    def _():
        def one(i, _):
            signal((mine + i // COLS, lax.rem(i, COLS)))
            return 0

        lax.fori_loop(0, 3 * COLS, one, 0)

    mid = slice(OY, OY + CY)
    keep = jnp.where(fluid, 1.0, 0.0)
    for j in range(TILES - 1):
        tile = slice(128 * j, 128 * j + 128)
        e[0, j, mid, :] = temp[:, tile]
        e[1, j, mid, :] = cond[:, tile]
        e[2, j, mid, :] = vx[:, tile] * keep
        e[3, j, mid, :] = vy[:, tile] * keep

    @pl.when(low)
    def _():
        for a in range(6):
            for j in range(TILES - 1):
                e[a, j, OY - HALO:OY, :] = jnp.zeros((HALO, 128), F32)

    @pl.when(high)
    def _():
        for a in range(6):
            for j in range(TILES - 1):
                e[a, j, OY + CY:OY + CY + HALO, :] = jnp.zeros((HALO, 128), F32)

    pl.semaphore_wait(
        pltpu.get_barrier_semaphore(),
        4 - low.astype(I32) - high.astype(I32) + jnp.where(fluid, COLS, 3))

    def rows_copy(first, arrays, src, dst, i, to):
        return pltpu.make_async_remote_copy(
            e.at[pl.ds(first, arrays), pl.ds(0, TILES - 1), pl.ds(src, HALO)],
            e.at[pl.ds(first, arrays), pl.ds(0, TILES - 1), pl.ds(dst, HALO)],
            send.at[i], recv.at[i], device_id=to, device_id_type=MESH)

    def rows_pair(first, arrays, i):
        return (rows_copy(first, arrays, OY, OY + CY, i, (sec - 1, blk)),
                rows_copy(first, arrays, OY + CY - HALO, OY - HALO, i + 1, (sec + 1, blk)))

    def rows_start(pair):
        pl.when(has_low)(pair[0].start)
        pl.when(has_high)(pair[1].start)

    def rows_wait(pair):
        @pl.when(has_low)
        def _():
            pair[0].wait_send()
            pair[1].wait_recv()

        @pl.when(has_high)
        def _():
            pair[1].wait_send()
            pair[0].wait_recv()

    def cols_start(first, arrays, i, pack, land):
        lane = iota((8, 128), 1)

        def strip(r):
            rows = pl.ds(r, 8)
            lo = e[first, 0, rows, :]
            hi = lane_roll(e[first, TILES - 2, rows, :], HALO)
            for a in range(1, arrays):
                here = (lane >> 4) == a
                lo = jnp.where(here, lane_roll(e[first + a, 0, rows, :], HALO * a), lo)
                hi = jnp.where(here, lane_roll(e[first + a, TILES - 2, rows, :], HALO * a + HALO), hi)
            pack[0, rows, :] = lo
            pack[1, rows, :] = hi

        strips(strip, 1, 36, 4)
        return (push(pack.at[0, pl.ds(8, 288)], land.at[0, pl.ds(8, 288)], send.at[i], recv.at[i], (sec, left)),
                push(pack.at[1, pl.ds(8, 288)], land.at[1, pl.ds(8, 288)], send.at[i + 1], recv.at[i + 1], (sec, right)))

    def cols_wait(pair, first, arrays, land):
        pair[0].wait()
        pair[1].wait()
        lane = iota((8, 128), 1)

        def strip(r):
            rows = pl.ds(r, 8)
            lo, hi = land[0, rows, :], land[1, rows, :]
            for a in range(arrays):
                e[first + a, TILES - 1, rows, :] = jnp.where(
                    lane < 64, lane_roll(lo, -HALO * a), lane_roll(hi, 128 - HALO - HALO * a))

        strips(strip, 1, 36, 4)

    def maps(b, _):
        s, k = lane_row(slot, b, 8), lane_row(coef, b, 8)
        parts = split2(k) + split2(k * lane_row(prior, b, 8))
        hit = iota((CY, 1024), 0) == (s >> 10)
        a = jnp.concatenate([jnp.where(hit, v, 0.0).astype(BF16) for v in parts], axis=0)
        acc[...] += dot_nt(a, onehot(iota((CX, 1024), 0) == (s & 1023)))
        return 0

    static_rows, map_rows = rows_pair(0, 4, 0), rows_pair(4, 2, 4)

    def place_maps():
        for j in range(TILES - 1):
            tile = slice(128 * j, 128 * j + 128)
            e[4, j, mid, :] = acc[0:CY, tile] + acc[CY:2 * CY, tile]
            e[5, j, mid, :] = acc[2 * CY:3 * CY, tile] + acc[3 * CY:4 * CY, tile]

    def all_coefficients():
        rows_start(map_rows)
        strips(lambda r: coefficients(e, c, low, high, r), 1, 18, 3)
        rows_wait(map_rows)
        map_cols = cols_start(4, 2, 6, packm, landm)
        strips(lambda r: coefficients(e, c, low, high, r), 19, 18, 3)
        cols_wait(map_cols, 4, 2, landm)
        strips(lambda r: face_terms(e, c, r), 1, 36, 4)

    rows_start(static_rows)
    acc[...] = jnp.zeros_like(acc)

    @pl.when(fluid)
    def _():
        totals = ranks(lambda b: lane_row(lateral, b, 4), FROWS // 4, COLS, o_ref, p_ref)
        carry = jnp.zeros((COLS, 128), F32)
        for b in range(FROWS // 4):
            put_lane_row(pos1, b, 4, lane_row(lateral, b, 4) * (BROWS * 128) + ranked(b, COLS, carry, o_ref, p_ref))
            carry = carry + totals[b * COLS:(b + 1) * COLS]
        spread_all(pos1, lambda b: target_parts(lane_row(dest, b, 16) + 1024), 3, SLOTS, FROWS, tb_out)
        tb[...] = target_join(tb_out[...], SLOTS)

        def one(q, _):
            push(tb.at[pl.ds(pl.multiple_of(q * BROWS, 8), BROWS)],
                 tb_land.at[pl.ds(pl.multiple_of(lax.rem(sec, 3) * SLOTS + blk * BROWS, 8), BROWS)],
                 face_send.at[0], face_recv.at[0], (server, q))
            return 0

        lax.fori_loop(0, COLS, one, 0)

    @pl.when(solid)
    def _():
        pos1[...] = jnp.zeros_like(pos1)

    lax.fori_loop(0, 4, maps, 0)
    rows_wait(static_rows)
    static_cols = cols_start(0, 4, 2, pack, land)

    @pl.when(fluid)
    def _():
        lax.fori_loop(4, 8, maps, 0)
        place_maps()

    @pl.when(solid)
    def _():
        arrive(tb_land, face_recv.at[0])
        for i in range(3):
            t = tb_land.at[pl.ds(i * SLOTS, SLOTS)]
            compact(t, p2.at[i], t2.at[0, pl.ds(i * CROWS, CROWS)], o_ref, p_ref, t2_out)
            push(p2.at[i], p2_land, face_send.at[1], face_recv.at[1], (mine + i, blk))
        push(t2.at[0], t2.at[1], face_send.at[2], face_recv.at[2], (other, blk))
        lax.fori_loop(4, 8, maps, 0)
        place_maps()

    cols_wait(static_cols, 0, 4, land)
    all_coefficients()

    @pl.when(fluid)
    def _():
        total[...] = jnp.zeros_like(total)
        substeps(e.at[0], t_b, c, total, FLUID_STEPS)
        for j in range(TILES - 1):
            t_out[:, 128 * j:128 * j + 128] = e[0, j, mid, :]
            s_out[j] = total[j, mid, :]
        t3[...] = jnp.zeros_like(t3)
        arrive(tb, face_send.at[0])
        arrive(p2_land, face_recv.at[1])
        pos2[...] = p2_land[...]

    @pl.when(solid)
    def _():
        rest = pltpu.make_async_copy(c, ext.at[pl.ds(1, 6)], local.at[1])
        rest.start()
        strips(lambda r: advance(e.at[0], t_b, c, None, r), 1, 36, 6)
        first = pltpu.make_async_copy(t_b, ext.at[0], local.at[0])
        first.start()
        t_out[...] = jnp.zeros_like(t_out)
        s_out[...] = jnp.zeros_like(s_out)
        pos2[...] = jnp.zeros_like(pos2)
        arrive(p2, face_send.at[1])
        arrive(t2.at[0], face_send.at[2])
        arrive(t2.at[1], face_recv.at[2])
        half = 3 * CROWS

        @pl.when(sec == FLUID_ROWS)
        def _():
            t3[0:half] = t2[0]
            t3[half:2 * half] = t2[1]

        @pl.when(sec == SECS - 1)
        def _():
            t3[0:half] = t2[1]
            t3[half:2 * half] = t2[0]

        t3[2 * half:] = jnp.zeros((8, 128), I32)
        first.wait()
        rest.wait()


def fluid(temp, cond, vx, vy, slot, coef, prior, lateral, dest):
    vm = pl.BlockSpec(memory_space=pltpu.VMEM)
    return pl.pallas_call(
        fluid_kernel,
        out_shape=[
            jax.ShapeDtypeStruct((CY, CX), F32), jax.ShapeDtypeStruct((TILES - 1, CY, 128), F32),
            jax.ShapeDtypeStruct((7, TILES, HY, 128), F32),
            jax.ShapeDtypeStruct((FROWS, 128), I32), jax.ShapeDtypeStruct((SLOTS, 128), I32),
            jax.ShapeDtypeStruct((2 * ALLP + 8, 128), I32),
        ],
        in_specs=[vm] * 9,
        out_specs=[vm, vm, pl.BlockSpec(memory_space=pl.ANY), vm, vm, vm],
        scratch_shapes=[
            pltpu.VMEM((6, TILES, HY, 128), F32), pltpu.VMEM((TILES, HY, 128), F32), pltpu.VMEM((6, TILES, HY, 128), F32),
            pltpu.VMEM((TILES - 1, HY, 128), F32), pltpu.VMEM((4 * CY, CX), F32),
            pltpu.VMEM((2, HY, 128), F32), pltpu.VMEM((2, HY, 128), F32),
            pltpu.VMEM((2, HY, 128), F32), pltpu.VMEM((2, HY, 128), F32),
            pltpu.VMEM((SLOTS, 128), I32), pltpu.VMEM((3 * SLOTS, 128), I32),
            pltpu.VMEM((3, SLOTS, 128), I32), pltpu.VMEM((SLOTS, 128), I32), pltpu.VMEM((2, 3 * CROWS, 128), I32),
            pltpu.VMEM((256, KR), F32), pltpu.VMEM((256, KR), F32),
            pltpu.VMEM((3 * SLOTS, 128), F32), pltpu.VMEM((3 * CROWS, 128), F32),
            pltpu.SemaphoreType.DMA((8,)), pltpu.SemaphoreType.DMA((8,)),
            pltpu.SemaphoreType.DMA((3,)), pltpu.SemaphoreType.DMA((3,)), pltpu.SemaphoreType.DMA((2,)),
        ],
        compiler_params=params(collective_id=0, has_side_effects=True),
    )(temp, cond, vx, vy, slot, coef, prior, lateral, dest)


def list_kernel(t, counts, lists):
    sec = lax.axis_index("sec")

    @pl.when(sec < FLUID_ROWS)
    def _():
        counts[...] = jnp.zeros_like(counts)
        lists[...] = jnp.zeros_like(lists)

    @pl.when(sec >= FLUID_ROWS)
    def _():
        n = 768
        v = jnp.concatenate([t[...].T[0:8], jnp.zeros((8, n - 2 * ALLP - 8), I32)], axis=1)[0:1]
        row = iota((1, n), 1)
        ours = (v >= 1024) & (((v - 1024) >> 17) == sec - FLUID_ROWS) & ((row & 1) == 0)
        group = jnp.where(ours, (v >> 8) & 3, -1)
        member = jnp.where(iota((8, n), 0) == group, 1.0, 0.0)
        before = dot(member.astype(BF16), onehot(iota((n, n), 0) < iota((n, n), 1)))
        rank = jnp.sum(member * before, axis=0, keepdims=True).astype(I32)
        pos = jnp.where(ours, group * (LROWS * 128) + rank, -1)
        back = (row >> 1) - ALLP
        x = spread_rows(pos, ((back >> 1).astype(F32), (back & 1).astype(F32)), 4 * LROWS)
        lists[...] = (2.0 * x[0:4 * LROWS] + x[4 * LROWS:]).astype(I32) + ALLP
        counts[...] = dot(member.astype(BF16), onehot(iota((n, 128), 0) >= 0)).astype(I32)


def make_lists(t):
    return pl.pallas_call(
        list_kernel,
        out_shape=[jax.ShapeDtypeStruct((8, 128), I32), jax.ShapeDtypeStruct((4 * LROWS, 128), I32)],
        compiler_params=params(),
    )(t)


def listed(lists, g, n):
    return lists[g * LROWS + (n >> 7), n & 127]


def pair_row(ref, lists, g, i, n):
    rows = []
    for j in range(n):
        p = listed(lists, g, n * i + j)
        rows += [ref[pl.ds(2 * p, 1), :], ref[pl.ds(2 * p + 1, 1), :]]
    return jnp.concatenate(rows, axis=1)


def flux_kernel(total, slot, coef, prior, pos1, pos2, counts, f3, st, fb, land, f2, f3_land, spread, send, recv):
    sec, blk = lax.axis_index("sec"), lax.axis_index("blk")

    @pl.when(sec < FLUID_ROWS)
    def _():
        greet_peers(sec, blk)
        gather_cells(lambda j: total[j], st)
        spread[...] = jnp.zeros_like(spread)

        def one(b, _):
            value = cell_values(st, lane_row(slot, b, 8)) * (1.0 / FLUID_STEPS)
            flux = lane_row(coef, b, 8) * (value - lane_row(prior, b, 8))
            spread[...] += spread_rows(lane_row(pos1, b, 8), split2(flux), SLOTS)
            return 0

        lax.fori_loop(0, FROWS // 8, one, 0)
        fb[...] = spread[0:SLOTS] + spread[SLOTS:2 * SLOTS]
        pl.semaphore_wait(pltpu.get_barrier_semaphore(), COLS + 1)
        exchange(fb, land, send.at[0], recv.at[0], sec, blk)
        part = spread.at[pl.ds(0, 2 * CROWS)]
        spread_all(pos2, lambda b: split2(lane_row(land, b, 16)), 2, CROWS, SLOTS, part)
        f2[...] = part[0:CROWS] + part[CROWS:2 * CROWS]
        place = f3_land.at[pl.ds(pl.multiple_of(sec * CROWS, 8), CROWS)]
        a = push(f2, place, send.at[1], recv.at[1], (FLUID_ROWS, blk))
        b = push(f2, place, send.at[2], recv.at[1], (SECS - 1, blk))
        f3[...] = jnp.zeros_like(f3)
        a.wait_send()
        b.wait_send()

    @pl.when(sec >= FLUID_ROWS)
    def _():
        for r in range(FLUID_ROWS):
            signal((r, blk))
        arrive(f3_land, recv.at[1])
        f3[0:2 * ALLP] = f3_land[...]
        f3[2 * ALLP:] = jnp.zeros((8, 128), F32)


def face_flux(total, slot, coef, prior, pos1, pos2, counts):
    return pl.pallas_call(
        flux_kernel,
        out_shape=jax.ShapeDtypeStruct((2 * ALLP + 8, 128), F32),
        in_specs=[pl.BlockSpec(memory_space=pltpu.VMEM)] * 6 + [pl.BlockSpec(memory_space=pl.ANY)],
        scratch_shapes=[
            pltpu.VMEM((CX, 2 * CY), BF16), pltpu.VMEM((SLOTS, 128), F32), pltpu.VMEM((SLOTS, 128), F32),
            pltpu.VMEM((CROWS, 128), F32), pltpu.VMEM((2 * ALLP, 128), F32), pltpu.VMEM((2 * SLOTS, 128), F32),
            pltpu.SemaphoreType.DMA((3,)), pltpu.SemaphoreType.DMA((2,)),
        ],
        compiler_params=params(collective_id=1, has_side_effects=True),
    )(total, slot, coef, prior, pos1, pos2, counts)


def source_kernel(counts, lists, t, f, out, acc):
    sec = lax.axis_index("sec")

    @pl.when(sec >= FLUID_ROWS)
    def _():
        base = 128 * (sec - FLUID_ROWS) + 1
        n = HEAT_PAIRS * 256
        for g in range(4):
            acc[...] = jnp.zeros_like(acc)

            def one(i, _):
                v = pair_row(t, lists, g, i, HEAT_PAIRS)
                hi, lo = split2(pair_row(f, lists, g, i, HEAT_PAIRS))
                hit = iota((128, n), 0) == (v >> 10) - base
                a = jnp.concatenate([jnp.where(hit, p, 0.0).astype(BF16) for p in (hi, lo)], axis=0)
                acc[...] += dot_nt(a, onehot(iota((256, n), 0) == (v & 255)))
                return 0

            lax.fori_loop(0, (counts[g, 0] + HEAT_PAIRS - 1) // HEAT_PAIRS, one, 0)
            for h in range(2):
                out[2 * g + h] = DT * (acc[0:128, 128 * h:128 * h + 128] + acc[128:256, 128 * h:128 * h + 128])

    @pl.when(sec < FLUID_ROWS)
    def _():
        out[...] = jnp.zeros_like(out)


def wall_source(counts, lists, t, f):
    return pl.pallas_call(
        source_kernel,
        in_specs=[pl.BlockSpec(memory_space=pltpu.SMEM)] * 2 + [pl.BlockSpec(memory_space=pltpu.VMEM)] * 2,
        out_shape=jax.ShapeDtypeStruct((TILES - 1, 128, 128), F32),
        scratch_shapes=[pltpu.VMEM((256, 256), F32)],
        compiler_params=params(),
    )(counts, lists, t, f)


def wall_kernel(counts, lists, t, state, out, t_out):
    sec = lax.axis_index("sec")
    out[...] = jnp.zeros_like(out)
    t_out[...] = state[...]

    @pl.when(sec >= FLUID_ROWS)
    def _():
        base = 128 * (sec - FLUID_ROWS) + 1
        n = WALL_PAIRS * 256
        for g in range(4):
            table = transposed_parts(state[0:128, 256 * g:256 * (g + 1)])

            def one(i, _):
                v = pair_row(t, lists, g, i, WALL_PAIRS)
                r = onehot(iota((128, n), 0) == (v >> 10) - base)
                x = dot(table, jnp.concatenate([r, r], axis=0))
                x = jnp.where(((v >> 7) & 1) == 1, x[128:256], x[0:128])
                x = jnp.sum(jnp.where(iota((128, n), 0) == (v & 127), x, 0.0), axis=0, keepdims=True)
                for j in range(WALL_PAIRS):
                    p = listed(lists, g, WALL_PAIRS * i + j)
                    out[pl.ds(2 * p, 1), :] = x[:, 256 * j:256 * j + 128]
                    out[pl.ds(2 * p + 1, 1), :] = x[:, 256 * j + 128:256 * j + 256]
                return 0

            lax.fori_loop(0, (counts[g, 0] + WALL_PAIRS - 1) // WALL_PAIRS, one, 0)


def wall_values(counts, lists, t, state):
    return pl.pallas_call(
        wall_kernel,
        in_specs=[pl.BlockSpec(memory_space=pltpu.SMEM)] * 2 + [pl.BlockSpec(memory_space=pltpu.VMEM)] * 2,
        out_shape=[jax.ShapeDtypeStruct((2 * ALLP + 8, 128), F32), jax.ShapeDtypeStruct((CY, CX), F32)],
        compiler_params=params(),
    )(counts, lists, t, state)


def solid_kernel(heat, t_fluid, ext, t_out, e, c, side, below, corner, send, recv, local):
    sec, blk = lax.axis_index("sec"), lax.axis_index("blk")
    mid = slice(OY, OY + CY)

    @pl.when(sec < FLUID_ROWS)
    def _():
        t_out[...] = t_fluid[...]

    @pl.when(sec >= FLUID_ROWS)
    def _():
        upper, lower = FLUID_ROWS, SECS - 1
        left, right = lax.rem(blk + COLS - 1, COLS), lax.rem(blk + 1, COLS)
        first = pltpu.make_async_copy(ext.at[0], e.at[0], local.at[0])
        rest = pltpu.make_async_copy(ext.at[pl.ds(1, 6)], c, local.at[1])
        first.start()
        rest.start()
        signal((sec, left))
        signal((sec, right))

        @pl.when(sec == upper)
        def _():
            for q in (left, blk, right):
                signal((lower, q))

        pl.semaphore_wait(pltpu.get_barrier_semaphore(), jnp.where(sec == upper, 2, 5))
        end = TILES - 2
        copies = [push(heat.at[0], side.at[0], send.at[0], recv.at[0], (sec, left)),
                  push(heat.at[end], side.at[1], send.at[1], recv.at[1], (sec, right))]
        top = pl.ds(0, HALO)
        down = [
            pltpu.make_async_remote_copy(heat.at[pl.ds(0, TILES - 1), top], below, send.at[2], recv.at[2],
                                         device_id=(upper, blk), device_id_type=MESH),
            pltpu.make_async_remote_copy(heat.at[0, top], corner.at[0], send.at[3], recv.at[3],
                                         device_id=(upper, left), device_id_type=MESH),
            pltpu.make_async_remote_copy(heat.at[end, top], corner.at[1], send.at[4], recv.at[4],
                                         device_id=(upper, right), device_id_type=MESH)]

        @pl.when(sec == lower)
        def _():
            for d in down:
                d.start()

        first.wait()
        rest.wait()

        def warm(j, rows, x):
            e[0, j, rows, :] += x
            c[5, j, rows, :] += x

        for j in range(TILES - 1):
            warm(j, slice(OY, OY + 128), heat[j])
        for d in copies:
            d.wait()
        warm(TILES - 1, slice(OY, OY + 128), jnp.where(iota((128, 128), 1) < 64, side[0], side[1]))

        @pl.when(sec == lower)
        def _():
            for d in down:
                d.wait_send()

        @pl.when(sec == upper)
        def _():
            for d in down:
                d.wait_recv()
            last = slice(OY + CY, OY + CY + HALO)
            for j in range(TILES - 1):
                warm(j, last, below[j])
            warm(TILES - 1, last, jnp.where(iota((HALO, 128), 1) < 64, corner[0], corner[1]))

        for n in range(SOLID_STEPS - 1):
            strips(lambda r: advance(e.at[n % 2], e.at[1 - n % 2], c, None, r), 1, 36, 6)
        for j in range(TILES - 1):
            t_out[:, 128 * j:128 * j + 128] = e[(SOLID_STEPS - 1) % 2, j, mid, :]


def solid_steps(heat, t_fluid, ext):
    vm = pl.BlockSpec(memory_space=pltpu.VMEM)
    return pl.pallas_call(
        solid_kernel,
        out_shape=jax.ShapeDtypeStruct((CY, CX), F32),
        in_specs=[vm, vm, pl.BlockSpec(memory_space=pl.ANY)],
        out_specs=vm,
        scratch_shapes=[
            pltpu.VMEM((2, TILES, HY, 128), F32), pltpu.VMEM((6, TILES, HY, 128), F32),
            pltpu.VMEM((2, 128, 128), F32), pltpu.VMEM((TILES - 1, HALO, 128), F32), pltpu.VMEM((2, HALO, 128), F32),
            pltpu.SemaphoreType.DMA((5,)), pltpu.SemaphoreType.DMA((5,)), pltpu.SemaphoreType.DMA((2,)),
        ],
        compiler_params=params(collective_id=2, has_side_effects=True),
    )(heat, t_fluid, ext)


def back_kernel(values, pos1, pos2, state, slot, out, reply, fb, land, st, send, recv):
    sec, blk = lax.axis_index("sec"), lax.axis_index("blk")

    @pl.when(sec < FLUID_ROWS)
    def _():
        greet_peers(sec, blk)
        signal((FLUID_ROWS, blk))
        signal((SECS - 1, blk))
        pl.semaphore_wait(pltpu.get_barrier_semaphore(), COLS - 1)
        arrive(reply, recv.at[0])
        pick_all(transposed_parts(reply[0] + reply[1]), pos2, CROWS, SLOTS, fb)
        exchange(fb, land, send.at[1], recv.at[1], sec, blk)
        pick_all(transposed_parts(land[...]), pos1, SLOTS, FROWS, out)

    @pl.when(sec >= FLUID_ROWS)
    def _():
        pl.semaphore_wait(pltpu.get_barrier_semaphore(), FLUID_ROWS)
        for r in range(FLUID_ROWS):
            push(values.at[pl.ds(r * CROWS, CROWS)], reply.at[sec - FLUID_ROWS], send.at[0], recv.at[0], (r, blk))
        gather_cells(lambda j: state[:, 128 * j:128 * j + 128], st)

        def one(b, _):
            put_lane_row(out, b, 8, cell_values(st, lane_row(slot, b, 8)))
            return 0

        lax.fori_loop(0, FROWS // 8, one, 0)
        arrive(values.at[pl.ds(0, 2 * ALLP)], send.at[0])


def back(values, pos1, pos2, state, slot):
    return pl.pallas_call(
        back_kernel,
        out_shape=jax.ShapeDtypeStruct((FROWS, 128), F32),
        in_specs=[pl.BlockSpec(memory_space=pltpu.VMEM)] * 5,
        scratch_shapes=[
            pltpu.VMEM((2, CROWS, 128), F32), pltpu.VMEM((SLOTS, 128), F32), pltpu.VMEM((SLOTS, 128), F32),
            pltpu.VMEM((CX, 2 * CY), BF16), pltpu.SemaphoreType.DMA((2,)), pltpu.SemaphoreType.DMA((2,)),
        ],
        compiler_params=params(collective_id=3, has_side_effects=True),
    )(values, pos1, pos2, state, slot)


def body(temp, cond, vx, vy, slot, lateral, dest, coef, prior):
    slot, lateral, dest, coef, prior = (v.reshape(FROWS, 128) for v in (slot, lateral, dest, coef, prior))
    t_fluid, total, ext, pos1, pos2, t3 = fluid(temp, cond, vx, vy, slot, coef, prior, lateral, dest)
    counts, lists = make_lists(t3)
    f3 = face_flux(total, slot, coef, prior, pos1, pos2, counts)
    source = wall_source(counts, lists, t3, f3)
    t_new = solid_steps(source, t_fluid, ext)
    values, t_new = wall_values(counts, lists, t3, t_new)
    wall = back(values, pos1, pos2, t_new, slot)
    return t_new, wall.reshape(FACES)


def solution(mesh):
    block, face = P("sec", "blk"), P(("sec", "blk"))
    in_specs = (block, block, block, block, face, P(("sec", "blk"), None), face, face, face)
    return jax.shard_map(body, mesh=mesh, in_specs=in_specs, out_specs=(block, face), check_vma=False)
```

```python
import functools

import jax
import jax.numpy as jnp
from jax import lax
from jax.experimental import pallas as pl
from jax.experimental.pallas import tpu as pltpu
from jax.sharding import PartitionSpec as P

F32, BF16, I32 = jnp.float32, jnp.bfloat16, jnp.int32
MESH = pl.DeviceIdType.MESH
NT = (((1,), (1,)), ((), ()))

CY, CX = 256, 1024
FACES = 8192
FLUID_ROWS, SECS, COLS = 6, 8, 16
FLUID_STEPS, SOLID_STEPS = 10, 4
DT = 0.2
FROWS = FACES // 128
KR = 512
HALO = 16
BROWS = 8
SLOTS = COLS * BROWS
PAIRS = 56
CROWS = 2 * PAIRS
ALLP = FLUID_ROWS * PAIRS
HEAT_PAIRS, WALL_PAIRS = 10, 8
LROWS = 4
HY, OY, TILES = 304, 24, 9
VLIM = 60 << 20


def params(**kw):
    return pltpu.CompilerParams(vmem_limit_bytes=VLIM, **kw)


def iota(shape, dim):
    return lax.broadcasted_iota(I32, shape, dim)


def split2(x):
    hi = x.astype(BF16).astype(F32)
    return hi, (x - hi).astype(BF16).astype(F32)


def onehot(mask):
    return jnp.where(mask, 1.0, 0.0).astype(BF16)


def dot(a, b):
    return jnp.dot(a, b, preferred_element_type=F32)


def dot_nt(a, b):
    return lax.dot_general(a, b, NT, preferred_element_type=F32)


def lane_row(ref, b, n):
    return jnp.concatenate([ref[pl.ds(n * b + i, 1), :] for i in range(n)], axis=1)


def put_lane_row(ref, b, n, v):
    for i in range(n):
        ref[pl.ds(n * b + i, 1), :] = v[:, i * 128:(i + 1) * 128]


def ranks(group, nb, ng, o_ref, p_ref):
    for b in range(nb):
        o_ref[b * ng:(b + 1) * ng, :] = jnp.where(iota((ng, KR), 0) == group(b), 1.0, 0.0)
    o = o_ref[...].astype(BF16)
    p_ref[...] = dot(o, onehot(iota((KR, KR), 0) < iota((KR, KR), 1)))
    return dot(o, onehot(iota((KR, 128), 0) >= 0))


def ranked(b, ng, carry, o_ref, p_ref):
    rows = slice(b * ng, (b + 1) * ng)
    place = p_ref[rows] + jnp.concatenate([carry] * (KR // 128), axis=1)
    return jnp.sum(o_ref[rows] * place, axis=0, keepdims=True).astype(I32)


def spread_rows(pos, pieces, rows):
    k = pos.shape[1]
    hit = iota((rows, k), 0) == (pos >> 7)
    a = jnp.concatenate([jnp.where(hit, v, 0.0).astype(BF16) for v in pieces], axis=0)
    return dot_nt(a, onehot(iota((128, k), 0) == (pos & 127)))


def spread_all(pos, parts_of, n_parts, rows, total_rows, out):
    out[...] = jnp.zeros_like(out)

    def one(b, _):
        out[...] += spread_rows(lane_row(pos, b, 16), parts_of(b), rows)
        return 0

    lax.fori_loop(0, total_rows // 16, one, 0)


def pick(vt, pos, rows):
    k = pos.shape[1]
    r = onehot(iota((rows, k), 0) == (pos >> 7))
    g = dot(vt, jnp.concatenate([r, r], axis=0))
    return jnp.sum(jnp.where(iota((128, k), 0) == (pos & 127), g, 0.0), axis=0, keepdims=True)


def pick_all(vt, pos, rows, total_rows, out):
    def one(b, _):
        put_lane_row(out, b, 16, pick(vt, lane_row(pos, b, 16), rows))
        return 0

    lax.fori_loop(0, total_rows // 16, one, 0)


def transposed_parts(v):
    hi, lo = split2(v.T)
    return jnp.concatenate([hi, lo], axis=1).astype(BF16)


def target_parts(t):
    return (t >> 10).astype(F32), ((t >> 5) & 31).astype(F32), (t & 31).astype(F32)


def target_join(x, rows):
    return (x[0:rows] * 1024.0 + x[rows:2 * rows] * 32.0 + x[2 * rows:3 * rows]).astype(I32)


def gather_cells(tile_of, st):
    for j in range(CX // 128):
        hi, lo = split2(tile_of(j).T)
        st[128 * j:128 * j + 128, 0:CY] = hi.astype(BF16)
        st[128 * j:128 * j + 128, CY:2 * CY] = lo.astype(BF16)


def cell_values(st, s):
    k = s.shape[1]
    r = onehot(iota((CY, k), 0) == (s >> 10))
    g = dot(st[...], jnp.concatenate([r, r], axis=0))
    tile = (s & 1023) >> 7
    a = g[0:128]
    for i in range(1, CX // 128):
        a = jnp.where(tile == i, g[128 * i:128 * i + 128], a)
    return jnp.sum(jnp.where(iota((128, k), 0) == (s & 127), a, 0.0), axis=0, keepdims=True)


def signal(to):
    pl.semaphore_signal(pltpu.get_barrier_semaphore(), inc=1, device_id=to, device_id_type=MESH)


def arrive(ref, sem):
    pltpu.make_async_copy(ref, ref, sem).wait()


def push(src, dst, send, recv, to):
    copy = pltpu.make_async_remote_copy(src, dst, send, recv, device_id=to, device_id_type=MESH)
    copy.start()
    return copy


def exchange(src, land, send, recv, sec, blk):
    def one(q, _):
        @pl.when(q != blk)
        def _():
            push(src.at[pl.ds(pl.multiple_of(q * BROWS, 8), BROWS)], land.at[pl.ds(pl.multiple_of(blk * BROWS, 8), BROWS)],
                 send, recv, (sec, q))
        return 0

    lax.fori_loop(0, COLS, one, 0)
    own = pl.ds(pl.multiple_of(blk * BROWS, 8), BROWS)
    land[own, :] = src[own, :]
    arrive(src.at[pl.ds(0, SLOTS - BROWS)], send)
    arrive(land.at[pl.ds(0, SLOTS - BROWS)], recv)


def greet_peers(sec, blk):
    def one(q, _):
        @pl.when(q != blk)
        def _():
            signal((sec, q))
        return 0

    lax.fori_loop(0, COLS, one, 0)


def lane_roll(x, n):
    return pltpu.roll(x, n % 128, 1)


def beside(x):
    lane = iota((8, 128), 1)
    east, west = [lane_roll(v, 127) for v in x], [lane_roll(v, 1) for v in x]
    e = [jnp.where(lane == 127, east[(j + 1) % TILES], east[j]) for j in range(TILES)]
    w = [jnp.where(lane == 0, west[j - 1], west[j]) for j in range(TILES)]
    return e, w


def advance(src, dst, c, total, r):
    rows = pl.ds(r, 8)
    x = [src[j, rows, :] for j in range(TILES)]
    e, w = beside(x)
    for j in range(TILES):
        n, s = src[j, pl.ds(r + 1, 8), :], src[j, pl.ds(r - 1, 8), :]
        if total is not None and j < TILES - 1:
            total[j, rows, :] += x[j]
        dst[j, rows, :] = (
            (c[4, j, rows, :] * x[j] + c[0, j, rows, :] * n)
            + (c[1, j, rows, :] * s + c[2, j, rows, :] * e[j])
            + (c[3, j, rows, :] * w[j] + c[5, j, rows, :])
        )


def strips(fn, first, count, unroll):
    def body(i, _):
        for u in range(unroll):
            fn(pl.multiple_of(8 * first + 8 * unroll * i + 8 * u, 8))
        return 0

    lax.fori_loop(0, count // unroll, body, 0)


def substeps(a, b, c, total, count):
    def two(i, _):
        strips(lambda r: advance(a, b, c, total, r), 1, 36, 12)
        strips(lambda r: advance(b, a, c, total, r), 1, 36, 12)
        return 0

    lax.fori_loop(0, count // 2, two, 0)


def coefficients(e, c, low, high, r):
    rows = pl.ds(r, 8)
    x = [e[1, j, rows, :] for j in range(TILES)]
    east, west = beside(x)
    at = r + iota((8, 128), 0)
    first, last = low & (at == OY), high & (at == OY + CY - 1)
    h = 0.5 * DT
    for j in range(TILES):
        hn, hs = h * (x[j] + e[1, j, pl.ds(r + 1, 8), :]), h * (x[j] + e[1, j, pl.ds(r - 1, 8), :])
        he, hw = h * (x[j] + east[j]), h * (x[j] + west[j])
        vx, vy = h * e[2, j, rows, :], h * e[3, j, rows, :]
        an, as_ = hn - vy, hs + vy
        c0 = 1.0 - ((hn + hs) + (he + hw))
        c[0, j, rows, :] = jnp.where(last, 0.0, an)
        c[1, j, rows, :] = jnp.where(first, 0.0, as_)
        c[2, j, rows, :] = he - vx
        c[3, j, rows, :] = hw + vx
        c[4, j, rows, :] = c0 + jnp.where(first, as_, 0.0) + jnp.where(last, an, 0.0)


def face_terms(e, c, r):
    rows = pl.ds(r, 8)
    for j in range(TILES):
        c[4, j, rows, :] -= DT * e[4, j, rows, :]
        c[5, j, rows, :] = DT * e[5, j, rows, :]


def compact(t, pos, t2, o_ref, p_ref, out):
    nb, ng = SLOTS // 4, 8

    def group(b):
        v = lane_row(t, b, 4)
        return jnp.where(v >= 1024, ((v - 1024) >> 17) * 4 + ((v >> 8) & 3), -1)

    totals = ranks(group, nb, ng, o_ref, p_ref)
    count = jnp.zeros((ng, 128), F32)
    for b in range(nb):
        count = count + totals[b * ng:(b + 1) * ng]
    units = ((count.astype(I32) + 255) >> 8).astype(F32).astype(BF16)
    carry = dot(onehot(iota((ng, ng), 1) < iota((ng, ng), 0)), units) * 256.0
    for b in range(nb):
        put_lane_row(pos, b, 4, jnp.where(lane_row(t, b, 4) >= 1024, ranked(b, ng, carry, o_ref, p_ref), -1))
        carry = carry + totals[b * ng:(b + 1) * ng]
    spread_all(pos, lambda b: target_parts(lane_row(t, b, 16)), 3, CROWS, SLOTS, out)
    t2[...] = target_join(out[...], CROWS)


def list_pairs(t, counts, lists, mine):
    n = 768
    v = jnp.concatenate([t[...].T[0:8], jnp.zeros((8, n - 2 * ALLP - 8), I32)], axis=1)[0:1]
    row = iota((1, n), 1)
    ours = (v >= 1024) & (((v - 1024) >> 17) == mine) & ((row & 1) == 0)
    group = jnp.where(ours, (v >> 8) & 3, -1)
    member = jnp.where(iota((8, n), 0) == group, 1.0, 0.0)
    before = dot(member.astype(BF16), onehot(iota((n, n), 0) < iota((n, n), 1)))
    rank = jnp.sum(member * before, axis=0, keepdims=True).astype(I32)
    pos = jnp.where(ours, group * (LROWS * 128) + rank, -1)
    back = (row >> 1) - ALLP
    x = spread_rows(pos, ((back >> 1).astype(F32), (back & 1).astype(F32)), 4 * LROWS)
    lists[...] = (2.0 * x[0:4 * LROWS] + x[4 * LROWS:]).astype(I32) + ALLP
    counts[...] = dot(member.astype(BF16), onehot(iota((n, 128), 0) >= 0)).astype(I32)


def fluid_kernel(temp, cond, vx, vy, slot, coef, prior, lateral, dest,
                 t_out, s_out, ext, pos1, pos2, t3, counts, lists,
                 e, t_b, c, total, acc, pack, land, packm, landm, tb, tb_land, p2, p2_land, t2, o_ref, p_ref, tb_out, t2_out,
                 send, recv, face_send, face_recv, local):
    sec, blk = lax.axis_index("sec"), lax.axis_index("blk")
    fluid = sec < FLUID_ROWS
    solid = jnp.logical_not(fluid)
    low = (sec == 0) | (sec == FLUID_ROWS)
    high = (sec == FLUID_ROWS - 1) | (sec == SECS - 1)
    has_low, has_high = jnp.logical_not(low), jnp.logical_not(high)
    left, right = lax.rem(blk + COLS - 1, COLS), lax.rem(blk + 1, COLS)
    server = FLUID_ROWS + sec // 3
    mine = 3 * (sec - FLUID_ROWS)
    other = 2 * FLUID_ROWS + 1 - sec

    signal((sec, left))
    signal((sec, right))

    @pl.when(has_low)
    def _():
        for q in (left, blk, right):
            signal((sec - 1, q))

    @pl.when(has_high)
    def _():
        for q in (left, blk, right):
            signal((sec + 1, q))

    @pl.when(fluid)
    def _():
        signal((server, blk))

    @pl.when(solid)
    def _():
        def one(i, _):
            signal((mine + i // COLS, lax.rem(i, COLS)))
            return 0

        lax.fori_loop(0, 3 * COLS, one, 0)

    mid = slice(OY, OY + CY)
    keep = jnp.where(fluid, 1.0, 0.0)
    for j in range(TILES - 1):
        tile = slice(128 * j, 128 * j + 128)
        e[0, j, mid, :] = temp[:, tile]
        e[1, j, mid, :] = cond[:, tile]
        e[2, j, mid, :] = vx[:, tile] * keep
        e[3, j, mid, :] = vy[:, tile] * keep

    @pl.when(low)
    def _():
        for a in range(6):
            for j in range(TILES - 1):
                e[a, j, OY - HALO:OY, :] = jnp.zeros((HALO, 128), F32)
        for ref in (land, landm):
            ref[:, OY - HALO:OY, :] = jnp.zeros((2, HALO, 128), F32)

    @pl.when(high)
    def _():
        for a in range(6):
            for j in range(TILES - 1):
                e[a, j, OY + CY:OY + CY + HALO, :] = jnp.zeros((HALO, 128), F32)
        for ref in (land, landm):
            ref[:, OY + CY:OY + CY + HALO, :] = jnp.zeros((2, HALO, 128), F32)

    pl.semaphore_wait(
        pltpu.get_barrier_semaphore(),
        8 - 3 * (low.astype(I32) + high.astype(I32)) + jnp.where(fluid, COLS, 3))

    first_rows, last_rows = pl.ds(OY, HALO), pl.ds(OY + CY - HALO, HALO)
    below, above = pl.ds(OY + CY, HALO), pl.ds(OY - HALO, HALO)

    def halo_copies(first, arrays, i, pack, land):
        count = [0]

        def copy(src, dst, to):
            at = i + count[0]
            count[0] += 1
            return pltpu.make_async_remote_copy(src, dst, send.at[at], recv.at[at], device_id=to, device_id_type=MESH)

        body = e.at[pl.ds(first, arrays), pl.ds(0, TILES - 1)]
        up = [copy(body.at[:, :, first_rows], body.at[:, :, below], (sec - 1, blk))]
        down = [copy(body.at[:, :, last_rows], body.at[:, :, above], (sec + 1, blk))]
        here = []
        for side, to in ((0, left), (1, right)):
            own, there = pack.at[side], land.at[side]
            here.append(copy(own.at[pl.ds(OY, CY)], there.at[pl.ds(OY, CY)], (sec, to)))
            up.append(copy(own.at[first_rows], there.at[below], (sec - 1, to)))
            down.append(copy(own.at[last_rows], there.at[above], (sec + 1, to)))
        return here, up, down

    def halo_start(copies, first, arrays, pack):
        here, up, down = copies
        lane = iota((8, 128), 1)

        def strip(r):
            rows = pl.ds(r, 8)
            lo = e[first, 0, rows, :]
            hi = lane_roll(e[first, TILES - 2, rows, :], HALO)
            for a in range(1, arrays):
                mine = (lane >> 4) == a
                lo = jnp.where(mine, lane_roll(e[first + a, 0, rows, :], HALO * a), lo)
                hi = jnp.where(mine, lane_roll(e[first + a, TILES - 2, rows, :], HALO * a + HALO), hi)
            pack[0, rows, :] = lo
            pack[1, rows, :] = hi

        pl.when(has_low)(up[0].start)
        pl.when(has_high)(down[0].start)
        strips(strip, 3, 32, 8)
        for d in here:
            d.start()

        @pl.when(has_low)
        def _():
            for d in up[1:]:
                d.start()

        @pl.when(has_high)
        def _():
            for d in down[1:]:
                d.start()

    def halo_wait(copies, first, arrays, land):
        here, up, down = copies
        for d in here:
            d.wait()

        @pl.when(has_low)
        def _():
            for d in up:
                d.wait_send()
            for d in down:
                d.wait_recv()

        @pl.when(has_high)
        def _():
            for d in down:
                d.wait_send()
            for d in up:
                d.wait_recv()

        lane = iota((8, 128), 1)

        def strip(r):
            rows = pl.ds(r, 8)
            lo, hi = land[0, rows, :], land[1, rows, :]
            for a in range(arrays):
                e[first + a, TILES - 1, rows, :] = jnp.where(
                    lane < 64, lane_roll(lo, -HALO * a), lane_roll(hi, 128 - HALO - HALO * a))

        strips(strip, 1, 36, 6)

    def maps(b, _):
        s, k = lane_row(slot, b, 8), lane_row(coef, b, 8)
        parts = split2(k) + split2(k * lane_row(prior, b, 8))
        hit = iota((CY, 1024), 0) == (s >> 10)
        a = jnp.concatenate([jnp.where(hit, v, 0.0).astype(BF16) for v in parts], axis=0)
        acc[...] += dot_nt(a, onehot(iota((CX, 1024), 0) == (s & 1023)))
        return 0

    static, of_maps = halo_copies(0, 4, 0, pack, land), halo_copies(4, 2, 8, packm, landm)

    def place_maps():
        for j in range(TILES - 1):
            tile = slice(128 * j, 128 * j + 128)
            e[4, j, mid, :] = acc[0:CY, tile] + acc[CY:2 * CY, tile]
            e[5, j, mid, :] = acc[2 * CY:3 * CY, tile] + acc[3 * CY:4 * CY, tile]

    halo_start(static, 0, 4, pack)
    acc[...] = jnp.zeros_like(acc)

    @pl.when(fluid)
    def _():
        totals = ranks(lambda b: lane_row(lateral, b, 4), FROWS // 4, COLS, o_ref, p_ref)
        carry = jnp.zeros((COLS, 128), F32)
        for b in range(FROWS // 4):
            put_lane_row(pos1, b, 4, lane_row(lateral, b, 4) * (BROWS * 128) + ranked(b, COLS, carry, o_ref, p_ref))
            carry = carry + totals[b * COLS:(b + 1) * COLS]
        spread_all(pos1, lambda b: target_parts(lane_row(dest, b, 16) + 1024), 3, SLOTS, FROWS, tb_out)
        tb[...] = target_join(tb_out[...], SLOTS)

        def one(q, _):
            push(tb.at[pl.ds(pl.multiple_of(q * BROWS, 8), BROWS)],
                 tb_land.at[pl.ds(pl.multiple_of(lax.rem(sec, 3) * SLOTS + blk * BROWS, 8), BROWS)],
                 face_send.at[0], face_recv.at[0], (server, q))
            return 0

        lax.fori_loop(0, COLS, one, 0)

    @pl.when(solid)
    def _():
        pos1[...] = jnp.zeros_like(pos1)

    lax.fori_loop(0, 4, maps, 0)

    @pl.when(fluid)
    def _():
        lax.fori_loop(4, 8, maps, 0)
        place_maps()

    @pl.when(solid)
    def _():
        arrive(tb_land, face_recv.at[0])
        for i in range(3):
            t = tb_land.at[pl.ds(i * SLOTS, SLOTS)]
            compact(t, p2.at[i], t2.at[0, pl.ds(i * CROWS, CROWS)], o_ref, p_ref, t2_out)
            push(p2.at[i], p2_land, face_send.at[1], face_recv.at[1], (mine + i, blk))
        push(t2.at[0], t2.at[1], face_send.at[2], face_recv.at[2], (other, blk))
        lax.fori_loop(4, 8, maps, 0)
        place_maps()

    halo_start(of_maps, 4, 2, packm)
    halo_wait(static, 0, 4, land)
    strips(lambda r: coefficients(e, c, low, high, r), 1, 36, 4)
    halo_wait(of_maps, 4, 2, landm)
    strips(lambda r: face_terms(e, c, r), 1, 36, 4)

    @pl.when(fluid)
    def _():
        total[...] = jnp.zeros_like(total)
        substeps(e.at[0], t_b, c, total, FLUID_STEPS)
        for j in range(TILES - 1):
            t_out[:, 128 * j:128 * j + 128] = e[0, j, mid, :]
            s_out[j] = total[j, mid, :]
        t3[...] = jnp.zeros_like(t3)
        counts[...] = jnp.zeros_like(counts)
        lists[...] = jnp.zeros_like(lists)
        arrive(tb, face_send.at[0])
        arrive(p2_land, face_recv.at[1])
        pos2[...] = p2_land[...]

    @pl.when(solid)
    def _():
        rest = pltpu.make_async_copy(c, ext.at[pl.ds(1, 6)], local.at[1])
        rest.start()
        strips(lambda r: advance(e.at[0], t_b, c, None, r), 1, 36, 6)
        first = pltpu.make_async_copy(t_b, ext.at[0], local.at[0])
        first.start()
        t_out[...] = jnp.zeros_like(t_out)
        s_out[...] = jnp.zeros_like(s_out)
        pos2[...] = jnp.zeros_like(pos2)
        arrive(p2, face_send.at[1])
        arrive(t2.at[0], face_send.at[2])
        arrive(t2.at[1], face_recv.at[2])
        half = 3 * CROWS

        @pl.when(sec == FLUID_ROWS)
        def _():
            t3[0:half] = t2[0]
            t3[half:2 * half] = t2[1]

        @pl.when(sec == SECS - 1)
        def _():
            t3[0:half] = t2[1]
            t3[half:2 * half] = t2[0]

        t3[2 * half:] = jnp.zeros((8, 128), I32)
        list_pairs(t3, counts, lists, sec - FLUID_ROWS)
        first.wait()
        rest.wait()


def fluid(temp, cond, vx, vy, slot, coef, prior, lateral, dest):
    vm = pl.BlockSpec(memory_space=pltpu.VMEM)
    return pl.pallas_call(
        fluid_kernel,
        out_shape=[
            jax.ShapeDtypeStruct((CY, CX), F32), jax.ShapeDtypeStruct((TILES - 1, CY, 128), F32),
            jax.ShapeDtypeStruct((7, TILES, HY, 128), F32),
            jax.ShapeDtypeStruct((FROWS, 128), I32), jax.ShapeDtypeStruct((SLOTS, 128), I32),
            jax.ShapeDtypeStruct((2 * ALLP + 8, 128), I32),
            jax.ShapeDtypeStruct((8, 128), I32), jax.ShapeDtypeStruct((4 * LROWS, 128), I32),
        ],
        in_specs=[vm] * 9,
        out_specs=[vm, vm, pl.BlockSpec(memory_space=pl.ANY)] + [vm] * 5,
        scratch_shapes=[
            pltpu.VMEM((6, TILES, HY, 128), F32), pltpu.VMEM((TILES, HY, 128), F32), pltpu.VMEM((6, TILES, HY, 128), F32),
            pltpu.VMEM((TILES - 1, HY, 128), F32), pltpu.VMEM((4 * CY, CX), F32),
            pltpu.VMEM((2, HY, 128), F32), pltpu.VMEM((2, HY, 128), F32),
            pltpu.VMEM((2, HY, 128), F32), pltpu.VMEM((2, HY, 128), F32),
            pltpu.VMEM((SLOTS, 128), I32), pltpu.VMEM((3 * SLOTS, 128), I32),
            pltpu.VMEM((3, SLOTS, 128), I32), pltpu.VMEM((SLOTS, 128), I32), pltpu.VMEM((2, 3 * CROWS, 128), I32),
            pltpu.VMEM((256, KR), F32), pltpu.VMEM((256, KR), F32),
            pltpu.VMEM((3 * SLOTS, 128), F32), pltpu.VMEM((3 * CROWS, 128), F32),
            pltpu.SemaphoreType.DMA((16,)), pltpu.SemaphoreType.DMA((16,)),
            pltpu.SemaphoreType.DMA((3,)), pltpu.SemaphoreType.DMA((3,)), pltpu.SemaphoreType.DMA((2,)),
        ],
        compiler_params=params(collective_id=0, has_side_effects=True),
    )(temp, cond, vx, vy, slot, coef, prior, lateral, dest)


def listed(lists, g, n):
    return lists[g * LROWS + (n >> 7), n & 127]


def pair_row(ref, lists, g, i, n):
    rows = []
    for j in range(n):
        p = listed(lists, g, n * i + j)
        rows += [ref[pl.ds(2 * p, 1), :], ref[pl.ds(2 * p + 1, 1), :]]
    return jnp.concatenate(rows, axis=1)


def flux_kernel(total, slot, coef, prior, pos1, pos2, f3, st, fb, land, f2, f3_land, spread, send, recv):
    sec, blk = lax.axis_index("sec"), lax.axis_index("blk")

    @pl.when(sec < FLUID_ROWS)
    def _():
        greet_peers(sec, blk)
        gather_cells(lambda j: total[j], st)
        spread[...] = jnp.zeros_like(spread)

        def one(b, _):
            value = cell_values(st, lane_row(slot, b, 8)) * (1.0 / FLUID_STEPS)
            flux = lane_row(coef, b, 8) * (value - lane_row(prior, b, 8))
            spread[...] += spread_rows(lane_row(pos1, b, 8), split2(flux), SLOTS)
            return 0

        lax.fori_loop(0, FROWS // 8, one, 0)
        fb[...] = spread[0:SLOTS] + spread[SLOTS:2 * SLOTS]
        pl.semaphore_wait(pltpu.get_barrier_semaphore(), COLS + 1)
        exchange(fb, land, send.at[0], recv.at[0], sec, blk)
        part = spread.at[pl.ds(0, 2 * CROWS)]
        spread_all(pos2, lambda b: split2(lane_row(land, b, 16)), 2, CROWS, SLOTS, part)
        f2[...] = part[0:CROWS] + part[CROWS:2 * CROWS]
        place = f3_land.at[pl.ds(pl.multiple_of(sec * CROWS, 8), CROWS)]
        a = push(f2, place, send.at[1], recv.at[1], (FLUID_ROWS, blk))
        b = push(f2, place, send.at[2], recv.at[1], (SECS - 1, blk))
        f3[...] = jnp.zeros_like(f3)
        a.wait_send()
        b.wait_send()

    @pl.when(sec >= FLUID_ROWS)
    def _():
        for r in range(FLUID_ROWS):
            signal((r, blk))
        arrive(f3_land, recv.at[1])
        f3[0:2 * ALLP] = f3_land[...]
        f3[2 * ALLP:] = jnp.zeros((8, 128), F32)


def face_flux(total, slot, coef, prior, pos1, pos2):
    return pl.pallas_call(
        flux_kernel,
        out_shape=jax.ShapeDtypeStruct((2 * ALLP + 8, 128), F32),
        in_specs=[pl.BlockSpec(memory_space=pltpu.VMEM)] * 6,
        scratch_shapes=[
            pltpu.VMEM((CX, 2 * CY), BF16), pltpu.VMEM((SLOTS, 128), F32), pltpu.VMEM((SLOTS, 128), F32),
            pltpu.VMEM((CROWS, 128), F32), pltpu.VMEM((2 * ALLP, 128), F32), pltpu.VMEM((2 * SLOTS, 128), F32),
            pltpu.SemaphoreType.DMA((3,)), pltpu.SemaphoreType.DMA((2,)),
        ],
        compiler_params=params(collective_id=1, has_side_effects=True),
    )(total, slot, coef, prior, pos1, pos2)


def source_kernel(counts, lists, t, f, out, acc):
    sec = lax.axis_index("sec")

    @pl.when(sec >= FLUID_ROWS)
    def _():
        base = 128 * (sec - FLUID_ROWS) + 1
        n = HEAT_PAIRS * 256
        for g in range(4):
            acc[...] = jnp.zeros_like(acc)

            def one(i, _):
                v = pair_row(t, lists, g, i, HEAT_PAIRS)
                hi, lo = split2(pair_row(f, lists, g, i, HEAT_PAIRS))
                hit = iota((128, n), 0) == (v >> 10) - base
                a = jnp.concatenate([jnp.where(hit, p, 0.0).astype(BF16) for p in (hi, lo)], axis=0)
                acc[...] += dot_nt(a, onehot(iota((256, n), 0) == (v & 255)))
                return 0

            lax.fori_loop(0, (counts[g, 0] + HEAT_PAIRS - 1) // HEAT_PAIRS, one, 0)
            for h in range(2):
                out[2 * g + h] = DT * (acc[0:128, 128 * h:128 * h + 128] + acc[128:256, 128 * h:128 * h + 128])

    @pl.when(sec < FLUID_ROWS)
    def _():
        out[...] = jnp.zeros_like(out)


def wall_source(counts, lists, t, f):
    return pl.pallas_call(
        source_kernel,
        in_specs=[pl.BlockSpec(memory_space=pltpu.SMEM)] * 2 + [pl.BlockSpec(memory_space=pltpu.VMEM)] * 2,
        out_shape=jax.ShapeDtypeStruct((TILES - 1, 128, 128), F32),
        scratch_shapes=[pltpu.VMEM((256, 256), F32)],
        compiler_params=params(),
    )(counts, lists, t, f)


def wall_kernel(counts, lists, t, state, out, t_out):
    sec = lax.axis_index("sec")
    out[...] = jnp.zeros_like(out)
    t_out[...] = state[...]

    @pl.when(sec >= FLUID_ROWS)
    def _():
        base = 128 * (sec - FLUID_ROWS) + 1
        n = WALL_PAIRS * 256
        for g in range(4):
            table = transposed_parts(state[0:128, 256 * g:256 * (g + 1)])

            def one(i, _):
                v = pair_row(t, lists, g, i, WALL_PAIRS)
                r = onehot(iota((128, n), 0) == (v >> 10) - base)
                x = dot(table, jnp.concatenate([r, r], axis=0))
                x = jnp.where(((v >> 7) & 1) == 1, x[128:256], x[0:128])
                x = jnp.sum(jnp.where(iota((128, n), 0) == (v & 127), x, 0.0), axis=0, keepdims=True)
                for j in range(WALL_PAIRS):
                    p = listed(lists, g, WALL_PAIRS * i + j)
                    out[pl.ds(2 * p, 1), :] = x[:, 256 * j:256 * j + 128]
                    out[pl.ds(2 * p + 1, 1), :] = x[:, 256 * j + 128:256 * j + 256]
                return 0

            lax.fori_loop(0, (counts[g, 0] + WALL_PAIRS - 1) // WALL_PAIRS, one, 0)


def wall_values(counts, lists, t, state):
    return pl.pallas_call(
        wall_kernel,
        in_specs=[pl.BlockSpec(memory_space=pltpu.SMEM)] * 2 + [pl.BlockSpec(memory_space=pltpu.VMEM)] * 2,
        out_shape=[jax.ShapeDtypeStruct((2 * ALLP + 8, 128), F32), jax.ShapeDtypeStruct((CY, CX), F32)],
        compiler_params=params(),
    )(counts, lists, t, state)


def solid_kernel(heat, t_fluid, ext, t_out, e, c, side, below, corner, send, recv, local):
    sec, blk = lax.axis_index("sec"), lax.axis_index("blk")
    mid = slice(OY, OY + CY)

    @pl.when(sec < FLUID_ROWS)
    def _():
        t_out[...] = t_fluid[...]

    @pl.when(sec >= FLUID_ROWS)
    def _():
        upper, lower = FLUID_ROWS, SECS - 1
        left, right = lax.rem(blk + COLS - 1, COLS), lax.rem(blk + 1, COLS)
        first = pltpu.make_async_copy(ext.at[0], e.at[0], local.at[0])
        rest = pltpu.make_async_copy(ext.at[pl.ds(1, 6)], c, local.at[1])
        first.start()
        rest.start()
        signal((sec, left))
        signal((sec, right))

        @pl.when(sec == upper)
        def _():
            for q in (left, blk, right):
                signal((lower, q))

        pl.semaphore_wait(pltpu.get_barrier_semaphore(), jnp.where(sec == upper, 2, 5))
        end = TILES - 2
        copies = [push(heat.at[0], side.at[0], send.at[0], recv.at[0], (sec, left)),
                  push(heat.at[end], side.at[1], send.at[1], recv.at[1], (sec, right))]
        top = pl.ds(0, HALO)
        down = [
            pltpu.make_async_remote_copy(heat.at[pl.ds(0, TILES - 1), top], below, send.at[2], recv.at[2],
                                         device_id=(upper, blk), device_id_type=MESH),
            pltpu.make_async_remote_copy(heat.at[0, top], corner.at[0], send.at[3], recv.at[3],
                                         device_id=(upper, left), device_id_type=MESH),
            pltpu.make_async_remote_copy(heat.at[end, top], corner.at[1], send.at[4], recv.at[4],
                                         device_id=(upper, right), device_id_type=MESH)]

        @pl.when(sec == lower)
        def _():
            for d in down:
                d.start()

        first.wait()
        rest.wait()

        def warm(j, rows, x):
            e[0, j, rows, :] += x
            c[5, j, rows, :] += x

        for j in range(TILES - 1):
            warm(j, slice(OY, OY + 128), heat[j])
        for d in copies:
            d.wait()
        warm(TILES - 1, slice(OY, OY + 128), jnp.where(iota((128, 128), 1) < 64, side[0], side[1]))

        @pl.when(sec == lower)
        def _():
            for d in down:
                d.wait_send()

        @pl.when(sec == upper)
        def _():
            for d in down:
                d.wait_recv()
            last = slice(OY + CY, OY + CY + HALO)
            for j in range(TILES - 1):
                warm(j, last, below[j])
            warm(TILES - 1, last, jnp.where(iota((HALO, 128), 1) < 64, corner[0], corner[1]))

        for n in range(SOLID_STEPS - 1):
            strips(lambda r: advance(e.at[n % 2], e.at[1 - n % 2], c, None, r), 1, 36, 12)
        for j in range(TILES - 1):
            t_out[:, 128 * j:128 * j + 128] = e[(SOLID_STEPS - 1) % 2, j, mid, :]


def solid_steps(heat, t_fluid, ext):
    vm = pl.BlockSpec(memory_space=pltpu.VMEM)
    return pl.pallas_call(
        solid_kernel,
        out_shape=jax.ShapeDtypeStruct((CY, CX), F32),
        in_specs=[vm, vm, pl.BlockSpec(memory_space=pl.ANY)],
        out_specs=vm,
        scratch_shapes=[
            pltpu.VMEM((2, TILES, HY, 128), F32), pltpu.VMEM((6, TILES, HY, 128), F32),
            pltpu.VMEM((2, 128, 128), F32), pltpu.VMEM((TILES - 1, HALO, 128), F32), pltpu.VMEM((2, HALO, 128), F32),
            pltpu.SemaphoreType.DMA((5,)), pltpu.SemaphoreType.DMA((5,)), pltpu.SemaphoreType.DMA((2,)),
        ],
        compiler_params=params(collective_id=2, has_side_effects=True),
    )(heat, t_fluid, ext)


def back_kernel(values, pos1, pos2, state, slot, out, reply, fb, land, st, send, recv):
    sec, blk = lax.axis_index("sec"), lax.axis_index("blk")

    @pl.when(sec < FLUID_ROWS)
    def _():
        greet_peers(sec, blk)
        signal((FLUID_ROWS, blk))
        signal((SECS - 1, blk))
        pl.semaphore_wait(pltpu.get_barrier_semaphore(), COLS - 1)
        arrive(reply, recv.at[0])
        pick_all(transposed_parts(reply[0] + reply[1]), pos2, CROWS, SLOTS, fb)
        exchange(fb, land, send.at[1], recv.at[1], sec, blk)
        pick_all(transposed_parts(land[...]), pos1, SLOTS, FROWS, out)

    @pl.when(sec >= FLUID_ROWS)
    def _():
        pl.semaphore_wait(pltpu.get_barrier_semaphore(), FLUID_ROWS)
        for r in range(FLUID_ROWS):
            push(values.at[pl.ds(r * CROWS, CROWS)], reply.at[sec - FLUID_ROWS], send.at[0], recv.at[0], (r, blk))
        gather_cells(lambda j: state[:, 128 * j:128 * j + 128], st)

        def one(b, _):
            put_lane_row(out, b, 8, cell_values(st, lane_row(slot, b, 8)))
            return 0

        lax.fori_loop(0, FROWS // 8, one, 0)
        arrive(values.at[pl.ds(0, 2 * ALLP)], send.at[0])


def back(values, pos1, pos2, state, slot):
    return pl.pallas_call(
        back_kernel,
        out_shape=jax.ShapeDtypeStruct((FROWS, 128), F32),
        in_specs=[pl.BlockSpec(memory_space=pltpu.VMEM)] * 5,
        scratch_shapes=[
            pltpu.VMEM((2, CROWS, 128), F32), pltpu.VMEM((SLOTS, 128), F32), pltpu.VMEM((SLOTS, 128), F32),
            pltpu.VMEM((CX, 2 * CY), BF16), pltpu.SemaphoreType.DMA((2,)), pltpu.SemaphoreType.DMA((2,)),
        ],
        compiler_params=params(collective_id=3, has_side_effects=True),
    )(values, pos1, pos2, state, slot)


def body(temp, cond, vx, vy, slot, lateral, dest, coef, prior):
    slot, lateral, dest, coef, prior = (v.reshape(FROWS, 128) for v in (slot, lateral, dest, coef, prior))
    t_fluid, total, ext, pos1, pos2, t3, counts, lists = fluid(temp, cond, vx, vy, slot, coef, prior, lateral, dest)
    f3 = face_flux(total, slot, coef, prior, pos1, pos2)
    source = wall_source(counts, lists, t3, f3)
    t_new = solid_steps(source, t_fluid, ext)
    values, t_new = wall_values(counts, lists, t3, t_new)
    wall = back(values, pos1, pos2, t_new, slot)
    return t_new, wall.reshape(FACES)


def solution(mesh):
    block, face = P("sec", "blk"), P(("sec", "blk"))
    in_specs = (block, block, block, block, face, P(("sec", "blk"), None), face, face, face)
    return jax.shard_map(body, mesh=mesh, in_specs=in_specs, out_specs=(block, face), check_vma=False)
```

```python
import functools

import jax
import jax.numpy as jnp
from jax import lax
from jax.experimental import pallas as pl
from jax.experimental.pallas import tpu as pltpu
from jax.sharding import PartitionSpec as P

F32, BF16, I32 = jnp.float32, jnp.bfloat16, jnp.int32
MESH = pl.DeviceIdType.MESH
NT = (((1,), (1,)), ((), ()))

CY, CX = 256, 1024
FACES = 8192
FLUID_ROWS, SECS, COLS = 6, 8, 16
FLUID_STEPS, SOLID_STEPS = 10, 4
DT = 0.2
FROWS = FACES // 128
KR = 512
HALO = 16
BROWS = 6
SLOTS = COLS * BROWS
PAIRS = 56
CROWS = 2 * PAIRS
ALLP = FLUID_ROWS * PAIRS
HEAT_PAIRS, WALL_PAIRS = 10, 8
LROWS = 4
HY, OY, TILES = 304, 24, 9
VLIM = 60 << 20


def params(**kw):
    return pltpu.CompilerParams(vmem_limit_bytes=VLIM, **kw)


def iota(shape, dim):
    return lax.broadcasted_iota(I32, shape, dim)


def split2(x):
    hi = x.astype(BF16).astype(F32)
    return hi, (x - hi).astype(BF16).astype(F32)


def onehot(mask):
    return jnp.where(mask, 1.0, 0.0).astype(BF16)


def dot(a, b):
    return jnp.dot(a, b, preferred_element_type=F32)


def dot_nt(a, b):
    return lax.dot_general(a, b, NT, preferred_element_type=F32)


def lane_row(ref, b, n):
    return jnp.concatenate([ref[pl.ds(n * b + i, 1), :] for i in range(n)], axis=1)


def put_lane_row(ref, b, n, v):
    for i in range(n):
        ref[pl.ds(n * b + i, 1), :] = v[:, i * 128:(i + 1) * 128]


def ranks(group, nb, ng, o_ref, p_ref):
    for b in range(nb):
        o_ref[b * ng:(b + 1) * ng, :] = jnp.where(iota((ng, KR), 0) == group(b), 1.0, 0.0)
    o = o_ref[...].astype(BF16)
    p_ref[...] = dot(o, onehot(iota((KR, KR), 0) < iota((KR, KR), 1)))
    return dot(o, onehot(iota((KR, 128), 0) >= 0))


def ranked(b, ng, carry, o_ref, p_ref):
    rows = slice(b * ng, (b + 1) * ng)
    place = p_ref[rows] + jnp.concatenate([carry] * (KR // 128), axis=1)
    return jnp.sum(o_ref[rows] * place, axis=0, keepdims=True).astype(I32)


def spread_rows(pos, pieces, rows):
    k = pos.shape[1]
    hit = iota((rows, k), 0) == (pos >> 7)
    a = jnp.concatenate([jnp.where(hit, v, 0.0).astype(BF16) for v in pieces], axis=0)
    return dot_nt(a, onehot(iota((128, k), 0) == (pos & 127)))


def spread_all(pos, parts_of, n_parts, rows, total_rows, out):
    out[...] = jnp.zeros_like(out)

    def one(b, _):
        out[...] += spread_rows(lane_row(pos, b, 16), parts_of(b), rows)
        return 0

    lax.fori_loop(0, total_rows // 16, one, 0)


def pick(vt, pos, rows):
    k = pos.shape[1]
    r = onehot(iota((rows, k), 0) == (pos >> 7))
    g = dot(vt, jnp.concatenate([r, r], axis=0))
    return jnp.sum(jnp.where(iota((128, k), 0) == (pos & 127), g, 0.0), axis=0, keepdims=True)


def pick_all(vt, pos, rows, total_rows, out):
    def one(b, _):
        put_lane_row(out, b, 16, pick(vt, lane_row(pos, b, 16), rows))
        return 0

    lax.fori_loop(0, total_rows // 16, one, 0)


def transposed_parts(v):
    hi, lo = split2(v.T)
    return jnp.concatenate([hi, lo], axis=1).astype(BF16)


def target_parts(t):
    return (t >> 10).astype(F32), ((t >> 5) & 31).astype(F32), (t & 31).astype(F32)


def target_join(x, rows):
    return (x[0:rows] * 1024.0 + x[rows:2 * rows] * 32.0 + x[2 * rows:3 * rows]).astype(I32)


def gather_cells(tile_of, st):
    for j in range(CX // 128):
        hi, lo = split2(tile_of(j).T)
        st[128 * j:128 * j + 128, 0:CY] = hi.astype(BF16)
        st[128 * j:128 * j + 128, CY:2 * CY] = lo.astype(BF16)


def cell_values(st, s):
    k = s.shape[1]
    r = onehot(iota((CY, k), 0) == (s >> 10))
    g = dot(st[...], jnp.concatenate([r, r], axis=0))
    tile = (s & 1023) >> 7
    a = g[0:128]
    for i in range(1, CX // 128):
        a = jnp.where(tile == i, g[128 * i:128 * i + 128], a)
    return jnp.sum(jnp.where(iota((128, k), 0) == (s & 127), a, 0.0), axis=0, keepdims=True)


def signal(to):
    pl.semaphore_signal(pltpu.get_barrier_semaphore(), inc=1, device_id=to, device_id_type=MESH)


def arrive(ref, sem):
    pltpu.make_async_copy(ref, ref, sem).wait()


def push(src, dst, send, recv, to):
    copy = pltpu.make_async_remote_copy(src, dst, send, recv, device_id=to, device_id_type=MESH)
    copy.start()
    return copy


def exchange(src, land, send, recv, sec, blk):
    def one(q, _):
        @pl.when(q != blk)
        def _():
            push(src.at[pl.ds(q * BROWS, BROWS)], land.at[pl.ds(blk * BROWS, BROWS)],
                 send, recv, (sec, q))
        return 0

    lax.fori_loop(0, COLS, one, 0)
    own = pl.ds(blk * BROWS, BROWS)
    land[own, :] = src[own, :]
    arrive(src.at[pl.ds(0, SLOTS - BROWS)], send)
    arrive(land.at[pl.ds(0, SLOTS - BROWS)], recv)


def greet_peers(sec, blk):
    def one(q, _):
        @pl.when(q != blk)
        def _():
            signal((sec, q))
        return 0

    lax.fori_loop(0, COLS, one, 0)


def lane_roll(x, n):
    return pltpu.roll(x, n % 128, 1)


def beside(x):
    lane = iota((8, 128), 1)
    east, west = [lane_roll(v, 127) for v in x], [lane_roll(v, 1) for v in x]
    e = [jnp.where(lane == 127, east[(j + 1) % TILES], east[j]) for j in range(TILES)]
    w = [jnp.where(lane == 0, west[j - 1], west[j]) for j in range(TILES)]
    return e, w


def advance(src, dst, c, total, r):
    rows = pl.ds(r, 8)
    x = [src[j, rows, :] for j in range(TILES)]
    e, w = beside(x)
    for j in range(TILES):
        n, s = src[j, pl.ds(r + 1, 8), :], src[j, pl.ds(r - 1, 8), :]
        if total is not None and j < TILES - 1:
            total[j, rows, :] += x[j]
        dst[j, rows, :] = (
            (c[4, j, rows, :] * x[j] + c[0, j, rows, :] * n)
            + (c[1, j, rows, :] * s + c[2, j, rows, :] * e[j])
            + (c[3, j, rows, :] * w[j] + c[5, j, rows, :])
        )


def strips(fn, first, count, unroll):
    def body(i, _):
        for u in range(unroll):
            fn(pl.multiple_of(8 * first + 8 * unroll * i + 8 * u, 8))
        return 0

    lax.fori_loop(0, count // unroll, body, 0)


def substeps(a, b, c, total, count):
    def two(i, _):
        strips(lambda r: advance(a, b, c, total, r), 1, 36, 12)
        strips(lambda r: advance(b, a, c, total, r), 1, 36, 12)
        return 0

    lax.fori_loop(0, count // 2, two, 0)


def coefficients(e, c, low, high, r):
    rows = pl.ds(r, 8)
    x = [e[1, j, rows, :] for j in range(TILES)]
    east, west = beside(x)
    at = r + iota((8, 128), 0)
    first, last = low & (at == OY), high & (at == OY + CY - 1)
    h = 0.5 * DT
    for j in range(TILES):
        hn, hs = h * (x[j] + e[1, j, pl.ds(r + 1, 8), :]), h * (x[j] + e[1, j, pl.ds(r - 1, 8), :])
        he, hw = h * (x[j] + east[j]), h * (x[j] + west[j])
        vx, vy = h * e[2, j, rows, :], h * e[3, j, rows, :]
        an, as_ = hn - vy, hs + vy
        c0 = 1.0 - ((hn + hs) + (he + hw))
        c[0, j, rows, :] = jnp.where(last, 0.0, an)
        c[1, j, rows, :] = jnp.where(first, 0.0, as_)
        c[2, j, rows, :] = he - vx
        c[3, j, rows, :] = hw + vx
        c[4, j, rows, :] = c0 + jnp.where(first, as_, 0.0) + jnp.where(last, an, 0.0)


def face_terms(e, c, r):
    rows = pl.ds(r, 8)
    for j in range(TILES):
        c[4, j, rows, :] -= DT * e[4, j, rows, :]
        c[5, j, rows, :] = DT * e[5, j, rows, :]


def compact(t, pos, t2, o_ref, p_ref, out):
    nb, ng = SLOTS // 4, 8

    def group(b):
        v = lane_row(t, b, 4)
        return jnp.where(v >= 1024, ((v - 1024) >> 17) * 4 + ((v >> 8) & 3), -1)

    totals = ranks(group, nb, ng, o_ref, p_ref)
    count = jnp.zeros((ng, 128), F32)
    for b in range(nb):
        count = count + totals[b * ng:(b + 1) * ng]
    units = ((count.astype(I32) + 255) >> 8).astype(F32).astype(BF16)
    carry = dot(onehot(iota((ng, ng), 1) < iota((ng, ng), 0)), units) * 256.0
    for b in range(nb):
        put_lane_row(pos, b, 4, jnp.where(lane_row(t, b, 4) >= 1024, ranked(b, ng, carry, o_ref, p_ref), -1))
        carry = carry + totals[b * ng:(b + 1) * ng]
    spread_all(pos, lambda b: target_parts(lane_row(t, b, 16)), 3, CROWS, SLOTS, out)
    t2[...] = target_join(out[...], CROWS)


def list_pairs(t, counts, lists, mine):
    n = 768
    v = jnp.concatenate([t[...].T[0:8], jnp.zeros((8, n - 2 * ALLP - 8), I32)], axis=1)[0:1]
    row = iota((1, n), 1)
    ours = (v >= 1024) & (((v - 1024) >> 17) == mine) & ((row & 1) == 0)
    group = jnp.where(ours, (v >> 8) & 3, -1)
    member = jnp.where(iota((8, n), 0) == group, 1.0, 0.0)
    before = dot(member.astype(BF16), onehot(iota((n, n), 0) < iota((n, n), 1)))
    rank = jnp.sum(member * before, axis=0, keepdims=True).astype(I32)
    pos = jnp.where(ours, group * (LROWS * 128) + rank, -1)
    back = (row >> 1) - ALLP
    x = spread_rows(pos, ((back >> 1).astype(F32), (back & 1).astype(F32)), 4 * LROWS)
    lists[...] = (2.0 * x[0:4 * LROWS] + x[4 * LROWS:]).astype(I32) + ALLP
    counts[...] = dot(member.astype(BF16), onehot(iota((n, 128), 0) >= 0)).astype(I32)


def fluid_kernel(temp, cond, vx, vy, slot, coef, prior, lateral, dest,
                 t_out, s_out, ext, pos1, pos2, t3, counts, lists,
                 e, t_b, c, total, acc, pack, land, packm, landm, tb, tb_land, p2, p2_land, t2, o_ref, p_ref, tb_out, t2_out,
                 send, recv, face_send, face_recv, local):
    sec, blk = lax.axis_index("sec"), lax.axis_index("blk")
    fluid = sec < FLUID_ROWS
    solid = jnp.logical_not(fluid)
    low = (sec == 0) | (sec == FLUID_ROWS)
    high = (sec == FLUID_ROWS - 1) | (sec == SECS - 1)
    has_low, has_high = jnp.logical_not(low), jnp.logical_not(high)
    left, right = lax.rem(blk + COLS - 1, COLS), lax.rem(blk + 1, COLS)
    server = FLUID_ROWS + sec // 3
    mine = 3 * (sec - FLUID_ROWS)
    other = 2 * FLUID_ROWS + 1 - sec

    signal((sec, left))
    signal((sec, right))

    @pl.when(has_low)
    def _():
        for q in (left, blk, right):
            signal((sec - 1, q))

    @pl.when(has_high)
    def _():
        for q in (left, blk, right):
            signal((sec + 1, q))

    @pl.when(fluid)
    def _():
        signal((server, blk))

    @pl.when(solid)
    def _():
        def one(i, _):
            signal((mine + i // COLS, lax.rem(i, COLS)))
            return 0

        lax.fori_loop(0, 3 * COLS, one, 0)

    mid = slice(OY, OY + CY)
    keep = jnp.where(fluid, 1.0, 0.0)
    for j in range(TILES - 1):
        tile = slice(128 * j, 128 * j + 128)
        e[0, j, mid, :] = temp[:, tile]
        e[1, j, mid, :] = cond[:, tile]
        e[2, j, mid, :] = vx[:, tile] * keep
        e[3, j, mid, :] = vy[:, tile] * keep

    @pl.when(low)
    def _():
        for a in range(6):
            for j in range(TILES - 1):
                e[a, j, OY - HALO:OY, :] = jnp.zeros((HALO, 128), F32)
        for ref in (land, landm):
            ref[:, OY - HALO:OY, :] = jnp.zeros((2, HALO, 128), F32)

    @pl.when(high)
    def _():
        for a in range(6):
            for j in range(TILES - 1):
                e[a, j, OY + CY:OY + CY + HALO, :] = jnp.zeros((HALO, 128), F32)
        for ref in (land, landm):
            ref[:, OY + CY:OY + CY + HALO, :] = jnp.zeros((2, HALO, 128), F32)

    pl.semaphore_wait(
        pltpu.get_barrier_semaphore(),
        8 - 3 * (low.astype(I32) + high.astype(I32)) + jnp.where(fluid, COLS, 3))

    first_rows, last_rows = pl.ds(OY, HALO), pl.ds(OY + CY - HALO, HALO)
    below, above = pl.ds(OY + CY, HALO), pl.ds(OY - HALO, HALO)

    def halo_copies(first, arrays, i, pack, land):
        count = [0]

        def copy(src, dst, to):
            at = i + count[0]
            count[0] += 1
            return pltpu.make_async_remote_copy(src, dst, send.at[at], recv.at[at], device_id=to, device_id_type=MESH)

        body = e.at[pl.ds(first, arrays), pl.ds(0, TILES - 1)]
        up = [copy(body.at[:, :, first_rows], body.at[:, :, below], (sec - 1, blk))]
        down = [copy(body.at[:, :, last_rows], body.at[:, :, above], (sec + 1, blk))]
        here = []
        for side, to in ((0, left), (1, right)):
            own, there = pack.at[side], land.at[side]
            here.append(copy(own.at[pl.ds(OY, CY)], there.at[pl.ds(OY, CY)], (sec, to)))
            up.append(copy(own.at[first_rows], there.at[below], (sec - 1, to)))
            down.append(copy(own.at[last_rows], there.at[above], (sec + 1, to)))
        return here, up, down

    def halo_start(copies, first, arrays, pack):
        here, up, down = copies
        lane = iota((8, 128), 1)

        def strip(r):
            rows = pl.ds(r, 8)
            lo = e[first, 0, rows, :]
            hi = lane_roll(e[first, TILES - 2, rows, :], HALO)
            for a in range(1, arrays):
                mine = (lane >> 4) == a
                lo = jnp.where(mine, lane_roll(e[first + a, 0, rows, :], HALO * a), lo)
                hi = jnp.where(mine, lane_roll(e[first + a, TILES - 2, rows, :], HALO * a + HALO), hi)
            pack[0, rows, :] = lo
            pack[1, rows, :] = hi

        pl.when(has_low)(up[0].start)
        pl.when(has_high)(down[0].start)
        strips(strip, 3, 32, 8)
        for d in here:
            d.start()

        @pl.when(has_low)
        def _():
            for d in up[1:]:
                d.start()

        @pl.when(has_high)
        def _():
            for d in down[1:]:
                d.start()

    def halo_wait(copies, first, arrays, land):
        here, up, down = copies
        for d in here:
            d.wait()

        @pl.when(has_low)
        def _():
            for d in up:
                d.wait_send()
            for d in down:
                d.wait_recv()

        @pl.when(has_high)
        def _():
            for d in down:
                d.wait_send()
            for d in up:
                d.wait_recv()

        lane = iota((8, 128), 1)

        def strip(r):
            rows = pl.ds(r, 8)
            lo, hi = land[0, rows, :], land[1, rows, :]
            for a in range(arrays):
                e[first + a, TILES - 1, rows, :] = jnp.where(
                    lane < 64, lane_roll(lo, -HALO * a), lane_roll(hi, 128 - HALO - HALO * a))

        strips(strip, 1, 36, 6)

    def maps(b, _):
        s, k = lane_row(slot, b, 8), lane_row(coef, b, 8)
        parts = split2(k) + split2(k * lane_row(prior, b, 8))
        hit = iota((CY, 1024), 0) == (s >> 10)
        a = jnp.concatenate([jnp.where(hit, v, 0.0).astype(BF16) for v in parts], axis=0)
        acc[...] += dot_nt(a, onehot(iota((CX, 1024), 0) == (s & 1023)))
        return 0

    static, of_maps = halo_copies(0, 4, 0, pack, land), halo_copies(4, 2, 8, packm, landm)

    def place_maps():
        for j in range(TILES - 1):
            tile = slice(128 * j, 128 * j + 128)
            e[4, j, mid, :] = acc[0:CY, tile] + acc[CY:2 * CY, tile]
            e[5, j, mid, :] = acc[2 * CY:3 * CY, tile] + acc[3 * CY:4 * CY, tile]

    halo_start(static, 0, 4, pack)
    acc[...] = jnp.zeros_like(acc)

    @pl.when(fluid)
    def _():
        totals = ranks(lambda b: lane_row(lateral, b, 4), FROWS // 4, COLS, o_ref, p_ref)
        carry = jnp.zeros((COLS, 128), F32)
        for b in range(FROWS // 4):
            put_lane_row(pos1, b, 4, lane_row(lateral, b, 4) * (BROWS * 128) + ranked(b, COLS, carry, o_ref, p_ref))
            carry = carry + totals[b * COLS:(b + 1) * COLS]
        spread_all(pos1, lambda b: target_parts(lane_row(dest, b, 16) + 1024), 3, SLOTS, FROWS, tb_out)
        tb[...] = target_join(tb_out[...], SLOTS)

        def one(q, _):
            push(tb.at[pl.ds(q * BROWS, BROWS)],
                 tb_land.at[pl.ds(lax.rem(sec, 3) * SLOTS + blk * BROWS, BROWS)],
                 face_send.at[0], face_recv.at[0], (server, q))
            return 0

        lax.fori_loop(0, COLS, one, 0)

    @pl.when(solid)
    def _():
        pos1[...] = jnp.zeros_like(pos1)

    lax.fori_loop(0, 4, maps, 0)

    @pl.when(fluid)
    def _():
        lax.fori_loop(4, 8, maps, 0)
        place_maps()

    @pl.when(solid)
    def _():
        arrive(tb_land, face_recv.at[0])
        for i in range(3):
            t = tb_land.at[pl.ds(i * SLOTS, SLOTS)]
            compact(t, p2.at[i], t2.at[0, pl.ds(i * CROWS, CROWS)], o_ref, p_ref, t2_out)
            push(p2.at[i], p2_land, face_send.at[1], face_recv.at[1], (mine + i, blk))
        push(t2.at[0], t2.at[1], face_send.at[2], face_recv.at[2], (other, blk))
        lax.fori_loop(4, 8, maps, 0)
        place_maps()

    halo_start(of_maps, 4, 2, packm)
    halo_wait(static, 0, 4, land)
    strips(lambda r: coefficients(e, c, low, high, r), 1, 36, 4)
    halo_wait(of_maps, 4, 2, landm)
    strips(lambda r: face_terms(e, c, r), 1, 36, 4)

    @pl.when(fluid)
    def _():
        total[...] = jnp.zeros_like(total)
        substeps(e.at[0], t_b, c, total, FLUID_STEPS)
        for j in range(TILES - 1):
            t_out[:, 128 * j:128 * j + 128] = e[0, j, mid, :]
            s_out[j] = total[j, mid, :]
        t3[...] = jnp.zeros_like(t3)
        counts[...] = jnp.zeros_like(counts)
        lists[...] = jnp.zeros_like(lists)
        arrive(tb, face_send.at[0])
        arrive(p2_land, face_recv.at[1])
        pos2[...] = p2_land[...]

    @pl.when(solid)
    def _():
        rest = pltpu.make_async_copy(c, ext.at[pl.ds(1, 6)], local.at[1])
        rest.start()
        strips(lambda r: advance(e.at[0], t_b, c, None, r), 1, 36, 6)
        first = pltpu.make_async_copy(t_b, ext.at[0], local.at[0])
        first.start()
        t_out[...] = jnp.zeros_like(t_out)
        s_out[...] = jnp.zeros_like(s_out)
        pos2[...] = jnp.zeros_like(pos2)
        arrive(p2, face_send.at[1])
        arrive(t2.at[0], face_send.at[2])
        arrive(t2.at[1], face_recv.at[2])
        half = 3 * CROWS

        @pl.when(sec == FLUID_ROWS)
        def _():
            t3[0:half] = t2[0]
            t3[half:2 * half] = t2[1]

        @pl.when(sec == SECS - 1)
        def _():
            t3[0:half] = t2[1]
            t3[half:2 * half] = t2[0]

        t3[2 * half:] = jnp.zeros((8, 128), I32)
        list_pairs(t3, counts, lists, sec - FLUID_ROWS)
        first.wait()
        rest.wait()


def fluid(temp, cond, vx, vy, slot, coef, prior, lateral, dest):
    vm = pl.BlockSpec(memory_space=pltpu.VMEM)
    return pl.pallas_call(
        fluid_kernel,
        out_shape=[
            jax.ShapeDtypeStruct((CY, CX), F32), jax.ShapeDtypeStruct((TILES - 1, CY, 128), F32),
            jax.ShapeDtypeStruct((7, TILES, HY, 128), F32),
            jax.ShapeDtypeStruct((FROWS, 128), I32), jax.ShapeDtypeStruct((SLOTS, 128), I32),
            jax.ShapeDtypeStruct((2 * ALLP + 8, 128), I32),
            jax.ShapeDtypeStruct((8, 128), I32), jax.ShapeDtypeStruct((4 * LROWS, 128), I32),
        ],
        in_specs=[vm] * 9,
        out_specs=[vm, vm, pl.BlockSpec(memory_space=pl.ANY)] + [vm] * 5,
        scratch_shapes=[
            pltpu.VMEM((6, TILES, HY, 128), F32), pltpu.VMEM((TILES, HY, 128), F32), pltpu.VMEM((6, TILES, HY, 128), F32),
            pltpu.VMEM((TILES - 1, HY, 128), F32), pltpu.VMEM((4 * CY, CX), F32),
            pltpu.VMEM((2, HY, 128), F32), pltpu.VMEM((2, HY, 128), F32),
            pltpu.VMEM((2, HY, 128), F32), pltpu.VMEM((2, HY, 128), F32),
            pltpu.VMEM((SLOTS, 128), I32), pltpu.VMEM((3 * SLOTS, 128), I32),
            pltpu.VMEM((3, SLOTS, 128), I32), pltpu.VMEM((SLOTS, 128), I32), pltpu.VMEM((2, 3 * CROWS, 128), I32),
            pltpu.VMEM((256, KR), F32), pltpu.VMEM((256, KR), F32),
            pltpu.VMEM((3 * SLOTS, 128), F32), pltpu.VMEM((3 * CROWS, 128), F32),
            pltpu.SemaphoreType.DMA((16,)), pltpu.SemaphoreType.DMA((16,)),
            pltpu.SemaphoreType.DMA((3,)), pltpu.SemaphoreType.DMA((3,)), pltpu.SemaphoreType.DMA((2,)),
        ],
        compiler_params=params(collective_id=0, has_side_effects=True),
    )(temp, cond, vx, vy, slot, coef, prior, lateral, dest)


def listed(lists, g, n):
    return lists[g * LROWS + (n >> 7), n & 127]


def pair_row(ref, lists, g, i, n):
    rows = []
    for j in range(n):
        p = listed(lists, g, n * i + j)
        rows += [ref[pl.ds(2 * p, 1), :], ref[pl.ds(2 * p + 1, 1), :]]
    return jnp.concatenate(rows, axis=1)


def flux_kernel(total, slot, coef, prior, pos1, pos2, f3, st, fb, land, f2, f3_land, spread, send, recv):
    sec, blk = lax.axis_index("sec"), lax.axis_index("blk")

    @pl.when(sec < FLUID_ROWS)
    def _():
        greet_peers(sec, blk)
        gather_cells(lambda j: total[j], st)
        placed = spread.at[pl.ds(0, 2 * SLOTS)]
        placed[...] = jnp.zeros((2 * SLOTS, 128), F32)

        def one(b, _):
            value = cell_values(st, lane_row(slot, b, 8)) * (1.0 / FLUID_STEPS)
            flux = lane_row(coef, b, 8) * (value - lane_row(prior, b, 8))
            placed[...] += spread_rows(lane_row(pos1, b, 8), split2(flux), SLOTS)
            return 0

        lax.fori_loop(0, FROWS // 8, one, 0)
        fb[...] = spread[0:SLOTS] + spread[SLOTS:2 * SLOTS]
        pl.semaphore_wait(pltpu.get_barrier_semaphore(), COLS + 1)
        exchange(fb, land, send.at[0], recv.at[0], sec, blk)
        part = spread.at[pl.ds(0, 2 * CROWS)]
        spread_all(pos2, lambda b: split2(lane_row(land, b, 16)), 2, CROWS, SLOTS, part)
        f2[...] = part[0:CROWS] + part[CROWS:2 * CROWS]
        place = f3_land.at[pl.ds(pl.multiple_of(sec * CROWS, 8), CROWS)]
        a = push(f2, place, send.at[1], recv.at[1], (FLUID_ROWS, blk))
        b = push(f2, place, send.at[2], recv.at[1], (SECS - 1, blk))
        f3[...] = jnp.zeros_like(f3)
        a.wait_send()
        b.wait_send()

    @pl.when(sec >= FLUID_ROWS)
    def _():
        for r in range(FLUID_ROWS):
            signal((r, blk))
        arrive(f3_land, recv.at[1])
        f3[0:2 * ALLP] = f3_land[...]
        f3[2 * ALLP:] = jnp.zeros((8, 128), F32)


def face_flux(total, slot, coef, prior, pos1, pos2):
    return pl.pallas_call(
        flux_kernel,
        out_shape=jax.ShapeDtypeStruct((2 * ALLP + 8, 128), F32),
        in_specs=[pl.BlockSpec(memory_space=pltpu.VMEM)] * 6,
        scratch_shapes=[
            pltpu.VMEM((CX, 2 * CY), BF16), pltpu.VMEM((SLOTS, 128), F32), pltpu.VMEM((SLOTS, 128), F32),
            pltpu.VMEM((CROWS, 128), F32), pltpu.VMEM((2 * ALLP, 128), F32), pltpu.VMEM((2 * CROWS, 128), F32),
            pltpu.SemaphoreType.DMA((3,)), pltpu.SemaphoreType.DMA((2,)),
        ],
        compiler_params=params(collective_id=1, has_side_effects=True),
    )(total, slot, coef, prior, pos1, pos2)


def source_kernel(counts, lists, t, f, out, acc):
    sec = lax.axis_index("sec")

    @pl.when(sec >= FLUID_ROWS)
    def _():
        base = 128 * (sec - FLUID_ROWS) + 1
        n = HEAT_PAIRS * 256
        for g in range(4):
            acc[...] = jnp.zeros_like(acc)

            def one(i, _):
                v = pair_row(t, lists, g, i, HEAT_PAIRS)
                hi, lo = split2(pair_row(f, lists, g, i, HEAT_PAIRS))
                hit = iota((128, n), 0) == (v >> 10) - base
                a = jnp.concatenate([jnp.where(hit, p, 0.0).astype(BF16) for p in (hi, lo)], axis=0)
                acc[...] += dot_nt(a, onehot(iota((256, n), 0) == (v & 255)))
                return 0

            lax.fori_loop(0, (counts[g, 0] + HEAT_PAIRS - 1) // HEAT_PAIRS, one, 0)
            for h in range(2):
                out[2 * g + h] = DT * (acc[0:128, 128 * h:128 * h + 128] + acc[128:256, 128 * h:128 * h + 128])

    @pl.when(sec < FLUID_ROWS)
    def _():
        out[...] = jnp.zeros_like(out)


def wall_source(counts, lists, t, f):
    return pl.pallas_call(
        source_kernel,
        in_specs=[pl.BlockSpec(memory_space=pltpu.SMEM)] * 2 + [pl.BlockSpec(memory_space=pltpu.VMEM)] * 2,
        out_shape=jax.ShapeDtypeStruct((TILES - 1, 128, 128), F32),
        scratch_shapes=[pltpu.VMEM((256, 256), F32)],
        compiler_params=params(),
    )(counts, lists, t, f)


def wall_kernel(counts, lists, t, state, out, t_out, sem):
    sec = lax.axis_index("sec")
    out[...] = jnp.zeros_like(out)
    whole = pltpu.make_async_copy(state, t_out, sem.at[0])
    whole.start()

    @pl.when(sec >= FLUID_ROWS)
    def _():
        base = 128 * (sec - FLUID_ROWS) + 1
        n = WALL_PAIRS * 256
        for g in range(4):
            table = transposed_parts(state[0:128, 256 * g:256 * (g + 1)])

            def one(i, _):
                v = pair_row(t, lists, g, i, WALL_PAIRS)
                r = onehot(iota((128, n), 0) == (v >> 10) - base)
                x = dot(table, jnp.concatenate([r, r], axis=0))
                x = jnp.where(((v >> 7) & 1) == 1, x[128:256], x[0:128])
                x = jnp.sum(jnp.where(iota((128, n), 0) == (v & 127), x, 0.0), axis=0, keepdims=True)
                for j in range(WALL_PAIRS):
                    p = listed(lists, g, WALL_PAIRS * i + j)
                    out[pl.ds(2 * p, 1), :] = x[:, 256 * j:256 * j + 128]
                    out[pl.ds(2 * p + 1, 1), :] = x[:, 256 * j + 128:256 * j + 256]
                return 0

            lax.fori_loop(0, (counts[g, 0] + WALL_PAIRS - 1) // WALL_PAIRS, one, 0)

    whole.wait()


def wall_values(counts, lists, t, state):
    sm, vm, hbm = (pl.BlockSpec(memory_space=m) for m in (pltpu.SMEM, pltpu.VMEM, pl.ANY))
    return pl.pallas_call(
        wall_kernel,
        in_specs=[sm, sm, vm, vm],
        out_specs=[vm, hbm],
        out_shape=[jax.ShapeDtypeStruct((2 * ALLP + 8, 128), F32), jax.ShapeDtypeStruct((CY, CX), F32)],
        scratch_shapes=[pltpu.SemaphoreType.DMA((1,))],
        compiler_params=params(),
    )(counts, lists, t, state)


def solid_kernel(heat, t_fluid, ext, t_out, e, c, side, below, corner, send, recv, local, finish):
    sec, blk = lax.axis_index("sec"), lax.axis_index("blk")

    @pl.when(sec < FLUID_ROWS)
    def _():
        pass_on = pltpu.make_async_copy(t_fluid, t_out, local.at[0])
        pass_on.start()
        pass_on.wait()

    @pl.when(sec >= FLUID_ROWS)
    def _():
        upper, lower = FLUID_ROWS, SECS - 1
        left, right = lax.rem(blk + COLS - 1, COLS), lax.rem(blk + 1, COLS)
        first = pltpu.make_async_copy(ext.at[0], e.at[0], local.at[0])
        rest = pltpu.make_async_copy(ext.at[pl.ds(1, 6)], c, local.at[1])
        first.start()
        rest.start()
        signal((sec, left))
        signal((sec, right))

        @pl.when(sec == upper)
        def _():
            for q in (left, blk, right):
                signal((lower, q))

        pl.semaphore_wait(pltpu.get_barrier_semaphore(), jnp.where(sec == upper, 2, 5))
        end = TILES - 2
        copies = [push(heat.at[0], side.at[0], send.at[0], recv.at[0], (sec, left)),
                  push(heat.at[end], side.at[1], send.at[1], recv.at[1], (sec, right))]
        top = pl.ds(0, HALO)
        down = [
            pltpu.make_async_remote_copy(heat.at[pl.ds(0, TILES - 1), top], below, send.at[2], recv.at[2],
                                         device_id=(upper, blk), device_id_type=MESH),
            pltpu.make_async_remote_copy(heat.at[0, top], corner.at[0], send.at[3], recv.at[3],
                                         device_id=(upper, left), device_id_type=MESH),
            pltpu.make_async_remote_copy(heat.at[end, top], corner.at[1], send.at[4], recv.at[4],
                                         device_id=(upper, right), device_id_type=MESH)]

        @pl.when(sec == lower)
        def _():
            for d in down:
                d.start()

        first.wait()
        rest.wait()

        def warm(j, rows, x):
            e[0, j, rows, :] += x
            c[5, j, rows, :] += x

        for j in range(TILES - 1):
            warm(j, slice(OY, OY + 128), heat[j])
        for d in copies:
            d.wait()
        warm(TILES - 1, slice(OY, OY + 128), jnp.where(iota((128, 128), 1) < 64, side[0], side[1]))

        @pl.when(sec == lower)
        def _():
            for d in down:
                d.wait_send()

        @pl.when(sec == upper)
        def _():
            for d in down:
                d.wait_recv()
            last = slice(OY + CY, OY + CY + HALO)
            for j in range(TILES - 1):
                warm(j, last, below[j])
            warm(TILES - 1, last, jnp.where(iota((HALO, 128), 1) < 64, corner[0], corner[1]))

        for n in range(SOLID_STEPS - 1):
            strips(lambda r: advance(e.at[n % 2], e.at[1 - n % 2], c, None, r), 1, 36, 12)
        done = [pltpu.make_async_copy(e.at[(SOLID_STEPS - 1) % 2, j, pl.ds(OY, CY)], t_out.at[:, pl.ds(128 * j, 128)], finish.at[j])
                for j in range(TILES - 1)]
        for d in done:
            d.start()
        for d in done:
            d.wait()


def solid_steps(heat, t_fluid, ext):
    vm, hbm = pl.BlockSpec(memory_space=pltpu.VMEM), pl.BlockSpec(memory_space=pl.ANY)
    return pl.pallas_call(
        solid_kernel,
        out_shape=jax.ShapeDtypeStruct((CY, CX), F32),
        in_specs=[vm, vm, hbm],
        out_specs=hbm,
        scratch_shapes=[
            pltpu.VMEM((2, TILES, HY, 128), F32), pltpu.VMEM((6, TILES, HY, 128), F32),
            pltpu.VMEM((2, 128, 128), F32), pltpu.VMEM((TILES - 1, HALO, 128), F32), pltpu.VMEM((2, HALO, 128), F32),
            pltpu.SemaphoreType.DMA((5,)), pltpu.SemaphoreType.DMA((5,)), pltpu.SemaphoreType.DMA((2,)), pltpu.SemaphoreType.DMA((TILES - 1,)),
        ],
        compiler_params=params(collective_id=2, has_side_effects=True),
    )(heat, t_fluid, ext)


def back_kernel(values, pos1, pos2, state, slot, out, reply, fb, land, st, send, recv):
    sec, blk = lax.axis_index("sec"), lax.axis_index("blk")

    @pl.when(sec < FLUID_ROWS)
    def _():
        greet_peers(sec, blk)
        signal((FLUID_ROWS, blk))
        signal((SECS - 1, blk))
        pl.semaphore_wait(pltpu.get_barrier_semaphore(), COLS - 1)
        arrive(reply, recv.at[0])
        pick_all(transposed_parts(reply[0] + reply[1]), pos2, CROWS, SLOTS, fb)
        exchange(fb, land, send.at[1], recv.at[1], sec, blk)
        pick_all(transposed_parts(land[...]), pos1, SLOTS, FROWS, out)

    @pl.when(sec >= FLUID_ROWS)
    def _():
        pl.semaphore_wait(pltpu.get_barrier_semaphore(), FLUID_ROWS)
        for r in range(FLUID_ROWS):
            push(values.at[pl.ds(r * CROWS, CROWS)], reply.at[sec - FLUID_ROWS], send.at[0], recv.at[0], (r, blk))
        gather_cells(lambda j: state[:, 128 * j:128 * j + 128], st)

        def one(b, _):
            put_lane_row(out, b, 8, cell_values(st, lane_row(slot, b, 8)))
            return 0

        lax.fori_loop(0, FROWS // 8, one, 0)
        arrive(values.at[pl.ds(0, 2 * ALLP)], send.at[0])


def back(values, pos1, pos2, state, slot):
    return pl.pallas_call(
        back_kernel,
        out_shape=jax.ShapeDtypeStruct((FROWS, 128), F32),
        in_specs=[pl.BlockSpec(memory_space=pltpu.VMEM)] * 5,
        scratch_shapes=[
            pltpu.VMEM((2, CROWS, 128), F32), pltpu.VMEM((SLOTS, 128), F32), pltpu.VMEM((SLOTS, 128), F32),
            pltpu.VMEM((CX, 2 * CY), BF16), pltpu.SemaphoreType.DMA((2,)), pltpu.SemaphoreType.DMA((2,)),
        ],
        compiler_params=params(collective_id=3, has_side_effects=True),
    )(values, pos1, pos2, state, slot)


def body(temp, cond, vx, vy, slot, lateral, dest, coef, prior):
    slot, lateral, dest, coef, prior = (v.reshape(FROWS, 128) for v in (slot, lateral, dest, coef, prior))
    t_fluid, total, ext, pos1, pos2, t3, counts, lists = fluid(temp, cond, vx, vy, slot, coef, prior, lateral, dest)
    f3 = face_flux(total, slot, coef, prior, pos1, pos2)
    source = wall_source(counts, lists, t3, f3)
    t_new = solid_steps(source, t_fluid, ext)
    values, t_new = wall_values(counts, lists, t3, t_new)
    wall = back(values, pos1, pos2, t_new, slot)
    return t_new, wall.reshape(FACES)


def solution(mesh):
    block, face = P("sec", "blk"), P(("sec", "blk"))
    in_specs = (block, block, block, block, face, P(("sec", "blk"), None), face, face, face)
    return jax.shard_map(body, mesh=mesh, in_specs=in_specs, out_specs=(block, face), check_vma=False)
```

```python
import functools

import jax
import jax.numpy as jnp
from jax import lax
from jax.experimental import pallas as pl
from jax.experimental.pallas import tpu as pltpu
from jax.sharding import PartitionSpec as P

F32, BF16, I32 = jnp.float32, jnp.bfloat16, jnp.int32
MESH = pl.DeviceIdType.MESH
NT = (((1,), (1,)), ((), ()))

CY, CX = 256, 1024
FACES = 8192
FLUID_ROWS, SECS, COLS = 6, 8, 16
FLUID_STEPS, SOLID_STEPS = 10, 4
DT = 0.2
FROWS = FACES // 128
KR = 512
HALO = 16
BROWS = 6
SLOTS = COLS * BROWS
PAIRS = 56
CROWS = 2 * PAIRS
ALLP = FLUID_ROWS * PAIRS
HEAT_PAIRS, WALL_PAIRS = 10, 8
LROWS = 4
HY, OY, TILES = 304, 24, 9
VLIM = 60 << 20


def params(**kw):
    return pltpu.CompilerParams(vmem_limit_bytes=VLIM, **kw)


def iota(shape, dim):
    return lax.broadcasted_iota(I32, shape, dim)


def split2(x):
    hi = x.astype(BF16).astype(F32)
    return hi, (x - hi).astype(BF16).astype(F32)


def onehot(mask):
    return jnp.where(mask, 1.0, 0.0).astype(BF16)


def dot(a, b):
    return jnp.dot(a, b, preferred_element_type=F32)


def dot_nt(a, b):
    return lax.dot_general(a, b, NT, preferred_element_type=F32)


def lane_row(ref, b, n):
    return jnp.concatenate([ref[pl.ds(n * b + i, 1), :] for i in range(n)], axis=1)


def put_lane_row(ref, b, n, v):
    for i in range(n):
        ref[pl.ds(n * b + i, 1), :] = v[:, i * 128:(i + 1) * 128]


def ranks(group, nb, ng, o_ref, p_ref):
    for b in range(nb):
        o_ref[b * ng:(b + 1) * ng, :] = jnp.where(iota((ng, KR), 0) == group(b), 1.0, 0.0)
    o = o_ref[...].astype(BF16)
    p_ref[...] = dot(o, onehot(iota((KR, KR), 0) < iota((KR, KR), 1)))
    return dot(o, onehot(iota((KR, 128), 0) >= 0))


def ranked(b, ng, carry, o_ref, p_ref):
    rows = slice(b * ng, (b + 1) * ng)
    place = p_ref[rows] + jnp.concatenate([carry] * (KR // 128), axis=1)
    return jnp.sum(o_ref[rows] * place, axis=0, keepdims=True).astype(I32)


def spread_rows(pos, pieces, rows):
    k = pos.shape[1]
    hit = iota((rows, k), 0) == (pos >> 7)
    a = jnp.concatenate([jnp.where(hit, v, 0.0).astype(BF16) for v in pieces], axis=0)
    return dot_nt(a, onehot(iota((128, k), 0) == (pos & 127)))


def spread_all(pos, parts_of, n_parts, rows, total_rows, out):
    out[...] = jnp.zeros_like(out)

    def one(b, _):
        out[...] += spread_rows(lane_row(pos, b, 16), parts_of(b), rows)
        return 0

    lax.fori_loop(0, total_rows // 16, one, 0)


def pick(vt, pos, rows):
    k = pos.shape[1]
    r = onehot(iota((rows, k), 0) == (pos >> 7))
    g = dot(vt, jnp.concatenate([r, r], axis=0))
    return jnp.sum(jnp.where(iota((128, k), 0) == (pos & 127), g, 0.0), axis=0, keepdims=True)


def pick_all(vt, pos, rows, total_rows, out):
    def one(b, _):
        put_lane_row(out, b, 16, pick(vt, lane_row(pos, b, 16), rows))
        return 0

    lax.fori_loop(0, total_rows // 16, one, 0)


def transposed_parts(v):
    hi, lo = split2(v.T)
    return jnp.concatenate([hi, lo], axis=1).astype(BF16)


def target_parts(t):
    return (t >> 10).astype(F32), ((t >> 5) & 31).astype(F32), (t & 31).astype(F32)


def target_join(x, rows):
    return (x[0:rows] * 1024.0 + x[rows:2 * rows] * 32.0 + x[2 * rows:3 * rows]).astype(I32)


def gather_cells(tile_of, st):
    for j in range(CX // 128):
        hi, lo = split2(tile_of(j).T)
        st[128 * j:128 * j + 128, 0:CY] = hi.astype(BF16)
        st[128 * j:128 * j + 128, CY:2 * CY] = lo.astype(BF16)


def cell_values(st, s):
    k = s.shape[1]
    r = onehot(iota((CY, k), 0) == (s >> 10))
    g = dot(st[...], jnp.concatenate([r, r], axis=0))
    tile = (s & 1023) >> 7
    a = g[0:128]
    for i in range(1, CX // 128):
        a = jnp.where(tile == i, g[128 * i:128 * i + 128], a)
    return jnp.sum(jnp.where(iota((128, k), 0) == (s & 127), a, 0.0), axis=0, keepdims=True)


def signal(to):
    pl.semaphore_signal(pltpu.get_barrier_semaphore(), inc=1, device_id=to, device_id_type=MESH)


def arrive(ref, sem):
    pltpu.make_async_copy(ref, ref, sem).wait()


def push(src, dst, send, recv, to):
    copy = pltpu.make_async_remote_copy(src, dst, send, recv, device_id=to, device_id_type=MESH)
    copy.start()
    return copy


def exchange(src, land, send, recv, sec, blk):
    def one(q, _):
        @pl.when(q != blk)
        def _():
            push(src.at[pl.ds(q * BROWS, BROWS)], land.at[pl.ds(blk * BROWS, BROWS)],
                 send, recv, (sec, q))
        return 0

    lax.fori_loop(0, COLS, one, 0)
    own = pl.ds(blk * BROWS, BROWS)
    land[own, :] = src[own, :]
    arrive(src.at[pl.ds(0, SLOTS - BROWS)], send)
    arrive(land.at[pl.ds(0, SLOTS - BROWS)], recv)


def greet_peers(sec, blk):
    def one(q, _):
        @pl.when(q != blk)
        def _():
            signal((sec, q))
        return 0

    lax.fori_loop(0, COLS, one, 0)


def lane_roll(x, n):
    return pltpu.roll(x, n % 128, 1)


def beside(x):
    lane = iota((8, 128), 1)
    east, west = [lane_roll(v, 127) for v in x], [lane_roll(v, 1) for v in x]
    e = [jnp.where(lane == 127, east[(j + 1) % TILES], east[j]) for j in range(TILES)]
    w = [jnp.where(lane == 0, west[j - 1], west[j]) for j in range(TILES)]
    return e, w


def advance(src, dst, c, total, r):
    rows = pl.ds(r, 8)
    x = [src[j, rows, :] for j in range(TILES)]
    e, w = beside(x)
    for j in range(TILES):
        n, s = src[j, pl.ds(r + 1, 8), :], src[j, pl.ds(r - 1, 8), :]
        if total is not None and j < TILES - 1:
            total[j, rows, :] += x[j]
        dst[j, rows, :] = (
            (c[4, j, rows, :] * x[j] + c[0, j, rows, :] * n)
            + (c[1, j, rows, :] * s + c[2, j, rows, :] * e[j])
            + (c[3, j, rows, :] * w[j] + c[5, j, rows, :])
        )


def strips(fn, first, count, unroll):
    def body(i, _):
        for u in range(unroll):
            fn(pl.multiple_of(8 * first + 8 * unroll * i + 8 * u, 8))
        return 0

    lax.fori_loop(0, count // unroll, body, 0)


def substeps(a, b, c, total, count):
    def sweep(src, dst):
        strips(lambda r: advance(src, dst, c, total, r), 2, 34, 17)

    def two(i, _):
        sweep(a, b)
        sweep(b, a)
        return 0

    strips(lambda r: advance(a, b, c, total, r), 1, 36, 12)
    sweep(b, a)
    lax.fori_loop(1, count // 2, two, 0)


def coefficients(e, c, low, high, r):
    rows = pl.ds(r, 8)
    x = [e[1, j, rows, :] for j in range(TILES)]
    east, west = beside(x)
    at = r + iota((8, 128), 0)
    first, last = low & (at == OY), high & (at == OY + CY - 1)
    h = 0.5 * DT
    for j in range(TILES):
        hn, hs = h * (x[j] + e[1, j, pl.ds(r + 1, 8), :]), h * (x[j] + e[1, j, pl.ds(r - 1, 8), :])
        he, hw = h * (x[j] + east[j]), h * (x[j] + west[j])
        vx, vy = h * e[2, j, rows, :], h * e[3, j, rows, :]
        an, as_ = hn - vy, hs + vy
        c0 = 1.0 - ((hn + hs) + (he + hw))
        c[0, j, rows, :] = jnp.where(last, 0.0, an)
        c[1, j, rows, :] = jnp.where(first, 0.0, as_)
        c[2, j, rows, :] = he - vx
        c[3, j, rows, :] = hw + vx
        c[4, j, rows, :] = c0 + jnp.where(first, as_, 0.0) + jnp.where(last, an, 0.0)


def face_terms(e, c, r):
    rows = pl.ds(r, 8)
    for j in range(TILES):
        c[4, j, rows, :] -= DT * e[4, j, rows, :]
        c[5, j, rows, :] = DT * e[5, j, rows, :]


def compact(t, pos, t2, o_ref, p_ref, out):
    nb, ng = SLOTS // 4, 8

    def group(b):
        v = lane_row(t, b, 4)
        return jnp.where(v >= 1024, ((v - 1024) >> 17) * 4 + ((v >> 8) & 3), -1)

    totals = ranks(group, nb, ng, o_ref, p_ref)
    count = jnp.zeros((ng, 128), F32)
    for b in range(nb):
        count = count + totals[b * ng:(b + 1) * ng]
    units = ((count.astype(I32) + 255) >> 8).astype(F32).astype(BF16)
    carry = dot(onehot(iota((ng, ng), 1) < iota((ng, ng), 0)), units) * 256.0
    for b in range(nb):
        put_lane_row(pos, b, 4, jnp.where(lane_row(t, b, 4) >= 1024, ranked(b, ng, carry, o_ref, p_ref), -1))
        carry = carry + totals[b * ng:(b + 1) * ng]
    spread_all(pos, lambda b: target_parts(lane_row(t, b, 16)), 3, CROWS, SLOTS, out)
    t2[...] = target_join(out[...], CROWS)


def list_pairs(t, counts, lists, mine):
    n = 768
    v = jnp.concatenate([t[...].T[0:8], jnp.zeros((8, n - 2 * ALLP - 8), I32)], axis=1)[0:1]
    row = iota((1, n), 1)
    ours = (v >= 1024) & (((v - 1024) >> 17) == mine) & ((row & 1) == 0)
    group = jnp.where(ours, (v >> 8) & 3, -1)
    member = jnp.where(iota((8, n), 0) == group, 1.0, 0.0)
    before = dot(member.astype(BF16), onehot(iota((n, n), 0) < iota((n, n), 1)))
    rank = jnp.sum(member * before, axis=0, keepdims=True).astype(I32)
    pos = jnp.where(ours, group * (LROWS * 128) + rank, -1)
    back = (row >> 1) - ALLP
    x = spread_rows(pos, ((back >> 1).astype(F32), (back & 1).astype(F32)), 4 * LROWS)
    lists[...] = (2.0 * x[0:4 * LROWS] + x[4 * LROWS:]).astype(I32) + ALLP
    counts[...] = dot(member.astype(BF16), onehot(iota((n, 128), 0) >= 0)).astype(I32)


def fluid_kernel(temp, cond, vx, vy, slot, coef, prior, lateral, dest,
                 t_out, s_out, ext, pos1, pos2, t3, counts, lists,
                 e, t_b, c, total, acc, pack, land, packm, landm, tb, tb_land, p2, p2_land, t2, o_ref, p_ref, tb_out, t2_out,
                 send, recv, face_send, face_recv, local):
    sec, blk = lax.axis_index("sec"), lax.axis_index("blk")
    fluid = sec < FLUID_ROWS
    solid = jnp.logical_not(fluid)
    low = (sec == 0) | (sec == FLUID_ROWS)
    high = (sec == FLUID_ROWS - 1) | (sec == SECS - 1)
    has_low, has_high = jnp.logical_not(low), jnp.logical_not(high)
    left, right = lax.rem(blk + COLS - 1, COLS), lax.rem(blk + 1, COLS)
    server = FLUID_ROWS + sec // 3
    mine = 3 * (sec - FLUID_ROWS)
    other = 2 * FLUID_ROWS + 1 - sec

    signal((sec, left))
    signal((sec, right))

    @pl.when(has_low)
    def _():
        for q in (left, blk, right):
            signal((sec - 1, q))

    @pl.when(has_high)
    def _():
        for q in (left, blk, right):
            signal((sec + 1, q))

    @pl.when(fluid)
    def _():
        signal((server, blk))

    @pl.when(solid)
    def _():
        def one(i, _):
            signal((mine + i // COLS, lax.rem(i, COLS)))
            return 0

        lax.fori_loop(0, 3 * COLS, one, 0)

    mid = slice(OY, OY + CY)
    keep = jnp.where(fluid, 1.0, 0.0)
    for j in range(TILES - 1):
        tile = slice(128 * j, 128 * j + 128)
        e[0, j, mid, :] = temp[:, tile]
        e[1, j, mid, :] = cond[:, tile]
        e[2, j, mid, :] = vx[:, tile] * keep
        e[3, j, mid, :] = vy[:, tile] * keep

    @pl.when(low)
    def _():
        for a in range(6):
            for j in range(TILES - 1):
                e[a, j, OY - HALO:OY, :] = jnp.zeros((HALO, 128), F32)
        for ref in (land, landm):
            ref[:, OY - HALO:OY, :] = jnp.zeros((2, HALO, 128), F32)

    @pl.when(high)
    def _():
        for a in range(6):
            for j in range(TILES - 1):
                e[a, j, OY + CY:OY + CY + HALO, :] = jnp.zeros((HALO, 128), F32)
        for ref in (land, landm):
            ref[:, OY + CY:OY + CY + HALO, :] = jnp.zeros((2, HALO, 128), F32)

    pl.semaphore_wait(
        pltpu.get_barrier_semaphore(),
        8 - 3 * (low.astype(I32) + high.astype(I32)) + jnp.where(fluid, COLS, 3))

    first_rows, last_rows = pl.ds(OY, HALO), pl.ds(OY + CY - HALO, HALO)
    below, above = pl.ds(OY + CY, HALO), pl.ds(OY - HALO, HALO)

    def halo_copies(first, arrays, i, pack, land):
        count = [0]

        def copy(src, dst, to):
            at = i + count[0]
            count[0] += 1
            return pltpu.make_async_remote_copy(src, dst, send.at[at], recv.at[at], device_id=to, device_id_type=MESH)

        body = e.at[pl.ds(first, arrays), pl.ds(0, TILES - 1)]
        up = [copy(body.at[:, :, first_rows], body.at[:, :, below], (sec - 1, blk))]
        down = [copy(body.at[:, :, last_rows], body.at[:, :, above], (sec + 1, blk))]
        here = []
        for side, to in ((0, left), (1, right)):
            own, there = pack.at[side], land.at[side]
            here.append(copy(own.at[pl.ds(OY, CY)], there.at[pl.ds(OY, CY)], (sec, to)))
            up.append(copy(own.at[first_rows], there.at[below], (sec - 1, to)))
            down.append(copy(own.at[last_rows], there.at[above], (sec + 1, to)))
        return here, up, down

    def halo_start(copies, first, arrays, pack):
        here, up, down = copies
        lane = iota((8, 128), 1)

        def strip(r):
            rows = pl.ds(r, 8)
            lo = e[first, 0, rows, :]
            hi = lane_roll(e[first, TILES - 2, rows, :], HALO)
            for a in range(1, arrays):
                mine = (lane >> 4) == a
                lo = jnp.where(mine, lane_roll(e[first + a, 0, rows, :], HALO * a), lo)
                hi = jnp.where(mine, lane_roll(e[first + a, TILES - 2, rows, :], HALO * a + HALO), hi)
            pack[0, rows, :] = lo
            pack[1, rows, :] = hi

        pl.when(has_low)(up[0].start)
        pl.when(has_high)(down[0].start)
        strips(strip, 3, 32, 8)
        for d in here:
            d.start()

        @pl.when(has_low)
        def _():
            for d in up[1:]:
                d.start()

        @pl.when(has_high)
        def _():
            for d in down[1:]:
                d.start()

    def halo_wait(copies, first, arrays, land):
        here, up, down = copies
        for d in here:
            d.wait()

        @pl.when(has_low)
        def _():
            for d in up:
                d.wait_send()
            for d in down:
                d.wait_recv()

        @pl.when(has_high)
        def _():
            for d in down:
                d.wait_send()
            for d in up:
                d.wait_recv()

        lane = iota((8, 128), 1)

        def strip(r):
            rows = pl.ds(r, 8)
            lo, hi = land[0, rows, :], land[1, rows, :]
            for a in range(arrays):
                e[first + a, TILES - 1, rows, :] = jnp.where(
                    lane < 64, lane_roll(lo, -HALO * a), lane_roll(hi, 128 - HALO - HALO * a))

        strips(strip, 1, 36, 6)

    def maps(b, _):
        s, k = lane_row(slot, b, 16), lane_row(coef, b, 16)
        parts = split2(k) + split2(k * lane_row(prior, b, 16))
        hit = iota((CY, 2048), 0) == (s >> 10)
        a = jnp.concatenate([jnp.where(hit, v, 0.0).astype(BF16) for v in parts], axis=0)
        acc[...] += dot_nt(a, onehot(iota((CX, 2048), 0) == (s & 1023)))
        return 0

    static, of_maps = halo_copies(0, 4, 0, pack, land), halo_copies(4, 2, 8, packm, landm)

    def place_maps():
        for j in range(TILES - 1):
            tile = slice(128 * j, 128 * j + 128)
            e[4, j, mid, :] = acc[0:CY, tile] + acc[CY:2 * CY, tile]
            e[5, j, mid, :] = acc[2 * CY:3 * CY, tile] + acc[3 * CY:4 * CY, tile]

    halo_start(static, 0, 4, pack)
    acc[...] = jnp.zeros_like(acc)

    @pl.when(fluid)
    def _():
        totals = ranks(lambda b: lane_row(lateral, b, 4), FROWS // 4, COLS, o_ref, p_ref)
        carry = jnp.zeros((COLS, 128), F32)
        for b in range(FROWS // 4):
            put_lane_row(pos1, b, 4, lane_row(lateral, b, 4) * (BROWS * 128) + ranked(b, COLS, carry, o_ref, p_ref))
            carry = carry + totals[b * COLS:(b + 1) * COLS]
        spread_all(pos1, lambda b: target_parts(lane_row(dest, b, 16) + 1024), 3, SLOTS, FROWS, tb_out)
        tb[...] = target_join(tb_out[...], SLOTS)

        def one(q, _):
            push(tb.at[pl.ds(q * BROWS, BROWS)],
                 tb_land.at[pl.ds(lax.rem(sec, 3) * SLOTS + blk * BROWS, BROWS)],
                 face_send.at[0], face_recv.at[0], (server, q))
            return 0

        lax.fori_loop(0, COLS, one, 0)

    @pl.when(solid)
    def _():
        pos1[...] = jnp.zeros_like(pos1)

    lax.fori_loop(0, 2, maps, 0)

    @pl.when(fluid)
    def _():
        lax.fori_loop(2, 4, maps, 0)
        place_maps()

    @pl.when(solid)
    def _():
        arrive(tb_land, face_recv.at[0])
        for i in range(3):
            t = tb_land.at[pl.ds(i * SLOTS, SLOTS)]
            compact(t, p2.at[i], t2.at[0, pl.ds(i * CROWS, CROWS)], o_ref, p_ref, t2_out)
            push(p2.at[i], p2_land, face_send.at[1], face_recv.at[1], (mine + i, blk))
        push(t2.at[0], t2.at[1], face_send.at[2], face_recv.at[2], (other, blk))
        lax.fori_loop(2, 4, maps, 0)
        place_maps()

    halo_start(of_maps, 4, 2, packm)
    halo_wait(static, 0, 4, land)
    strips(lambda r: coefficients(e, c, low, high, r), 1, 36, 4)
    halo_wait(of_maps, 4, 2, landm)
    strips(lambda r: face_terms(e, c, r), 1, 36, 4)

    @pl.when(fluid)
    def _():
        total[...] = jnp.zeros_like(total)
        substeps(e.at[0], t_b, c, total, FLUID_STEPS)
        for j in range(TILES - 1):
            t_out[:, 128 * j:128 * j + 128] = e[0, j, mid, :]
            s_out[j] = total[j, mid, :]
        t3[...] = jnp.zeros_like(t3)
        counts[...] = jnp.zeros_like(counts)
        lists[...] = jnp.zeros_like(lists)
        arrive(tb, face_send.at[0])
        arrive(p2_land, face_recv.at[1])
        pos2[...] = p2_land[...]

    @pl.when(solid)
    def _():
        rest = pltpu.make_async_copy(c, ext.at[pl.ds(1, 6)], local.at[1])
        rest.start()
        strips(lambda r: advance(e.at[0], t_b, c, None, r), 1, 36, 6)
        first = pltpu.make_async_copy(t_b, ext.at[0], local.at[0])
        first.start()
        t_out[...] = jnp.zeros_like(t_out)
        s_out[...] = jnp.zeros_like(s_out)
        pos2[...] = jnp.zeros_like(pos2)
        arrive(p2, face_send.at[1])
        arrive(t2.at[0], face_send.at[2])
        arrive(t2.at[1], face_recv.at[2])
        half = 3 * CROWS

        @pl.when(sec == FLUID_ROWS)
        def _():
            t3[0:half] = t2[0]
            t3[half:2 * half] = t2[1]

        @pl.when(sec == SECS - 1)
        def _():
            t3[0:half] = t2[1]
            t3[half:2 * half] = t2[0]

        t3[2 * half:] = jnp.zeros((8, 128), I32)
        list_pairs(t3, counts, lists, sec - FLUID_ROWS)
        first.wait()
        rest.wait()


def fluid(temp, cond, vx, vy, slot, coef, prior, lateral, dest):
    vm = pl.BlockSpec(memory_space=pltpu.VMEM)
    return pl.pallas_call(
        fluid_kernel,
        out_shape=[
            jax.ShapeDtypeStruct((CY, CX), F32), jax.ShapeDtypeStruct((TILES - 1, CY, 128), F32),
            jax.ShapeDtypeStruct((7, TILES, HY, 128), F32),
            jax.ShapeDtypeStruct((FROWS, 128), I32), jax.ShapeDtypeStruct((SLOTS, 128), I32),
            jax.ShapeDtypeStruct((2 * ALLP + 8, 128), I32),
            jax.ShapeDtypeStruct((8, 128), I32), jax.ShapeDtypeStruct((4 * LROWS, 128), I32),
        ],
        in_specs=[vm] * 9,
        out_specs=[vm, vm, pl.BlockSpec(memory_space=pl.ANY)] + [vm] * 5,
        scratch_shapes=[
            pltpu.VMEM((6, TILES, HY, 128), F32), pltpu.VMEM((TILES, HY, 128), F32), pltpu.VMEM((6, TILES, HY, 128), F32),
            pltpu.VMEM((TILES - 1, HY, 128), F32), pltpu.VMEM((4 * CY, CX), F32),
            pltpu.VMEM((2, HY, 128), F32), pltpu.VMEM((2, HY, 128), F32),
            pltpu.VMEM((2, HY, 128), F32), pltpu.VMEM((2, HY, 128), F32),
            pltpu.VMEM((SLOTS, 128), I32), pltpu.VMEM((3 * SLOTS, 128), I32),
            pltpu.VMEM((3, SLOTS, 128), I32), pltpu.VMEM((SLOTS, 128), I32), pltpu.VMEM((2, 3 * CROWS, 128), I32),
            pltpu.VMEM((256, KR), F32), pltpu.VMEM((256, KR), F32),
            pltpu.VMEM((3 * SLOTS, 128), F32), pltpu.VMEM((3 * CROWS, 128), F32),
            pltpu.SemaphoreType.DMA((16,)), pltpu.SemaphoreType.DMA((16,)),
            pltpu.SemaphoreType.DMA((3,)), pltpu.SemaphoreType.DMA((3,)), pltpu.SemaphoreType.DMA((2,)),
        ],
        compiler_params=params(collective_id=0, has_side_effects=True),
    )(temp, cond, vx, vy, slot, coef, prior, lateral, dest)


def listed(lists, g, n):
    return lists[g * LROWS + (n >> 7), n & 127]


def pair_row(ref, lists, g, i, n):
    rows = []
    for j in range(n):
        p = listed(lists, g, n * i + j)
        rows += [ref[pl.ds(2 * p, 1), :], ref[pl.ds(2 * p + 1, 1), :]]
    return jnp.concatenate(rows, axis=1)


def flux_kernel(total, slot, coef, prior, pos1, pos2, f3, st, fb, land, f2, f3_land, spread, send, recv):
    sec, blk = lax.axis_index("sec"), lax.axis_index("blk")

    @pl.when(sec < FLUID_ROWS)
    def _():
        greet_peers(sec, blk)
        gather_cells(lambda j: total[j], st)
        placed = spread.at[pl.ds(0, 2 * SLOTS)]
        placed[...] = jnp.zeros((2 * SLOTS, 128), F32)

        def one(b, _):
            value = cell_values(st, lane_row(slot, b, 8)) * (1.0 / FLUID_STEPS)
            flux = lane_row(coef, b, 8) * (value - lane_row(prior, b, 8))
            placed[...] += spread_rows(lane_row(pos1, b, 8), split2(flux), SLOTS)
            return 0

        lax.fori_loop(0, FROWS // 8, one, 0)
        fb[...] = spread[0:SLOTS] + spread[SLOTS:2 * SLOTS]
        pl.semaphore_wait(pltpu.get_barrier_semaphore(), COLS + 1)
        exchange(fb, land, send.at[0], recv.at[0], sec, blk)
        part = spread.at[pl.ds(0, 2 * CROWS)]
        spread_all(pos2, lambda b: split2(lane_row(land, b, 16)), 2, CROWS, SLOTS, part)
        f2[...] = part[0:CROWS] + part[CROWS:2 * CROWS]
        place = f3_land.at[pl.ds(pl.multiple_of(sec * CROWS, 8), CROWS)]
        a = push(f2, place, send.at[1], recv.at[1], (FLUID_ROWS, blk))
        b = push(f2, place, send.at[2], recv.at[1], (SECS - 1, blk))
        f3[...] = jnp.zeros_like(f3)
        a.wait_send()
        b.wait_send()

    @pl.when(sec >= FLUID_ROWS)
    def _():
        for r in range(FLUID_ROWS):
            signal((r, blk))
        arrive(f3_land, recv.at[1])
        f3[0:2 * ALLP] = f3_land[...]
        f3[2 * ALLP:] = jnp.zeros((8, 128), F32)


def face_flux(total, slot, coef, prior, pos1, pos2):
    return pl.pallas_call(
        flux_kernel,
        out_shape=jax.ShapeDtypeStruct((2 * ALLP + 8, 128), F32),
        in_specs=[pl.BlockSpec(memory_space=pltpu.VMEM)] * 6,
        scratch_shapes=[
            pltpu.VMEM((CX, 2 * CY), BF16), pltpu.VMEM((SLOTS, 128), F32), pltpu.VMEM((SLOTS, 128), F32),
            pltpu.VMEM((CROWS, 128), F32), pltpu.VMEM((2 * ALLP, 128), F32), pltpu.VMEM((2 * CROWS, 128), F32),
            pltpu.SemaphoreType.DMA((3,)), pltpu.SemaphoreType.DMA((2,)),
        ],
        compiler_params=params(collective_id=1, has_side_effects=True),
    )(total, slot, coef, prior, pos1, pos2)


def source_kernel(counts, lists, t, f, out, acc):
    sec = lax.axis_index("sec")

    @pl.when(sec >= FLUID_ROWS)
    def _():
        base = 128 * (sec - FLUID_ROWS) + 1
        n = HEAT_PAIRS * 256
        for g in range(4):
            acc[...] = jnp.zeros_like(acc)

            def one(i, _):
                v = pair_row(t, lists, g, i, HEAT_PAIRS)
                hi, lo = split2(pair_row(f, lists, g, i, HEAT_PAIRS))
                hit = iota((128, n), 0) == (v >> 10) - base
                a = jnp.concatenate([jnp.where(hit, p, 0.0).astype(BF16) for p in (hi, lo)], axis=0)
                acc[...] += dot_nt(a, onehot(iota((256, n), 0) == (v & 255)))
                return 0

            lax.fori_loop(0, (counts[g, 0] + HEAT_PAIRS - 1) // HEAT_PAIRS, one, 0)
            for h in range(2):
                out[2 * g + h] = DT * (acc[0:128, 128 * h:128 * h + 128] + acc[128:256, 128 * h:128 * h + 128])

    @pl.when(sec < FLUID_ROWS)
    def _():
        out[...] = jnp.zeros_like(out)


def wall_source(counts, lists, t, f):
    return pl.pallas_call(
        source_kernel,
        in_specs=[pl.BlockSpec(memory_space=pltpu.SMEM)] * 2 + [pl.BlockSpec(memory_space=pltpu.VMEM)] * 2,
        out_shape=jax.ShapeDtypeStruct((TILES - 1, 128, 128), F32),
        scratch_shapes=[pltpu.VMEM((256, 256), F32)],
        compiler_params=params(),
    )(counts, lists, t, f)


def wall_kernel(counts, lists, t, state, out, t_out, sem):
    sec = lax.axis_index("sec")
    out[...] = jnp.zeros_like(out)
    whole = pltpu.make_async_copy(state, t_out, sem.at[0])
    whole.start()

    @pl.when(sec >= FLUID_ROWS)
    def _():
        base = 128 * (sec - FLUID_ROWS) + 1
        n = WALL_PAIRS * 256
        for g in range(4):
            table = transposed_parts(state[0:128, 256 * g:256 * (g + 1)])

            def one(i, _):
                v = pair_row(t, lists, g, i, WALL_PAIRS)
                r = onehot(iota((128, n), 0) == (v >> 10) - base)
                x = dot(table, jnp.concatenate([r, r], axis=0))
                x = jnp.where(((v >> 7) & 1) == 1, x[128:256], x[0:128])
                x = jnp.sum(jnp.where(iota((128, n), 0) == (v & 127), x, 0.0), axis=0, keepdims=True)
                for j in range(WALL_PAIRS):
                    p = listed(lists, g, WALL_PAIRS * i + j)
                    out[pl.ds(2 * p, 1), :] = x[:, 256 * j:256 * j + 128]
                    out[pl.ds(2 * p + 1, 1), :] = x[:, 256 * j + 128:256 * j + 256]
                return 0

            lax.fori_loop(0, (counts[g, 0] + WALL_PAIRS - 1) // WALL_PAIRS, one, 0)

    whole.wait()


def wall_values(counts, lists, t, state):
    sm, vm, hbm = (pl.BlockSpec(memory_space=m) for m in (pltpu.SMEM, pltpu.VMEM, pl.ANY))
    return pl.pallas_call(
        wall_kernel,
        in_specs=[sm, sm, vm, vm],
        out_specs=[vm, hbm],
        out_shape=[jax.ShapeDtypeStruct((2 * ALLP + 8, 128), F32), jax.ShapeDtypeStruct((CY, CX), F32)],
        scratch_shapes=[pltpu.SemaphoreType.DMA((1,))],
        compiler_params=params(),
    )(counts, lists, t, state)


def solid_kernel(heat, t_fluid, ext, t_out, e, c, side, below, corner, send, recv, local, finish):
    sec, blk = lax.axis_index("sec"), lax.axis_index("blk")

    @pl.when(sec < FLUID_ROWS)
    def _():
        pass_on = pltpu.make_async_copy(t_fluid, t_out, local.at[0])
        pass_on.start()
        pass_on.wait()

    @pl.when(sec >= FLUID_ROWS)
    def _():
        upper, lower = FLUID_ROWS, SECS - 1
        left, right = lax.rem(blk + COLS - 1, COLS), lax.rem(blk + 1, COLS)
        first = pltpu.make_async_copy(ext.at[0], e.at[0], local.at[0])
        rest = pltpu.make_async_copy(ext.at[pl.ds(1, 6)], c, local.at[1])
        first.start()
        rest.start()
        signal((sec, left))
        signal((sec, right))

        @pl.when(sec == upper)
        def _():
            for q in (left, blk, right):
                signal((lower, q))

        pl.semaphore_wait(pltpu.get_barrier_semaphore(), jnp.where(sec == upper, 2, 5))
        end = TILES - 2
        copies = [push(heat.at[0], side.at[0], send.at[0], recv.at[0], (sec, left)),
                  push(heat.at[end], side.at[1], send.at[1], recv.at[1], (sec, right))]
        top = pl.ds(0, HALO)
        down = [
            pltpu.make_async_remote_copy(heat.at[pl.ds(0, TILES - 1), top], below, send.at[2], recv.at[2],
                                         device_id=(upper, blk), device_id_type=MESH),
            pltpu.make_async_remote_copy(heat.at[0, top], corner.at[0], send.at[3], recv.at[3],
                                         device_id=(upper, left), device_id_type=MESH),
            pltpu.make_async_remote_copy(heat.at[end, top], corner.at[1], send.at[4], recv.at[4],
                                         device_id=(upper, right), device_id_type=MESH)]

        @pl.when(sec == lower)
        def _():
            for d in down:
                d.start()

        first.wait()
        rest.wait()

        def warm(j, rows, x):
            e[0, j, rows, :] += x
            c[5, j, rows, :] += x

        for j in range(TILES - 1):
            warm(j, slice(OY, OY + 128), heat[j])
        for d in copies:
            d.wait()
        warm(TILES - 1, slice(OY, OY + 128), jnp.where(iota((128, 128), 1) < 64, side[0], side[1]))

        @pl.when(sec == lower)
        def _():
            for d in down:
                d.wait_send()

        @pl.when(sec == upper)
        def _():
            for d in down:
                d.wait_recv()
            last = slice(OY + CY, OY + CY + HALO)
            for j in range(TILES - 1):
                warm(j, last, below[j])
            warm(TILES - 1, last, jnp.where(iota((HALO, 128), 1) < 64, corner[0], corner[1]))

        for n in range(SOLID_STEPS - 1):
            strips(lambda r: advance(e.at[n % 2], e.at[1 - n % 2], c, None, r), 2, 34, 17)
        done = [pltpu.make_async_copy(e.at[(SOLID_STEPS - 1) % 2, j, pl.ds(OY, CY)], t_out.at[:, pl.ds(128 * j, 128)], finish.at[j])
                for j in range(TILES - 1)]
        for d in done:
            d.start()
        for d in done:
            d.wait()


def solid_steps(heat, t_fluid, ext):
    vm, hbm = pl.BlockSpec(memory_space=pltpu.VMEM), pl.BlockSpec(memory_space=pl.ANY)
    return pl.pallas_call(
        solid_kernel,
        out_shape=jax.ShapeDtypeStruct((CY, CX), F32),
        in_specs=[vm, vm, hbm],
        out_specs=hbm,
        scratch_shapes=[
            pltpu.VMEM((2, TILES, HY, 128), F32), pltpu.VMEM((6, TILES, HY, 128), F32),
            pltpu.VMEM((2, 128, 128), F32), pltpu.VMEM((TILES - 1, HALO, 128), F32), pltpu.VMEM((2, HALO, 128), F32),
            pltpu.SemaphoreType.DMA((5,)), pltpu.SemaphoreType.DMA((5,)), pltpu.SemaphoreType.DMA((2,)), pltpu.SemaphoreType.DMA((TILES - 1,)),
        ],
        compiler_params=params(collective_id=2, has_side_effects=True),
    )(heat, t_fluid, ext)


def back_kernel(values, pos1, pos2, state, slot, out, reply, fb, land, st, send, recv):
    sec, blk = lax.axis_index("sec"), lax.axis_index("blk")

    @pl.when(sec < FLUID_ROWS)
    def _():
        greet_peers(sec, blk)
        signal((FLUID_ROWS, blk))
        signal((SECS - 1, blk))
        pl.semaphore_wait(pltpu.get_barrier_semaphore(), COLS - 1)
        arrive(reply, recv.at[0])
        pick_all(transposed_parts(reply[0] + reply[1]), pos2, CROWS, SLOTS, fb)
        exchange(fb, land, send.at[1], recv.at[1], sec, blk)
        pick_all(transposed_parts(land[...]), pos1, SLOTS, FROWS, out)

    @pl.when(sec >= FLUID_ROWS)
    def _():
        pl.semaphore_wait(pltpu.get_barrier_semaphore(), FLUID_ROWS)
        for r in range(FLUID_ROWS):
            push(values.at[pl.ds(r * CROWS, CROWS)], reply.at[sec - FLUID_ROWS], send.at[0], recv.at[0], (r, blk))
        gather_cells(lambda j: state[:, 128 * j:128 * j + 128], st)

        def one(b, _):
            put_lane_row(out, b, 8, cell_values(st, lane_row(slot, b, 8)))
            return 0

        lax.fori_loop(0, FROWS // 8, one, 0)
        arrive(values.at[pl.ds(0, 2 * ALLP)], send.at[0])


def back(values, pos1, pos2, state, slot):
    return pl.pallas_call(
        back_kernel,
        out_shape=jax.ShapeDtypeStruct((FROWS, 128), F32),
        in_specs=[pl.BlockSpec(memory_space=pltpu.VMEM)] * 5,
        scratch_shapes=[
            pltpu.VMEM((2, CROWS, 128), F32), pltpu.VMEM((SLOTS, 128), F32), pltpu.VMEM((SLOTS, 128), F32),
            pltpu.VMEM((CX, 2 * CY), BF16), pltpu.SemaphoreType.DMA((2,)), pltpu.SemaphoreType.DMA((2,)),
        ],
        compiler_params=params(collective_id=3, has_side_effects=True),
    )(values, pos1, pos2, state, slot)


def body(temp, cond, vx, vy, slot, lateral, dest, coef, prior):
    slot, lateral, dest, coef, prior = (v.reshape(FROWS, 128) for v in (slot, lateral, dest, coef, prior))
    t_fluid, total, ext, pos1, pos2, t3, counts, lists = fluid(temp, cond, vx, vy, slot, coef, prior, lateral, dest)
    f3 = face_flux(total, slot, coef, prior, pos1, pos2)
    source = wall_source(counts, lists, t3, f3)
    t_new = solid_steps(source, t_fluid, ext)
    values, t_new = wall_values(counts, lists, t3, t_new)
    wall = back(values, pos1, pos2, t_new, slot)
    return t_new, wall.reshape(FACES)


def solution(mesh):
    block, face = P("sec", "blk"), P(("sec", "blk"))
    in_specs = (block, block, block, block, face, P(("sec", "blk"), None), face, face, face)
    return jax.shard_map(body, mesh=mesh, in_specs=in_specs, out_specs=(block, face), check_vma=False)
```
